32 devices in a mesh: dp: 2 (over y), seq: 16 (over z, x, core).
Axes of the slice: x: 2, y: 2, z: 4, core: 2. Of those that a mesh axis runs over, the one named last changes fastest.
Arguments:
- atoms: float32 [4, 4096, 128], P('dp', 'seq'), may hold values from -6 to 6
- single_cond: float32 [4, 4096, 128], P('dp', 'seq'), may hold values from -6 to 6
- pair_block: float32 [4, 128, 16, 32, 128], P('dp', 'seq'), may hold values from -6 to 6
- atom_count: int32 [4], P('dp'), may hold values from 2048 to 4096, as said below
- s_gain1: float32 [128], replicated, may hold values from 0.5 to 1.5
- w_scale1: float32 [128, 128], replicated, may hold values from -0.5 to 0.5
- b_scale1: float32 [128], replicated, may hold values from -6 to 6
- w_shift1: float32 [128, 128], replicated, may hold values from -0.5 to 0.5
- w_query: float32 [128, 128], replicated, may hold values from -0.5 to 0.5
- b_query: float32 [128], replicated, may hold values from -3 to 3
- w_key: float32 [128, 128], replicated, may hold values from -0.5 to 0.5
- w_value: float32 [128, 128], replicated, may hold values from -0.5 to 0.5
- w_gate: float32 [128, 128], replicated, may hold values from -0.5 to 0.5
- pair_gain: float32 [16], replicated, may hold values from 0.5 to 1.5
- w_pair: float32 [16, 4], replicated, may hold values from -1.5 to 1.5
- w_out: float32 [128, 128], replicated, may hold values from -8 to 8
- w_zero1: float32 [128, 128], replicated, may hold values from -0.5 to 0.5
- b_zero1: float32 [128], replicated, may hold values from -6 to 6
- s_gain2: float32 [128], replicated, may hold values from 0.5 to 1.5
- w_scale2: float32 [128, 128], replicated, may hold values from -0.5 to 0.5
- b_scale2: float32 [128], replicated, may hold values from -6 to 6
- w_shift2: float32 [128, 128], replicated, may hold values from -0.5 to 0.5
- w_hidden_gate: float32 [128, 256], replicated, may hold values from -0.5 to 0.5
- w_hidden_up: float32 [128, 256], replicated, may hold values from -0.5 to 0.5
- w_down: float32 [256, 128], replicated, may hold values from -1.5 to 1.5
- w_zero2: float32 [128, 128], replicated, may hold values from -0.5 to 0.5
- b_zero2: float32 [128], replicated, may hold values from -6 to 6
- cotangent: float32 [4, 4096, 128], P('dp', 'seq'), may hold values from -6 to 6
Outputs:
- block_out: float32 [4, 4096, 128], P('dp', 'seq')
- grad_atoms: float32 [4, 4096, 128], P('dp', 'seq')
- grad_single: float32 [4, 4096, 128], P('dp', 'seq')
- grad_pair: float32 [4, 128, 16, 32, 128], P('dp', 'seq')
- grad_s_gain1: float32 [128], replicated
- grad_w_scale1: float32 [128, 128], replicated
- grad_b_scale1: float32 [128], replicated
- grad_w_shift1: float32 [128, 128], replicated
- grad_w_query: float32 [128, 128], replicated
- grad_b_query: float32 [128], replicated
- grad_w_key: float32 [128, 128], replicated
- grad_w_value: float32 [128, 128], replicated
- grad_w_gate: float32 [128, 128], replicated
- grad_pair_gain: float32 [16], replicated
- grad_w_pair: float32 [16, 4], replicated
- grad_w_out: float32 [128, 128], replicated
- grad_w_zero1: float32 [128, 128], replicated
- grad_b_zero1: float32 [128], replicated
- grad_s_gain2: float32 [128], replicated
- grad_w_scale2: float32 [128, 128], replicated
- grad_b_scale2: float32 [128], replicated
- grad_w_shift2: float32 [128, 128], replicated
- grad_w_hidden_gate: float32 [128, 256], replicated
- grad_w_hidden_up: float32 [128, 256], replicated
- grad_w_down: float32 [256, 128], replicated
- grad_w_zero2: float32 [128, 128], replicated
- grad_b_zero2: float32 [128], replicated
The draws below stay inside these ranges and needn't reach their ends.
Inputs may be any that keep to these rules, and one draw needn't show every extreme that they name: `atom_count`: each sample's real atoms come first and the rest is padding; among the 2 samples of each dp index one, drawn from the seed, is full.
All inputs are finite; a program needn't handle non-finite values.
Results may differ from the reference program's by a relative error of at most 0.0003.
Values sent between devices are 32-bit elements; how exact they have to be, the bound alone decides.
A program may use at most 128 MiB of HBM per device.

```python
import math
import jax
import jax.numpy as jnp
from jax import lax

C = 128
H = 4
P_SIZE = 16
S = 128
F = 256
WQ = 32
KW = 128
HALO = 48
MB = 2
SAMPLES = 4
ATOMS = 4096
WINDOWS = 128


def draw_atom_count(key, part):
    key = jax.random.fold_in(key, 11)
    first_key, second_key = jax.random.split(key)
    lengths = jax.random.randint(first_key, (SAMPLES,), ATOMS // 2, ATOMS + 1)
    picked = jax.random.randint(second_key, (SAMPLES // MB,), 0, MB)
    slots = jnp.arange(SAMPLES)
    full = slots == slots // MB * MB + jnp.repeat(picked, MB)
    return jnp.where(full, ATOMS, lengths).astype(jnp.int32)


def block_levels(rng, shape, pieces, low, high):
    def one(position, blocks):
        draws = jax.random.uniform(jax.random.fold_in(jax.random.fold_in(rng, 6), position), (blocks,), jnp.float32, low / len(pieces), high / len(pieces))
        return jnp.repeat(jnp.exp(draws), shape[position] // blocks).reshape((-1,) + (1,) * (len(shape) - position - 1))

    gain = one(*pieces[0])
    for cut in pieces[1:]:
        gain = gain * one(*cut)
    return gain


def normal_values(own_key, dims, scale, bound, cuts=(), kind=jnp.bfloat16):
    array = scale * jax.random.normal(own_key, dims, jnp.float32)
    if cuts:
        array = array * block_levels(own_key, dims, cuts, -0.22, 0.18)
    return jnp.clip(array, -bound, bound).astype(kind)


def setup_inputs(seed: int = 0) -> dict:
    seeds = jax.random.split(jax.random.key(seed), 29)
    atoms = normal_values(seeds[0], (SAMPLES, ATOMS, C), 1.0, 6.0, ((0, 2), (1, 16)), jnp.float32)
    single_cond = normal_values(seeds[1], (SAMPLES, ATOMS, S), 1.0, 6.0, ((0, 2), (1, 16)), jnp.float32)
    pair_block = normal_values(seeds[2], (SAMPLES, WINDOWS, P_SIZE, WQ, KW), 1.0, 6.0, ((0, 2), (1, 16)), jnp.float32)
    atom_count = draw_atom_count(jax.random.fold_in(seeds[28], 71), 0)
    s_gain1 = jnp.clip(jax.random.uniform(seeds[4], (S,), jnp.float32, 0.5, 1.5), 0.5, 1.5)
    w_scale1 = normal_values(seeds[5], (S, C), S ** -0.5, 0.5, (), jnp.float32)
    b_scale1 = normal_values(seeds[6], (C,), 1.0, 6.0, (), jnp.float32)
    w_shift1 = normal_values(seeds[7], (S, C), S ** -0.5, 0.5, (), jnp.float32)
    w_query = normal_values(seeds[8], (C, C), C ** -0.5, 0.5, (), jnp.float32)
    b_query = normal_values(seeds[9], (C,), 0.5, 3.0, (), jnp.float32)
    w_key = normal_values(seeds[10], (C, C), C ** -0.5, 0.5, (), jnp.float32)
    w_value = normal_values(seeds[11], (C, C), C ** -0.5, 0.5, (), jnp.float32)
    w_gate = normal_values(seeds[12], (C, C), C ** -0.5, 0.5, (), jnp.float32)
    pair_gain = jnp.clip(jax.random.uniform(seeds[13], (P_SIZE,), jnp.float32, 0.5, 1.5), 0.5, 1.5)
    w_pair = normal_values(seeds[14], (P_SIZE, H), P_SIZE ** -0.5, 1.5, (), jnp.float32)
    w_out = normal_values(seeds[15], (C, C), 1.4, 8.0, (), jnp.float32)
    w_zero1 = normal_values(seeds[16], (S, C), S ** -0.5, 0.5, (), jnp.float32)
    b_zero1 = normal_values(seeds[17], (C,), 1.0, 6.0, (), jnp.float32)
    s_gain2 = jnp.clip(jax.random.uniform(seeds[18], (S,), jnp.float32, 0.5, 1.5), 0.5, 1.5)
    w_scale2 = normal_values(seeds[19], (S, C), S ** -0.5, 0.5, (), jnp.float32)
    b_scale2 = normal_values(seeds[20], (C,), 1.0, 6.0, (), jnp.float32)
    w_shift2 = normal_values(seeds[21], (S, C), S ** -0.5, 0.5, (), jnp.float32)
    w_hidden_gate = normal_values(seeds[22], (C, F), C ** -0.5, 0.5, (), jnp.float32)
    w_hidden_up = normal_values(seeds[23], (C, F), C ** -0.5, 0.5, (), jnp.float32)
    w_down = normal_values(seeds[24], (F, C), 0.25, 1.5, (), jnp.float32)
    w_zero2 = normal_values(seeds[25], (S, C), S ** -0.5, 0.5, (), jnp.float32)
    b_zero2 = normal_values(seeds[26], (C,), 1.0, 6.0, (), jnp.float32)
    cotangent = normal_values(seeds[27], (SAMPLES, ATOMS, C), 1.0, 6.0, ((0, 2), (1, 16)), jnp.float32)
    return dict(atoms=atoms, single_cond=single_cond, pair_block=pair_block, atom_count=atom_count, s_gain1=s_gain1, w_scale1=w_scale1, b_scale1=b_scale1, w_shift1=w_shift1, w_query=w_query, b_query=b_query, w_key=w_key, w_value=w_value, w_gate=w_gate, pair_gain=pair_gain, w_pair=w_pair, w_out=w_out, w_zero1=w_zero1, b_zero1=b_zero1, s_gain2=s_gain2, w_scale2=w_scale2, b_scale2=b_scale2, w_shift2=w_shift2, w_hidden_gate=w_hidden_gate, w_hidden_up=w_hidden_up, w_down=w_down, w_zero2=w_zero2, b_zero2=b_zero2, cotangent=cotangent)


@jax.custom_vjp
def low(v):
    return lax.optimization_barrier(v.astype(jnp.bfloat16)).astype(jnp.float32)

@jax.custom_vjp
def low_back(v):
    return v

def low_keep(v):
    return (low(v), None)

def low_pass(kept, grad):
    return (grad,)

def back_keep(v):
    return (v, None)

def back_low(kept, grad):
    return (low(grad),)
low.defvjp(low_keep, low_pass)
low_back.defvjp(back_keep, back_low)

def norm_rows(x):
    mean = lax.optimization_barrier(jnp.mean(x, axis=-1, keepdims=True))
    cent = x - mean
    var = lax.optimization_barrier(jnp.mean(cent * cent, axis=-1, keepdims=True))
    return cent * lax.rsqrt(var + 1e-05)

def matmul(x, w):
    return jnp.dot(x, w, precision=lax.Precision.HIGHEST, preferred_element_type=jnp.float32)

def window_blocks(ext, nwin, wq, reps):
    blocks = ext.reshape(nwin + reps - 1, wq, ext.shape[1])
    return jnp.concatenate([blocks[i:i + nwin] for i in range(reps)], axis=1)

def attend_core(query, keys, values, pair, pair_gain, w_pair, valid):
    nwin, wq, width = query.shape
    heads = w_pair.shape[1]
    size = width // heads
    kwid = keys.shape[1]
    q_four = query.reshape(nwin, wq, heads, size)
    k_four = keys.reshape(nwin, kwid, heads, size)
    v_four = values.reshape(nwin, kwid, heads, size)
    mean = lax.optimization_barrier(jnp.mean(pair, axis=1, keepdims=True))
    cent = pair - mean
    var = lax.optimization_barrier(jnp.mean(cent * cent, axis=1, keepdims=True))
    pair_norm = cent * lax.rsqrt(jnp.maximum(var, 0.25)) * pair_gain[None, :, None, None]
    bias = jnp.einsum('wpij,ph->whij', pair_norm, w_pair, precision=lax.Precision.HIGHEST)
    scores = jnp.einsum('wihd,wjhd->whij', q_four, k_four, precision=lax.Precision.HIGHEST) / math.sqrt(size) + bias
    scores = jnp.where(valid[:, None], scores, -1000000000.0)
    top = lax.optimization_barrier(jnp.max(scores, axis=-1, keepdims=True))
    expo = jnp.exp(scores - top)
    weights = expo / lax.optimization_barrier(jnp.sum(expo, axis=-1, keepdims=True))
    mixed = jnp.einsum('whij,wjhd->wihd', weights, v_four, precision=lax.Precision.HIGHEST)
    return mixed.reshape(nwin, wq, width)

def prepare(params, atoms, single):
    cond = norm_rows(single) * params[0]
    normed = jax.nn.sigmoid(matmul(cond, params[1]) + params[2]) * norm_rows(atoms) + matmul(cond, params[3])
    query = matmul(normed, params[4]) + params[5]
    key_value = matmul(normed, jnp.concatenate([params[6], params[7]], axis=1))
    gate = jax.nn.sigmoid(matmul(normed, params[8]))
    return (query, key_value, gate)

def finish(params, atoms, single, pair, query, gate, kv_ext, valid):
    rows, width = query.shape
    nwin = rows // WQ
    reps = KW // WQ
    keys = window_blocks(kv_ext[:, :width], nwin, WQ, reps)
    values = window_blocks(kv_ext[:, width:], nwin, WQ, reps)
    mixed = jax.checkpoint(attend_core)(query.reshape(nwin, WQ, width), keys, values, pair, params[9], params[10], valid)
    gated = gate * mixed.reshape(rows, width)
    first = atoms + jax.nn.sigmoid(matmul(single, params[12]) + params[13]) * matmul(gated, params[11])
    cond = norm_rows(single) * params[14]
    normed = jax.nn.sigmoid(matmul(cond, params[15]) + params[16]) * norm_rows(first) + matmul(cond, params[17])
    hidden = jax.nn.silu(matmul(normed, params[18])) * matmul(normed, params[19])
    return first + jax.nn.sigmoid(matmul(single, params[21]) + params[22]) * matmul(hidden, params[20])

def reference(atoms, single_cond, pair_block, atom_count, s_gain1, w_scale1, b_scale1, w_shift1, w_query, b_query, w_key, w_value, w_gate, pair_gain, w_pair, w_out, w_zero1, b_zero1, s_gain2, w_scale2, b_scale2, w_shift2, w_hidden_gate, w_hidden_up, w_down, w_zero2, b_zero2, cotangent):
    params = (s_gain1, w_scale1, b_scale1, w_shift1, w_query, b_query, w_key, w_value, w_gate, pair_gain, w_pair, w_out, w_zero1, b_zero1, s_gain2, w_scale2, b_scale2, w_shift2, w_hidden_gate, w_hidden_up, w_down, w_zero2, b_zero2)
    nwin = atoms.shape[1] // WQ
    qpos = jnp.arange(nwin, dtype=jnp.int32)[:, None] * WQ + jnp.arange(WQ, dtype=jnp.int32)[None, :]
    kpos = jnp.arange(nwin, dtype=jnp.int32)[:, None] * WQ - HALO + jnp.arange(KW, dtype=jnp.int32)[None, :]

    def one(total, item):
        atoms_s, single_s, pair_s, count, cot = item
        inside = (kpos >= 0) & (kpos < count)
        valid = inside[:, None, :] | (kpos[:, None, :] == qpos[:, :, None])

        def forward(params, atoms_s, single_s, pair_s):
            query, key_value, gate = prepare(params, atoms_s, single_s)
            kv_ext = jnp.pad(key_value, ((HALO, HALO), (0, 0)))
            return finish(params, atoms_s, single_s, pair_s, query, gate, kv_ext, valid)
        out, back = jax.vjp(forward, params, atoms_s, single_s, pair_s)
        g_params, g_atoms, g_single, g_pair = back(cot)
        total = jax.tree.map(jnp.add, total, g_params)
        return (total, (out, g_atoms, g_single, g_pair))
    zeros = jax.tree.map(jnp.zeros_like, params)
    total, stacked = lax.scan(one, zeros, (atoms, single_cond, pair_block, atom_count, cotangent))
    return (stacked[0], stacked[1], stacked[2], stacked[3], total[0], total[1], total[2], total[3], total[4], total[5], total[6], total[7], total[8], total[9], total[10], total[11], total[12], total[13], total[14], total[15], total[16], total[17], total[18], total[19], total[20], total[21], total[22])
```

```python
import functools
import math

import jax
import jax.numpy as jnp
from jax import lax
from jax.experimental import pallas as pl
from jax.experimental.pallas import tpu as pltpu
from jax.sharding import PartitionSpec as P

WQ = 32
KW = 128
HALO = 48
LANES = 128
MESH = pl.DeviceIdType.MESH
F32 = jnp.float32
HIGH = lax.Precision.HIGH

MATRICES = (
    ("w_down", 2, 1),
    ("w_hidden_gate", 1, 2),
    ("w_hidden_up", 1, 2),
    ("w_zero2", 1, 1),
    ("w_scale2", 1, 1),
    ("w_shift2", 1, 1),
    ("w_out", 1, 1),
    ("w_zero1", 1, 1),
    ("w_query", 1, 1),
    ("w_key", 1, 1),
    ("w_value", 1, 1),
    ("w_gate", 1, 1),
    ("w_scale1", 1, 1),
    ("w_shift1", 1, 1),
)
VECTORS = ("b_scale1", "b_query", "b_scale2", "b_zero1", "b_zero2", "s_gain1", "s_gain2", "pair_gain")
PARAMS = (
    "s_gain1",
    "w_scale1",
    "b_scale1",
    "w_shift1",
    "w_query",
    "b_query",
    "w_key",
    "w_value",
    "w_gate",
    "pair_gain",
    "w_pair",
    "w_out",
    "w_zero1",
    "b_zero1",
    "s_gain2",
    "w_scale2",
    "b_scale2",
    "w_shift2",
    "w_hidden_gate",
    "w_hidden_up",
    "w_down",
    "w_zero2",
    "b_zero2",
)


def offsets():
    place, row = {}, 0
    for name, rows, columns in MATRICES:
        place[name] = row
        row += rows * columns * LANES
    place["vectors"] = row
    place["w_pair"] = row + 8
    return place, row + 16


PLACE, USED = offsets()


def nn(a, b):
    return lax.dot_general(a, b, (((1,), (0,)), ((), ())), precision=HIGH, preferred_element_type=F32)


def nt(a, b):
    return lax.dot_general(a, b, (((1,), (1,)), ((), ())), precision=HIGH, preferred_element_type=F32)


def tn(a, b):
    return lax.dot_general(a, b, (((0,), (0,)), ((), ())), precision=HIGH, preferred_element_type=F32)


def norm(x):
    mean = jnp.mean(x, axis=-1, keepdims=True)
    cent = x - mean
    var = jnp.mean(cent * cent, axis=-1, keepdims=True)
    inv = lax.rsqrt(var + 1e-05)
    return cent * inv, inv


def norm_back(d, xhat, inv):
    mean = jnp.mean(d, axis=-1, keepdims=True)
    along = jnp.mean(d * xhat, axis=-1, keepdims=True)
    return (d - mean - xhat * along) * inv


def sigmoid(x):
    return 1.0 / (1.0 + jnp.exp(-x))


def column_sum(x):
    return jnp.sum(x, axis=0, keepdims=True)


def block_kernel(sizes, *refs):
    samples, rows, dpn, seqn, packed = sizes
    nwin = rows // WQ
    nz = 4
    nx = seqn // (2 * nz)
    nxy = dpn * nx
    half = packed // 2
    part = half // nxy
    chunk = part // nz
    (
        count,
        gain_s,
        wpair_s,
        atoms,
        single,
        cot,
        p_s_gain1,
        p_w_scale1,
        p_b_scale1,
        p_w_shift1,
        p_w_query,
        p_b_query,
        p_w_key,
        p_w_value,
        p_w_gate,
        p_pair_gain,
        p_w_pair,
        p_w_out,
        p_w_zero1,
        p_b_zero1,
        p_s_gain2,
        p_w_scale2,
        p_b_scale2,
        p_w_shift2,
        p_w_hidden_gate,
        p_w_hidden_up,
        p_w_down,
        p_w_zero2,
        p_b_zero2,
        pair_hbm,
        out,
        g_atoms,
        g_single,
        g_pair_hbm,
        res,
        pair,
        bias,
        pmean,
        prs,
        prob,
        ds,
        kv,
        dkv,
        dhalo,
        q_s,
        gate_s,
        mixed_s,
        cond1_s,
        cond2_s,
        ns_s,
        na_s,
        n1_s,
        sc1_s,
        sc2_s,
        sh2_s,
        z1_s,
        z2_s,
        rs_s,
        ra_s,
        dq_s,
        dfirst_s,
        dz1_s,
        dz2_s,
        dn2_s,
        dsc2_s,
        gpre_s,
        gacc,
        acc,
        recv_c,
        recv_xy,
        recv_z,
        pair_sem,
        gp_sem,
        h_send,
        h_recv,
        c_send,
        c_recv,
        xy_send,
        xy_recv,
        z_send,
        z_recv,
    ) = refs
    dp = lax.axis_index("dp")
    me = lax.axis_index("seq")
    core = lax.rem(me, 2)
    x = lax.rem(me // 2, nx)
    z = me // (2 * nx)
    k = dp * nx + x
    left = (dp, lax.rem(me + seqn - 1, seqn))
    right = (dp, lax.rem(me + 1, seqn))
    other = (dp, me + 1 - 2 * core)

    def xy_peer(o):
        kk = lax.rem(k + o, nxy)
        return kk, (kk // nx, (z * nx + lax.rem(kk, nx)) * 2 + core)

    def z_peer(o):
        zz = lax.rem(z + o, nz)
        return zz, (dp, (zz * nx + x) * 2 + core)

    for s in range(samples):
        pltpu.make_async_copy(pair_hbm.at[s], pair.at[s], pair_sem.at[s]).start()

    barrier = pltpu.get_barrier_semaphore()
    greeted = [left, right, other]
    greeted += [xy_peer(o)[1] for o in range(1, nxy)]
    greeted += [z_peer(o)[1] for o in range(1, nz)]
    for device in greeted:
        pl.semaphore_signal(barrier, inc=1, device_id=device, device_id_type=MESH)

    def three(ref):
        return ref[...].reshape(samples * rows, ref.shape[-1])

    ns, rs = norm(single[...])
    na, ra = norm(atoms[...])
    ns_s[...] = ns
    na_s[...] = na
    rs_s[...] = rs
    ra_s[...] = ra
    cond1 = ns * p_s_gain1[...]
    cond1_s[...] = cond1
    sc1 = sigmoid(nn(cond1, p_w_scale1[...]) + p_b_scale1[...])
    sc1_s[...] = sc1
    n1 = sc1 * na + nn(cond1, p_w_shift1[...])
    n1_s[...] = n1
    keys = nn(n1, p_w_key[...])
    values = nn(n1, p_w_value[...])
    for s in range(samples):
        kv[s, HALO : HALO + rows, 0:LANES] = keys[s * rows : (s + 1) * rows]
        kv[s, HALO : HALO + rows, LANES : 2 * LANES] = values[s * rows : (s + 1) * rows]

    pl.semaphore_wait(barrier, len(greeted))
    to_right = pltpu.make_async_remote_copy(
        src_ref=kv.at[:, rows : rows + HALO],
        dst_ref=kv.at[:, 0:HALO],
        send_sem=h_send.at[0],
        recv_sem=h_recv.at[0],
        device_id=right,
        device_id_type=MESH,
    )
    to_left = pltpu.make_async_remote_copy(
        src_ref=kv.at[:, HALO : 2 * HALO],
        dst_ref=kv.at[:, HALO + rows : 2 * HALO + rows],
        send_sem=h_send.at[1],
        recv_sem=h_recv.at[1],
        device_id=left,
        device_id_type=MESH,
    )
    to_right.start()
    to_left.start()

    scale = 1.0 / math.sqrt(32)
    q_s[...] = (nn(n1, p_w_query[...]) + p_b_query[...]) * scale
    gate_s[...] = sigmoid(nn(n1, p_w_gate[...]))
    cond2 = ns * p_s_gain2[...]
    cond2_s[...] = cond2
    sc2_s[...] = sigmoid(nn(cond2, p_w_scale2[...]) + p_b_scale2[...])
    sh2_s[...] = nn(cond2, p_w_shift2[...])
    z1_s[...] = sigmoid(nn(single[...], p_w_zero1[...]) + p_b_zero1[...])
    z2_s[...] = sigmoid(nn(single[...], p_w_zero2[...]) + p_b_zero2[...])

    channels = gain_s.shape[0]
    heads = wpair_s.shape[0]
    wg = [[gain_s[p] * wpair_s[h, p] for h in range(heads)] for p in range(channels)]
    wsum = [functools.reduce(lambda a, b: a + b, [wg[p][h] for p in range(channels)]) for h in range(heads)]

    for s in range(samples):
        pltpu.make_async_copy(pair_hbm.at[s], pair.at[s], pair_sem.at[s]).wait()

    def pair_bias(t, carry):
        s, w = t // nwin, lax.rem(t, nwin)
        first = pair[s, w, 0]
        total, square = first, first * first
        b = [first * wg[0][h] for h in range(heads)]
        for p in range(1, channels):
            v = pair[s, w, p]
            total = total + v
            square = square + v * v
            b = [b[h] + v * wg[p][h] for h in range(heads)]
        mean = total * (1.0 / channels)
        var = square * (1.0 / channels) - mean * mean
        inv = lax.rsqrt(jnp.maximum(var, 0.25))
        pmean[t] = mean
        live = jnp.where(var > 0.25, 1.0, jnp.where(var == 0.25, 0.5, 0.0))
        prs[t, 0] = inv
        prs[t, 1] = inv * inv * live * (1.0 / channels)
        for h in range(heads):
            bias[t, h * WQ : (h + 1) * WQ] = inv * (b[h] - mean * wsum[h])
        return carry

    lax.fori_loop(0, samples * nwin, pair_bias, 0)

    to_right.wait()
    to_left.wait()
    for s in range(samples):
        kv[s, 0:HALO] = jnp.where(me == 0, 0.0, kv[s, 0:HALO])
        kv[s, HALO + rows :] = jnp.where(me == seqn - 1, 0.0, kv[s, HALO + rows :])

    lane = lax.broadcasted_iota(jnp.int32, (heads * WQ, LANES), 1)
    row = lax.broadcasted_iota(jnp.int32, (heads * WQ, LANES), 0)
    own = (lane // 32 == row // WQ).astype(F32)
    same = lane == lax.rem(row, WQ) + HALO

    def window(t):
        s, w = t // nwin, lax.rem(t, nwin)
        return s, w, pl.multiple_of(s * rows + w * WQ, WQ), pl.multiple_of(w * WQ, WQ)

    def heads_in(v):
        return jnp.concatenate([v] * heads, axis=0) * own

    def heads_out(v):
        v = v * own
        return (v[0:WQ] + v[WQ : 2 * WQ]) + (v[2 * WQ : 3 * WQ] + v[3 * WQ : 4 * WQ])

    def attend(t, carry):
        s, w, at, key_at = window(t)
        queries = heads_in(q_s[pl.ds(at, WQ), :])
        key = kv[s, pl.ds(key_at, KW), 0:LANES]
        value = kv[s, pl.ds(key_at, KW), LANES : 2 * LANES]
        scores = nt(queries, key) + bias[t]
        begin = me * rows + w * WQ - HALO
        inside = (lane >= -begin) & (lane < count[s] - begin)
        scores = jnp.where(inside | same, scores, -1e9)
        top = jnp.max(scores, axis=-1, keepdims=True)
        expo = jnp.exp(scores - top)
        weights = expo / jnp.sum(expo, axis=-1, keepdims=True)
        prob[t] = weights
        mixed_s[pl.ds(at, WQ), :] = heads_out(nn(weights, value))
        return carry

    lax.fori_loop(0, samples * nwin, attend, 0)

    gated = gate_s[...] * mixed_s[...]
    projected = nn(gated, p_w_out[...])
    first = atoms[...] + z1_s[...] * projected
    nf, rf = norm(first)
    n2 = sc2_s[...] * nf + sh2_s[...]
    hg = nn(n2, p_w_hidden_gate[...])
    hu = nn(n2, p_w_hidden_up[...])
    sg = sigmoid(hg)
    silu = hg * sg
    hidden = silu * hu
    down = nn(hidden, p_w_down[...])
    z2 = z2_s[...]
    g = cot[...]
    out[...] = first + z2 * down

    def put(name, value):
        base = PLACE[name]
        for b in range(value.shape[1] // LANES):
            at = base + b * value.shape[0]
            acc[at : at + value.shape[0]] = value[:, b * LANES : (b + 1) * LANES]

    d_down = g * z2
    dz2 = g * down * z2 * (1.0 - z2)
    dz2_s[...] = dz2
    put("w_down", tn(hidden, d_down))
    d_hidden = nt(d_down, p_w_down[...])
    d_hg = d_hidden * hu * (sg * (1.0 + hg * (1.0 - sg)))
    d_hu = d_hidden * silu
    put("w_hidden_gate", tn(n2, d_hg))
    put("w_hidden_up", tn(n2, d_hu))
    put("w_zero2", tn(single[...], dz2))
    d_n2 = nt(d_hg, p_w_hidden_gate[...]) + nt(d_hu, p_w_hidden_up[...])
    dn2_s[...] = d_n2
    sc2 = sc2_s[...]
    dsc2 = d_n2 * nf * sc2 * (1.0 - sc2)
    dsc2_s[...] = dsc2
    put("w_scale2", tn(cond2_s[...], dsc2))
    put("w_shift2", tn(cond2_s[...], d_n2))
    d_first = g + norm_back(d_n2 * sc2, nf, rf)
    dfirst_s[...] = d_first
    z1 = z1_s[...]
    d_proj = d_first * z1
    dz1 = d_first * projected * z1 * (1.0 - z1)
    dz1_s[...] = dz1
    put("w_out", tn(gated, d_proj))
    put("w_zero1", tn(single[...], dz1))
    d_gated = nt(d_proj, p_w_out[...])
    gate = gate_s[...]
    mixed = mixed_s[...]
    gpre_s[...] = d_gated * mixed * gate * (1.0 - gate)
    mixed_s[...] = d_gated * gate

    dkv[...] = jnp.zeros_like(dkv)

    def attend_back(t, carry):
        s, w, at, key_at = window(t)
        queries = heads_in(q_s[pl.ds(at, WQ), :])
        d_mixed = heads_in(mixed_s[pl.ds(at, WQ), :])
        key = kv[s, pl.ds(key_at, KW), 0:LANES]
        value = kv[s, pl.ds(key_at, KW), LANES : 2 * LANES]
        weights = prob[t]
        d_weights = nt(d_mixed, value)
        d_scores = weights * (d_weights - jnp.sum(weights * d_weights, axis=-1, keepdims=True))
        ds[t] = d_scores
        dq_s[pl.ds(at, WQ), :] = heads_out(nn(d_scores, key)) * scale
        dkv[s, pl.ds(key_at, KW), 0:LANES] += tn(d_scores, queries)
        dkv[s, pl.ds(key_at, KW), LANES : 2 * LANES] += tn(weights, d_mixed)
        return carry

    lax.fori_loop(0, samples * nwin, attend_back, 0)

    back_left = pltpu.make_async_remote_copy(
        src_ref=dkv.at[:, 0:HALO],
        dst_ref=dhalo.at[1],
        send_sem=h_send.at[2],
        recv_sem=h_recv.at[2],
        device_id=left,
        device_id_type=MESH,
    )
    back_right = pltpu.make_async_remote_copy(
        src_ref=dkv.at[:, HALO + rows : 2 * HALO + rows],
        dst_ref=dhalo.at[0],
        send_sem=h_send.at[3],
        recv_sem=h_recv.at[3],
        device_id=right,
        device_id_type=MESH,
    )
    back_left.start()
    back_right.start()

    gacc[...] = jnp.zeros_like(gacc)

    def pair_back(t, carry):
        s, w = t // nwin, lax.rem(t, nwin)
        inv, live = prs[t, 0], prs[t, 1]
        mean = pmean[t]
        u, along, level = [], None, None
        for h in range(heads):
            d = ds[t, h * WQ : (h + 1) * WQ]
            u.append(d * inv)
            a = d * bias[t, h * WQ : (h + 1) * WQ]
            b = u[h] * (wsum[h] * (1.0 / channels))
            along = a if along is None else along + a
            level = b if level is None else level + b
        c1 = along * live
        c0 = mean * c1 - level
        mu = [mean * u[h] for h in range(heads)]
        for p in range(channels):
            v = pair[s, w, p]
            d = c0 - v * c1
            for h in range(heads):
                d = d + u[h] * wg[p][h]
                product = v * u[h] - mu[h]
                gacc[h * channels + p] += (product[0:8] + product[8:16]) + (product[16:24] + product[24:32])
            pair[s, w, p] = d
        return carry

    lax.fori_loop(0, samples * nwin, pair_back, 0)

    for s in range(samples):
        pltpu.make_async_copy(pair.at[s], g_pair_hbm.at[s], gp_sem.at[s]).start()

    back_left.wait()
    back_right.wait()
    for s in range(samples):
        dkv[s, HALO : 2 * HALO] += dhalo[0, s]
        dkv[s, rows : rows + HALO] += dhalo[1, s]

    n1 = n1_s[...]
    dq = dq_s[...]
    d_keys = jnp.concatenate([dkv[s, HALO : HALO + rows, 0:LANES] for s in range(samples)], axis=0)
    d_values = jnp.concatenate([dkv[s, HALO : HALO + rows, LANES : 2 * LANES] for s in range(samples)], axis=0)
    d_gate = gpre_s[...]
    put("w_query", tn(n1, dq))
    put("w_key", tn(n1, d_keys))
    put("w_value", tn(n1, d_values))
    put("w_gate", tn(n1, d_gate))
    d_n1 = (nt(dq, p_w_query[...]) + nt(d_keys, p_w_key[...])) + (
        nt(d_values, p_w_value[...]) + nt(d_gate, p_w_gate[...])
    )
    na = na_s[...]
    sc1 = sc1_s[...]
    dsc1 = d_n1 * na * sc1 * (1.0 - sc1)
    put("w_scale1", tn(cond1_s[...], dsc1))
    put("w_shift1", tn(cond1_s[...], d_n1))
    g_atoms[...] = dfirst_s[...] + norm_back(d_n1 * sc1, na, ra_s[...])
    ns = ns_s[...]
    d_cond1 = nt(dsc1, p_w_scale1[...]) + nt(d_n1, p_w_shift1[...])
    d_cond2 = nt(dsc2_s[...], p_w_scale2[...]) + nt(dn2_s[...], p_w_shift2[...])
    d_ns = d_cond1 * p_s_gain1[...] + d_cond2 * p_s_gain2[...]
    g_single[...] = norm_back(d_ns, ns, rs_s[...]) + (
        nt(dz1_s[...], p_w_zero1[...]) + nt(dz2_s[...], p_w_zero2[...])
    )

    eye = (
        lax.broadcasted_iota(jnp.int32, (channels, LANES), 0) == lax.broadcasted_iota(jnp.int32, (channels, LANES), 1)
    ).astype(F32)
    gsum = jnp.sum(jnp.sum(gacc[...], axis=1), axis=-1, keepdims=True)
    rows_g = [column_sum(gsum[h * channels : (h + 1) * channels] * eye) for h in range(heads)]
    blank = jnp.zeros((1, LANES - channels), F32)
    gain_row = jnp.concatenate([p_pair_gain[...], blank], axis=1)
    pair_row = jnp.zeros((1, LANES), F32)
    for h in range(heads):
        pair_row = pair_row + rows_g[h] * jnp.concatenate([p_w_pair[h : h + 1, :], blank], axis=1)
    pair_grad = jnp.concatenate([v * gain_row for v in rows_g] + [jnp.zeros((8 - heads, LANES), F32)], axis=0)
    small = {
        "b_scale1": column_sum(dsc1),
        "b_query": column_sum(dq),
        "b_scale2": column_sum(dsc2_s[...]),
        "b_zero1": column_sum(dz1_s[...]),
        "b_zero2": column_sum(dz2_s[...]),
        "s_gain1": column_sum(d_cond1 * ns),
        "s_gain2": column_sum(d_cond2 * ns),
        "pair_gain": pair_row,
    }
    acc[PLACE["vectors"] : PLACE["vectors"] + 8] = jnp.concatenate([small[name] for name in VECTORS], axis=0)
    acc[PLACE["w_pair"] : PLACE["w_pair"] + 8] = pair_grad
    acc[USED:] = jnp.zeros((packed - USED, LANES), F32)

    def remote(src, dst, send, recv, device):
        return pltpu.make_async_remote_copy(
            src_ref=src, dst_ref=dst, send_sem=send, recv_sem=recv, device_id=device, device_id_type=MESH
        )

    def span(start, size):
        return pl.ds(pl.multiple_of(start, 8), size)

    mine = core * half
    copy = remote(acc.at[span((1 - core) * half, half)], recv_c, c_send.at[0], c_recv.at[0], other)
    copy.start()
    copy.wait()
    acc[span(mine, half), :] += recv_c[...]

    copies = []
    for o in range(1, nxy):
        kk, device = xy_peer(o)
        copies.append(
            remote(
                acc.at[span(mine + kk * part, part)], recv_xy.at[o - 1], xy_send.at[o - 1], xy_recv.at[o - 1], device
            )
        )
    for copy in copies:
        copy.start()
    for copy in copies:
        copy.wait()
    mine_xy = mine + k * part
    value = acc[span(mine_xy, part), :]
    for o in range(1, nxy):
        value = value + recv_xy[o - 1]
    acc[span(mine_xy, part), :] = value

    copies = []
    for o in range(1, nz):
        zz, device = z_peer(o)
        copies.append(
            remote(
                acc.at[span(mine_xy + zz * chunk, chunk)], recv_z.at[o - 1], z_send.at[o - 1], z_recv.at[o - 1], device
            )
        )
    for copy in copies:
        copy.start()
    for copy in copies:
        copy.wait()
    mine_z = mine_xy + z * chunk
    value = acc[span(mine_z, chunk), :]
    for o in range(1, nz):
        value = value + recv_z[o - 1]
    res[span(mine_z, chunk), :] = value

    def gather(src, peers, send, recv):
        copies = []
        for i, device in enumerate(peers):
            copies.append(remote(res.at[src], res.at[src], send.at[i], recv.at[i], device))
        for copy in copies:
            copy.start()
        for copy in copies:
            copy.wait()

    gather(span(mine_z, chunk), [z_peer(o)[1] for o in range(1, nz)], z_send.at[pl.ds(nz - 1, nz - 1)], z_recv.at[pl.ds(nz - 1, nz - 1)])
    gather(
        span(mine_xy, part),
        [xy_peer(o)[1] for o in range(1, nxy)],
        xy_send.at[pl.ds(nxy - 1, nxy - 1)],
        xy_recv.at[pl.ds(nxy - 1, nxy - 1)],
    )
    gather(span(mine, half), [other], c_send.at[pl.ds(1, 1)], c_recv.at[pl.ds(1, 1)])
    for s in range(samples):
        pltpu.make_async_copy(pair.at[s], g_pair_hbm.at[s], gp_sem.at[s]).wait()


def unpack_kernel(pieces, *refs):
    n, v = len(pieces), len(VECTORS)
    packed, big_in, refs = refs[0], refs[1:5], refs[5:]
    big_out, mats, rows, wp = refs[:4], refs[4 : 4 + n], refs[4 + n : 4 + n + v], refs[4 + n + v]
    stage, in_sems, out_sems, sems = refs[5 + n + v :][:4], *refs[-3:]
    moves = []
    for a, mid, b in zip(big_in, stage, big_out):
        for c in range(a.shape[0]):
            i = len(moves)
            moves.append(
                (
                    pltpu.make_async_copy(a.at[c], mid.at[c], in_sems.at[i]),
                    pltpu.make_async_copy(mid.at[c], b.at[c], out_sems.at[i]),
                )
            )
    for load, _ in moves:
        load.start()
    copies = []
    for name, ref in zip(pieces, mats):
        base = PLACE[name]
        height, width = ref.shape
        for b in range(width // LANES):
            copies.append(
                pltpu.make_async_copy(
                    packed.at[pl.ds(base + b * height, height)],
                    ref.at[:, pl.ds(b * LANES, LANES)],
                    sems.at[len(copies)],
                )
            )
    for copy in copies:
        copy.start()
    base = PLACE["vectors"]
    for i, ref in enumerate(rows):
        ref[...] = packed[base + i : base + i + 1, 0 : ref.shape[1]]
    base = PLACE["w_pair"]
    wp[...] = packed[base : base + wp.shape[0], 0 : wp.shape[1]]
    for load, store in moves:
        load.wait()
        store.start()
    for copy in copies:
        copy.wait()
    for _, store in moves:
        store.wait()


def shards(dpn, seqn, atoms, single_cond, pair_block, atom_count, *rest):
    params, cotangent = dict(zip(PARAMS, rest[:-1])), rest[-1]
    params["w_pair"] = params["w_pair"].T
    samples, rows, width = atoms.shape
    nwin, channels = pair_block.shape[1:3]
    heads = params["w_pair"].shape[0]
    flat = samples * rows
    grain = 8 * dpn * seqn
    packed = -(-USED // grain) * grain
    nz, nx = 4, seqn // 8
    nxy = dpn * nx
    half = packed // 2
    part = half // nxy
    chunk = part // nz
    windows = samples * nwin

    def row(v):
        return v.reshape(1, -1) if v.ndim == 1 else v

    vmem = pl.BlockSpec(memory_space=pltpu.VMEM)
    smem = pl.BlockSpec(memory_space=pltpu.SMEM)
    anyw = pl.BlockSpec(memory_space=pl.ANY)

    def buf(*shape):
        return pltpu.VMEM(shape, F32)

    tall = (flat, width)
    scratch = [
        buf(*pair_block.shape),
        buf(windows, heads * WQ, KW),
        buf(windows, WQ, KW),
        buf(windows, 2, WQ, KW),
        buf(windows, heads * WQ, KW),
        buf(windows, heads * WQ, KW),
        buf(samples, rows + 2 * HALO, 2 * width),
        buf(samples, rows + 2 * HALO, 2 * width),
        buf(2, samples, HALO, 2 * width),
    ]
    scratch += [buf(*tall) for _ in range(13)]
    scratch += [buf(flat, 1), buf(flat, 1)]
    scratch += [buf(*tall) for _ in range(7)]
    scratch += [
        buf(heads * channels, 8, KW),
        buf(packed, LANES),
        buf(half, LANES),
        buf(nxy - 1, part, LANES),
        buf(nz - 1, chunk, LANES),
        pltpu.SemaphoreType.DMA((samples,)),
        pltpu.SemaphoreType.DMA((samples,)),
        pltpu.SemaphoreType.DMA((4,)),
        pltpu.SemaphoreType.DMA((4,)),
        pltpu.SemaphoreType.DMA((2,)),
        pltpu.SemaphoreType.DMA((2,)),
        pltpu.SemaphoreType.DMA((2 * (nxy - 1),)),
        pltpu.SemaphoreType.DMA((2 * (nxy - 1),)),
        pltpu.SemaphoreType.DMA((2 * (nz - 1),)),
        pltpu.SemaphoreType.DMA((2 * (nz - 1),)),
    ]
    sizes = (samples, rows, dpn, seqn, packed)
    out, g_atoms, g_single, g_pair, res = pl.pallas_call(
        functools.partial(block_kernel, sizes),
        out_shape=[
            jax.ShapeDtypeStruct(tall, F32),
            jax.ShapeDtypeStruct(tall, F32),
            jax.ShapeDtypeStruct(tall, F32),
            jax.ShapeDtypeStruct(pair_block.shape, F32),
            jax.ShapeDtypeStruct((packed, LANES), F32),
        ],
        in_specs=[smem] * 3 + [vmem] * (3 + len(PARAMS)) + [anyw],
        out_specs=[vmem, vmem, vmem, anyw, vmem],
        scratch_shapes=scratch,
        compiler_params=pltpu.CompilerParams(
            collective_id=0, has_side_effects=True, vmem_limit_bytes=56 * 2**20
        ),
        name="block",
    )(
        atom_count,
        params["pair_gain"],
        params["w_pair"],
        atoms.reshape(tall),
        single_cond.reshape(tall),
        cotangent.reshape(tall),
        *[row(params[name]) for name in PARAMS],
        pair_block,
    )

    pieces = tuple(name for name, _, _ in MATRICES)
    mats = [jax.ShapeDtypeStruct(params[name].shape, F32) for name in pieces]
    vecs = [jax.ShapeDtypeStruct((1, params[name].shape[0]), F32) for name in VECTORS]
    big = [out.reshape(atoms.shape), g_atoms.reshape(atoms.shape), g_single.reshape(atoms.shape)]
    big.append(g_pair.reshape((windows,) + pair_block.shape[2:]))
    moves = sum(v.shape[0] for v in big)
    copies = sum(columns for _, _, columns in MATRICES)
    hbm = pl.BlockSpec(memory_space=pltpu.HBM)
    results = pl.pallas_call(
        functools.partial(unpack_kernel, pieces),
        out_shape=[jax.ShapeDtypeStruct(v.shape, F32) for v in big]
        + mats
        + vecs
        + [jax.ShapeDtypeStruct((heads, channels), F32)],
        in_specs=[vmem] + [hbm] * 4,
        out_specs=[hbm] * (4 + len(mats)) + [vmem] * (len(vecs) + 1),
        scratch_shapes=[buf(*v.shape) for v in big]
        + [
            pltpu.SemaphoreType.DMA((moves,)),
            pltpu.SemaphoreType.DMA((moves,)),
            pltpu.SemaphoreType.DMA((copies,)),
        ],
        compiler_params=pltpu.CompilerParams(vmem_limit_bytes=32 * 2**20),
        name="unpack",
    )(res, *big)
    grads = dict(zip(pieces, results[4:]))
    for name, value in zip(VECTORS, results[4 + len(mats) :]):
        grads[name] = value.reshape(-1)
    grads["w_pair"] = results[-1].T
    out, g_atoms, g_single, g_pair = results[:4]
    return (out, g_atoms, g_single, g_pair.reshape(pair_block.shape)) + tuple(grads[name] for name in PARAMS)


def solution(mesh):
    data = P("dp", "seq", None)
    pairs = P("dp", "seq", None, None, None)
    return jax.shard_map(
        functools.partial(shards, mesh.shape["dp"], mesh.shape["seq"]),
        mesh=mesh,
        in_specs=(data, data, pairs, P("dp")) + (P(),) * len(PARAMS) + (data,),
        out_specs=(data, data, data, pairs) + (P(),) * len(PARAMS),
        check_vma=False,
    )
```

```python
import functools
import math

import jax
import jax.numpy as jnp
from jax import lax
from jax.experimental import pallas as pl
from jax.experimental.pallas import tpu as pltpu
from jax.sharding import PartitionSpec as P

WQ = 32
KW = 128
HALO = 48
LANES = 128
MESH = pl.DeviceIdType.MESH
F32 = jnp.float32

EARLY = (
    ("w_down", 2, 1),
    ("w_hidden_gate", 1, 2),
    ("w_hidden_up", 1, 2),
    ("w_zero2", 1, 1),
    ("w_scale2", 1, 1),
    ("w_shift2", 1, 1),
    ("w_out", 1, 1),
    ("w_zero1", 1, 1),
    ("w_gate", 1, 1),
)
LATE = (
    ("w_query", 1, 1),
    ("w_key", 1, 1),
    ("w_value", 1, 1),
    ("w_scale1", 1, 1),
    ("w_shift1", 1, 1),
)
VECTORS = ("b_scale1", "b_query", "b_scale2", "b_zero1", "b_zero2", "s_gain1", "s_gain2", "pair_gain")
PARAMS = (
    "s_gain1",
    "w_scale1",
    "b_scale1",
    "w_shift1",
    "w_query",
    "b_query",
    "w_key",
    "w_value",
    "w_gate",
    "pair_gain",
    "w_pair",
    "w_out",
    "w_zero1",
    "b_zero1",
    "s_gain2",
    "w_scale2",
    "b_scale2",
    "w_shift2",
    "w_hidden_gate",
    "w_hidden_up",
    "w_down",
    "w_zero2",
    "b_zero2",
)


def offsets():
    place, used = {}, []
    for group in (EARLY, LATE):
        row = 0
        for name, rows, columns in group:
            place[name] = row
            row += rows * columns * LANES
        used.append(row)
    place["vectors"] = used[1]
    place["w_pair"] = used[1] + 8
    return place, used[0], used[1] + 16


PLACE, EARLY_ROWS, LATE_ROWS = offsets()
BF16 = jnp.bfloat16
NN = (((1,), (0,)), ((), ()))
NT = (((1,), (1,)), ((), ()))
TN = (((0,), (0,)), ((), ()))


def dot(a, b, dims):
    return lax.dot_general(a, b, dims, preferred_element_type=F32)


def cat(parts, axis):
    return jnp.concatenate(parts, axis=axis)


def split(x):
    high = x.astype(BF16)
    return high, (x - high.astype(F32)).astype(BF16)


def product(a, b, dims):
    (ah, al), (bh, bl) = a, b
    (ka,), (kb,) = dims[0]
    return dot(cat([ah, al, ah], ka), cat([bh, bh, bl], kb), dims)


def nn(a, b):
    return product(a, b, NN)


def nt(a, b):
    return product(a, b, NT)


def tn(a, b):
    return product(a, b, TN)


def mean_lanes(x):
    weight = jnp.full((2 * LANES, LANES), 1.0 / LANES, BF16)
    return dot(cat(split(x), 1), weight, NN)


def norm(x):
    cent = x - mean_lanes(x)
    inv = lax.rsqrt(mean_lanes(cent * cent) + 1e-05)
    return cent * inv, inv


def norm_back(d, xhat, inv):
    return (d - mean_lanes(d) - xhat * mean_lanes(d * xhat)) * inv


def sigmoid(x):
    return 1.0 / (1.0 + jnp.exp(-x))


def column_sum(x):
    return jnp.sum(x, axis=0, keepdims=True)


def block_kernel(sizes, *refs):
    samples, rows, dpn, seqn, early, late = sizes
    nwin = rows // WQ
    flat = samples * rows
    nz = 4
    nx = seqn // (2 * nz)
    nxy = dpn * nx
    (
        count,
        gain_s,
        wpair_s,
        atoms,
        single,
        cot,
        p_s_gain1,
        p_w_scale1,
        p_b_scale1,
        p_w_shift1,
        p_w_query,
        p_b_query,
        p_w_key,
        p_w_value,
        p_w_gate,
        p_pair_gain,
        p_w_pair,
        p_w_out,
        p_w_zero1,
        p_b_zero1,
        p_s_gain2,
        p_w_scale2,
        p_b_scale2,
        p_w_shift2,
        p_w_hidden_gate,
        p_w_hidden_up,
        p_w_down,
        p_w_zero2,
        p_b_zero2,
        pair_hbm,
        out_hbm,
        g_atoms_hbm,
        g_single_hbm,
        g_pair_hbm,
        early_hbm,
        late_hbm,
        pair,
        bias,
        pmean,
        prs,
        prob,
        ds,
        kv,
        dkv,
        dhalo,
        kvh,
        kvl,
        w1h,
        w1l,
        wqh,
        wql,
        wzh,
        wzl,
        w2h,
        w2l,
        whh,
        whl,
        wdh,
        wdl,
        woh,
        wol,
        qh_s,
        ql_s,
        mh_s,
        ml_s,
        th_s,
        tl_s,
        mixed_s,
        ns_s,
        na_s,
        n1_s,
        sc1_s,
        sc2_s,
        sh2_s,
        gate_s,
        z1_s,
        z2_s,
        rs_s,
        ra_s,
        dq_s,
        dfirst_s,
        dz1_s,
        dz2_s,
        dn2_s,
        dsc2_s,
        gpre_s,
        out,
        g_atoms,
        g_single,
        gacc,
        acc_e,
        res_e,
        acc_l,
        res_l,
        recv_ec,
        recv_exy,
        recv_ez,
        recv_lc,
        recv_lxy,
        recv_lz,
        pair_sem,
        out_sem,
        h_send,
        h_recv,
        ec_send,
        ec_recv,
        exy_send,
        exy_recv,
        ez_send,
        ez_recv,
        lc_send,
        lc_recv,
        lxy_send,
        lxy_recv,
        lz_send,
        lz_recv,
    ) = refs
    dp = lax.axis_index("dp")
    me = lax.axis_index("seq")
    core = lax.rem(me, 2)
    x = lax.rem(me // 2, nx)
    z = me // (2 * nx)
    k = dp * nx + x
    left = (dp, lax.rem(me + seqn - 1, seqn))
    right = (dp, lax.rem(me + 1, seqn))
    other = (dp, me + 1 - 2 * core)

    def xy_peer(o):
        kk = lax.rem(k + o, nxy)
        return kk, (kk // nx, (z * nx + lax.rem(kk, nx)) * 2 + core)

    def z_peer(o):
        zz = lax.rem(z + o, nz)
        return zz, (dp, (zz * nx + x) * 2 + core)

    for s in range(samples):
        pltpu.make_async_copy(pair_hbm.at[s], pair.at[s], pair_sem.at[s]).start()

    barrier = pltpu.get_barrier_semaphore()
    greeted = [left, right, other]
    greeted += [xy_peer(o)[1] for o in range(1, nxy)]
    greeted += [z_peer(o)[1] for o in range(1, nz)]
    for device in greeted:
        pl.semaphore_signal(barrier, inc=1, device_id=device, device_id_type=MESH)

    def remote(src, dst, send, recv, device):
        return pltpu.make_async_remote_copy(
            src_ref=src, dst_ref=dst, send_sem=send, recv_sem=recv, device_id=device, device_id_type=MESH
        )

    def start(copies):
        for copy in copies:
            copy.start()
        return copies

    def wait(copies):
        for copy in copies:
            copy.wait()

    def span(first, size):
        return pl.ds(pl.multiple_of(first, 8), size)

    def hold(high, low, *weights):
        for c, w in enumerate(weights):
            width = w.shape[1]
            high[:, c * width : (c + 1) * width], low[:, c * width : (c + 1) * width] = split(w[...])

    hold(w1h, w1l, p_w_scale1, p_w_shift1)
    hold(wqh, wql, p_w_query, p_w_key, p_w_value, p_w_gate)
    ns, rs = norm(single[...])
    na, ra = norm(atoms[...])
    ns_s[...] = ns
    na_s[...] = na
    rs_s[...] = rs
    ra_s[...] = ra
    first1 = nn(split(ns * p_s_gain1[...]), (w1h[...], w1l[...]))
    sc1 = sigmoid(first1[:, :LANES] + p_b_scale1[...])
    sc1_s[...] = sc1
    n1 = sc1 * na + first1[:, LANES:]
    n1_s[...] = n1
    n1_split = split(n1)
    keys_values = nn(n1_split, (wqh[:, LANES : 3 * LANES], wql[:, LANES : 3 * LANES]))
    for s in range(samples):
        kv[s, HALO : HALO + rows] = keys_values[s * rows : (s + 1) * rows]

    pl.semaphore_wait(barrier, len(greeted))
    halos = start(
        [
            remote(kv.at[:, rows : rows + HALO], kv.at[:, 0:HALO], h_send.at[0], h_recv.at[0], right),
            remote(
                kv.at[:, HALO : 2 * HALO], kv.at[:, HALO + rows : 2 * HALO + rows], h_send.at[1], h_recv.at[1], left
            ),
        ]
    )

    hold(wzh, wzl, p_w_zero1, p_w_zero2)
    hold(w2h, w2l, p_w_scale2, p_w_shift2)
    hold(whh, whl, p_w_hidden_gate, p_w_hidden_up)
    hold(wdh, wdl, p_w_down)
    hold(woh, wol, p_w_out)
    scale = 1.0 / math.sqrt(32)
    query = (nn(n1_split, (wqh[:, :LANES], wql[:, :LANES])) + p_b_query[...]) * scale
    qh_s[...], ql_s[...] = split(query)
    gate_s[...] = sigmoid(nn(n1_split, (wqh[:, 3 * LANES :], wql[:, 3 * LANES :])))
    first2 = nn(split(ns * p_s_gain2[...]), (w2h[...], w2l[...]))
    sc2_s[...] = sigmoid(first2[:, :LANES] + p_b_scale2[...])
    sh2_s[...] = first2[:, LANES:]
    zeros = nn(split(single[...]), (wzh[...], wzl[...]))
    z1_s[...] = sigmoid(zeros[:, :LANES] + p_b_zero1[...])
    z2_s[...] = sigmoid(zeros[:, LANES:] + p_b_zero2[...])

    channels = gain_s.shape[0]
    heads = wpair_s.shape[0]
    wg = [[gain_s[p] * wpair_s[h, p] for h in range(heads)] for p in range(channels)]
    wsum = [functools.reduce(lambda a, b: a + b, [wg[p][h] for p in range(channels)]) for h in range(heads)]

    for s in range(samples):
        pltpu.make_async_copy(pair_hbm.at[s], pair.at[s], pair_sem.at[s]).wait()

    key_lane = lax.broadcasted_iota(jnp.int32, (WQ, KW), 1)
    same = key_lane == lax.broadcasted_iota(jnp.int32, (WQ, KW), 0) + HALO

    def pair_bias(t, carry):
        s, w = t // nwin, lax.rem(t, nwin)
        first = pair[s, w, 0]
        total, square = first, first * first
        b = [first * wg[0][h] for h in range(heads)]
        for p in range(1, channels):
            v = pair[s, w, p]
            total = total + v
            square = square + v * v
            b = [b[h] + v * wg[p][h] for h in range(heads)]
        mean = total * (1.0 / channels)
        var = square * (1.0 / channels) - mean * mean
        inv = lax.rsqrt(jnp.maximum(var, 0.25))
        pmean[t] = mean
        live = jnp.where(var > 0.25, 1.0, jnp.where(var == 0.25, 0.5, 0.0))
        prs[t, 0] = inv
        prs[t, 1] = inv * inv * live * (1.0 / channels)
        begin = me * rows + w * WQ - HALO
        valid = ((key_lane >= -begin) & (key_lane < count[s] - begin)) | same
        for h in range(heads):
            bias[t, h * WQ : (h + 1) * WQ] = jnp.where(valid, inv * (b[h] - mean * wsum[h]), -1e9)
        return carry

    lax.fori_loop(0, samples * nwin, pair_bias, 0)

    wait(halos)
    for s in range(samples):
        kv[s, 0:HALO] = jnp.where(me == 0, 0.0, kv[s, 0:HALO])
        kv[s, HALO + rows :] = jnp.where(me == seqn - 1, 0.0, kv[s, HALO + rows :])
    kvh[...], kvl[...] = split(kv[...])

    lane = lax.broadcasted_iota(jnp.int32, (heads * WQ, LANES), 1)
    row = lax.broadcasted_iota(jnp.int32, (heads * WQ, LANES), 0)
    own = (lane // 32 == row // WQ).astype(F32)
    own_low = own.astype(BF16)
    ones = jnp.ones((KW, LANES), BF16)
    nothing = jnp.zeros((KW, LANES), BF16)

    def heads_in(ref, at):
        return cat([ref[pl.ds(at, WQ), :]] * heads, 0) * own_low

    def heads_out(v):
        v = v * own
        return (v[0:WQ] + v[WQ : 2 * WQ]) + (v[2 * WQ : 3 * WQ] + v[3 * WQ : 4 * WQ])

    def attend(s, carry):
        for w in range(nwin):
            t = s * nwin + w
            at = pl.multiple_of(s * rows + w * WQ, WQ)
            keys = slice(w * WQ, w * WQ + KW)
            queries = heads_in(qh_s, at), heads_in(ql_s, at)
            scores = nt(queries, (kvh[s, keys, :LANES], kvl[s, keys, :LANES])) + bias[t]
            expo = jnp.exp(scores - jnp.max(scores, axis=-1, keepdims=True))
            eh, el = split(expo)
            vh, vl = kvh[s, keys, LANES:], kvl[s, keys, LANES:]
            high = cat([vh, ones], 1)
            both = dot(cat([eh, el, eh], 1), cat([high, high, cat([vl, nothing], 1)], 0), NN)
            inv = 1.0 / both[:, LANES:]
            prob[t] = expo * inv
            mixed_s[pl.ds(at, WQ), :] = heads_out(both[:, :LANES] * inv)
        return carry

    lax.fori_loop(0, samples, attend, 0)

    gated = gate_s[...] * mixed_s[...]
    gated_split = split(gated)
    projected = nn(gated_split, (woh[...], wol[...]))
    first = atoms[...] + z1_s[...] * projected
    nf, rf = norm(first)
    n2 = sc2_s[...] * nf + sh2_s[...]
    n2_split = split(n2)
    up = nn(n2_split, (whh[...], whl[...]))
    hidden_width = up.shape[1] // 2
    hg, hu = up[:, :hidden_width], up[:, hidden_width:]
    sg = sigmoid(hg)
    silu = hg * sg
    hidden = silu * hu
    hidden_split = split(hidden)
    down = nn(hidden_split, (wdh[...], wdl[...]))
    z2 = z2_s[...]
    g = cot[...]
    out[...] = first + z2 * down
    outputs = start([pltpu.make_async_copy(out, out_hbm, out_sem.at[0])])

    def put(acc, names, value):
        at = 0
        for name in names:
            base = PLACE[name]
            for b in range(dict((n, c) for n, _, c in EARLY + LATE)[name]):
                acc[base + b * value.shape[0] : base + (b + 1) * value.shape[0]] = value[:, at : at + LANES]
                at += LANES

    d_down = g * z2
    dz2 = g * down * z2 * (1.0 - z2)
    dz2_s[...] = dz2
    d_down_split = split(d_down)
    put(acc_e, ["w_down"], tn(hidden_split, d_down_split))
    d_hidden = nt(d_down_split, (wdh[...], wdl[...]))
    d_up = cat([d_hidden * hu * (sg * (1.0 + hg * (1.0 - sg))), d_hidden * silu], 1)
    d_up_split = split(d_up)
    put(acc_e, ["w_hidden_gate", "w_hidden_up"], tn(n2_split, d_up_split))
    d_n2 = nt(d_up_split, (whh[...], whl[...]))
    dn2_s[...] = d_n2
    sc2 = sc2_s[...]
    dsc2 = d_n2 * nf * sc2 * (1.0 - sc2)
    dsc2_s[...] = dsc2
    cond2_split = split(ns_s[...] * p_s_gain2[...])
    put(acc_e, ["w_scale2", "w_shift2"], tn(cond2_split, split(cat([dsc2, d_n2], 1))))
    d_first = g + norm_back(d_n2 * sc2, nf, rf)
    dfirst_s[...] = d_first
    z1 = z1_s[...]
    d_proj = d_first * z1
    d_proj_split = split(d_proj)
    dz1 = d_first * projected * z1 * (1.0 - z1)
    dz1_s[...] = dz1
    put(acc_e, ["w_out"], tn(gated_split, d_proj_split))
    put(acc_e, ["w_zero1", "w_zero2"], tn(split(single[...]), split(cat([dz1, dz2], 1))))
    d_gated = nt(d_proj_split, (woh[...], wol[...]))
    gate = gate_s[...]
    mixed = mixed_s[...]
    d_gate = d_gated * mixed * gate * (1.0 - gate)
    gpre_s[...] = d_gate
    put(acc_e, ["w_gate"], tn(split(n1_s[...]), split(d_gate)))
    d_mixed = d_gated * gate
    mh_s[...], ml_s[...] = split(d_mixed)
    th_s[...], tl_s[...] = split(d_mixed * mixed)
    if early > EARLY_ROWS:
        acc_e[EARLY_ROWS:] = jnp.zeros((early - EARLY_ROWS, LANES), F32)

    def scatter_core(acc, size, recv, sems):
        half = size // 2
        return [remote(acc.at[span((1 - core) * half, half)], recv, sems[0].at[0], sems[1].at[0], other)]

    def add_core(acc, size, recv):
        mine = span(core * (size // 2), size // 2)
        acc[mine, :] += recv[...]

    def scatter_xy(acc, size, recv, sems):
        half = size // 2
        part = half // nxy
        copies = []
        for o in range(1, nxy):
            kk, device = xy_peer(o)
            source = acc.at[span(core * half + kk * part, part)]
            copies.append(remote(source, recv.at[o - 1], sems[0].at[o - 1], sems[1].at[o - 1], device))
        return copies

    def add_xy(acc, size, recv):
        half = size // 2
        part = half // nxy
        mine = span(core * half + k * part, part)
        value = acc[mine, :]
        for o in range(1, nxy):
            value = value + recv[o - 1]
        acc[mine, :] = value

    def gather_xy(res, size, sems):
        half = size // 2
        part = half // nxy
        mine = span(core * half + k * part, part)
        copies = []
        for o in range(1, nxy):
            at = nxy - 2 + o
            copies.append(remote(res.at[mine], res.at[mine], sems[0].at[at], sems[1].at[at], xy_peer(o)[1]))
        return copies

    def gather_core(res, size, hbm, sems):
        mine = span(core * (size // 2), size // 2)
        return [remote(res.at[mine], hbm.at[mine], sems[0].at[1], sems[1].at[1], other)]

    def keep(res, size, hbm, sem):
        mine = span(core * (size // 2), size // 2)
        return [pltpu.make_async_copy(res.at[mine], hbm.at[mine], sem)]

    ec, exy, ez = (ec_send, ec_recv), (exy_send, exy_recv), (ez_send, ez_recv)
    lc, lxy, lz = (lc_send, lc_recv), (lxy_send, lxy_recv), (lz_send, lz_recv)
    part_e = early // (2 * nxy)
    chunk_e = part_e // nz
    at_e = core * (early // 2) + k * part_e
    part_l = late // (2 * nxy)
    at_l = core * (late // 2) + k * part_l

    e1 = start(scatter_core(acc_e, early, recv_ec, ec))

    dkv[...] = jnp.zeros_like(dkv)
    less = -jnp.ones((KW, LANES), BF16)

    def attend_back(s):
        for w in range(nwin):
            t = s * nwin + w
            at = s * rows + w * WQ
            keys = slice(w * WQ, w * WQ + KW)
            queries = heads_in(qh_s, at), heads_in(ql_s, at)
            mh, ml = heads_in(mh_s, at), heads_in(ml_s, at)
            th, tl = heads_in(th_s, at), heads_in(tl_s, at)
            vh, vl = kvh[s, keys, LANES:], kvl[s, keys, LANES:]
            weights = prob[t]
            d_scores = weights * dot(cat([mh, ml, mh, th, tl], 1), cat([vh, vh, vl, less, less], 1), NT)
            ds[t] = d_scores
            d_split = split(d_scores)
            dq_s[pl.ds(at, WQ), :] = heads_out(nn(d_split, (kvh[s, keys, :LANES], kvl[s, keys, :LANES]))) * scale
            dkv[s, keys, :LANES] += tn(d_split, queries)
            dkv[s, keys, LANES:] += tn(split(weights), (mh, ml))

    for s in range(samples):
        attend_back(s)
        if s == 0:
            wait(e1)
            add_core(acc_e, early, recv_ec)
            e2 = start(scatter_xy(acc_e, early, recv_exy, exy))

    halos = start(
        [
            remote(dkv.at[:, 0:HALO], dhalo.at[1], h_send.at[2], h_recv.at[2], left),
            remote(dkv.at[:, HALO + rows : 2 * HALO + rows], dhalo.at[0], h_send.at[3], h_recv.at[3], right),
        ]
    )

    gacc[...] = jnp.zeros_like(gacc)

    def pair_back(t, carry):
        s, w = t // nwin, lax.rem(t, nwin)
        inv, live = prs[t, 0], prs[t, 1]
        mean = pmean[t]
        u, along, level = [], None, None
        for h in range(heads):
            d = ds[t, h * WQ : (h + 1) * WQ]
            u.append(d * inv)
            a = d * bias[t, h * WQ : (h + 1) * WQ]
            b = u[h] * (wsum[h] * (1.0 / channels))
            along = a if along is None else along + a
            level = b if level is None else level + b
        c1 = along * live
        c0 = mean * c1 - level
        mu = [mean * u[h] for h in range(heads)]
        for p in range(channels):
            v = pair[s, w, p]
            d = c0 - v * c1
            for h in range(heads):
                d = d + u[h] * wg[p][h]
                term = v * u[h] - mu[h]
                gacc[h * channels + p] += (term[0:8] + term[8:16]) + (term[16:24] + term[24:32])
            pair[s, w, p] = d
        return carry

    lax.fori_loop(0, samples * nwin, pair_back, 0)
    outputs += start([pltpu.make_async_copy(pair, g_pair_hbm, out_sem.at[1])])

    wait(halos)
    for s in range(samples):
        dkv[s, HALO : 2 * HALO] += dhalo[0, s]
        dkv[s, rows : rows + HALO] += dhalo[1, s]

    dq = dq_s[...]
    d_keys_values = cat([dkv[s, HALO : HALO + rows] for s in range(samples)], 0)
    d_all = split(cat([dq, d_keys_values, gpre_s[...]], 1))
    d_n1 = nt(d_all, (wqh[...], wql[...]))
    na = na_s[...]
    sc1 = sc1_s[...]
    dsc1 = d_n1 * na * sc1 * (1.0 - sc1)
    d_first1 = split(cat([dsc1, d_n1], 1))
    ns = ns_s[...]
    put(
        acc_l,
        ["w_query", "w_key", "w_value"],
        tn(split(n1_s[...]), (d_all[0][:, : 3 * LANES], d_all[1][:, : 3 * LANES])),
    )
    put(acc_l, ["w_scale1", "w_shift1"], tn(split(ns * p_s_gain1[...]), d_first1))
    d_cond1 = nt(d_first1, (w1h[...], w1l[...]))
    d_cond2 = nt(split(cat([dsc2_s[...], dn2_s[...]], 1)), (w2h[...], w2l[...]))

    eye = (
        lax.broadcasted_iota(jnp.int32, (channels, LANES), 0) == lax.broadcasted_iota(jnp.int32, (channels, LANES), 1)
    ).astype(F32)
    gsum = jnp.sum(jnp.sum(gacc[...], axis=1), axis=-1, keepdims=True)
    rows_g = [column_sum(gsum[h * channels : (h + 1) * channels] * eye) for h in range(heads)]
    blank = jnp.zeros((1, LANES - channels), F32)
    gain_row = cat([p_pair_gain[...], blank], 1)
    pair_row = jnp.zeros((1, LANES), F32)
    for h in range(heads):
        pair_row = pair_row + rows_g[h] * cat([p_w_pair[h : h + 1, :], blank], 1)
    pair_grad = cat([v * gain_row for v in rows_g] + [jnp.zeros((8 - heads, LANES), F32)], 0)
    small = {
        "b_scale1": column_sum(dsc1),
        "b_query": column_sum(dq),
        "b_scale2": column_sum(dsc2_s[...]),
        "b_zero1": column_sum(dz1_s[...]),
        "b_zero2": column_sum(dz2_s[...]),
        "s_gain1": column_sum(d_cond1 * ns),
        "s_gain2": column_sum(d_cond2 * ns),
        "pair_gain": pair_row,
    }
    acc_l[PLACE["vectors"] : PLACE["vectors"] + 8] = cat([small[name] for name in VECTORS], 0)
    acc_l[PLACE["w_pair"] : PLACE["w_pair"] + 8] = pair_grad
    if late > LATE_ROWS:
        acc_l[LATE_ROWS:] = jnp.zeros((late - LATE_ROWS, LANES), F32)

    l1 = start(scatter_core(acc_l, late, recv_lc, lc))
    wait(e2)
    add_xy(acc_e, early, recv_exy)
    copies = []
    for o in range(1, nz):
        zz, device = z_peer(o)
        source = acc_e.at[span(at_e + zz * chunk_e, chunk_e)]
        copies.append(remote(source, recv_ez.at[o - 1], ez_send.at[o - 1], ez_recv.at[o - 1], device))
    e3 = start(copies)
    wait(l1)
    add_core(acc_l, late, recv_lc)
    l2 = start(scatter_xy(acc_l, late, recv_lxy, lxy))

    g_atoms[...] = dfirst_s[...] + norm_back(d_n1 * sc1, na, ra_s[...])
    outputs += start([pltpu.make_async_copy(g_atoms, g_atoms_hbm, out_sem.at[2])])

    wait(e3)
    mine = span(at_e + z * chunk_e, chunk_e)
    value = acc_e[mine, :]
    for o in range(1, nz):
        value = value + recv_ez[o - 1]
    res_e[mine, :] = value
    copies = []
    for o in range(1, nz):
        at = nz - 2 + o
        copies.append(remote(res_e.at[mine], res_e.at[mine], ez_send.at[at], ez_recv.at[at], z_peer(o)[1]))
    e4 = start(copies)

    d_ns = d_cond1 * p_s_gain1[...] + d_cond2 * p_s_gain2[...]
    g_single[...] = norm_back(d_ns, ns, rs_s[...]) + nt(
        split(cat([dz1_s[...], dz2_s[...]], 1)), (wzh[...], wzl[...])
    )
    outputs += start([pltpu.make_async_copy(g_single, g_single_hbm, out_sem.at[3])])

    wait(l2)
    add_xy(acc_l, late, recv_lxy)
    copies = []
    for o in range(1, nz):
        copies.append(
            remote(
                acc_l.at[span(at_l, part_l)], recv_lz.at[z], lz_send.at[o - 1], lz_recv.at[o - 1], z_peer(o)[1]
            )
        )
    l3 = start(copies)
    wait(e4)
    e5 = start(gather_xy(res_e, early, exy))
    recv_lz[z] = acc_l[span(at_l, part_l), :]
    wait(l3)
    value = recv_lz[0]
    for i in range(1, nz):
        value = value + recv_lz[i]
    res_l[span(at_l, part_l), :] = value
    l4 = start(gather_xy(res_l, late, lxy))
    wait(e5)
    e6 = start(gather_core(res_e, early, early_hbm, ec) + keep(res_e, early, early_hbm, out_sem.at[4]))
    wait(l4)
    l5 = start(gather_core(res_l, late, late_hbm, lc) + keep(res_l, late, late_hbm, out_sem.at[5]))
    wait(e6)
    wait(l5)
    wait(outputs)


def unpack_kernel(*refs):
    n, v = len(EARLY) + len(LATE), len(VECTORS)
    ins, refs = refs[:6], refs[6:]
    outs, mats, rows, wp, refs = refs[:4], refs[4 : 4 + n], refs[4 + n : 4 + n + v], refs[4 + n + v], refs[5 + n + v :]
    stage, (in_sems, out_sems) = refs[:6], refs[6:]
    loads, stores = [], []

    def load(a, b):
        loads.append(pltpu.make_async_copy(a, b, in_sems.at[len(loads)]))
        loads[-1].start()
        return loads[-1]

    def store(a, b):
        stores.append(pltpu.make_async_copy(a, b, out_sems.at[len(stores)]))
        stores[-1].start()

    early, late = load(ins[4], stage[4]), load(ins[5], stage[5])
    big = [
        (load(a.at[c], mid.at[c]), mid.at[c], b.at[c])
        for a, mid, b in zip(ins[:4], stage[:4], outs)
        for c in range(a.shape[0])
    ]
    at = 0
    for group, arrived, packed in ((EARLY, early, stage[4]), (LATE, late, stage[5])):
        arrived.wait()
        for name, _, columns in group:
            base, height = PLACE[name], mats[at].shape[0]
            for b in range(columns):
                store(packed.at[pl.ds(base + b * height, height)], mats[at].at[:, pl.ds(b * LANES, LANES)])
            at += 1
    base = PLACE["vectors"]
    for i, ref in enumerate(rows):
        ref[...] = stage[5][base + i : base + i + 1, 0 : ref.shape[1]]
    base = PLACE["w_pair"]
    wp[...] = stage[5][base : base + wp.shape[0], 0 : wp.shape[1]]
    for arrived, mid, b in big:
        arrived.wait()
        store(mid, b)
    for copy in stores:
        copy.wait()


def shards(dpn, seqn, atoms, single_cond, pair_block, atom_count, *rest):
    params, cotangent = dict(zip(PARAMS, rest[:-1])), rest[-1]
    params["w_pair"] = params["w_pair"].T
    samples, rows, width = atoms.shape
    nwin, channels = pair_block.shape[1:3]
    heads = params["w_pair"].shape[0]
    flat = samples * rows
    nz, nx = 4, seqn // 8
    nxy = dpn * nx
    grain_e, grain_l = 8 * 2 * nxy * nz, 8 * 2 * nxy
    early = -(-EARLY_ROWS // grain_e) * grain_e
    late = -(-LATE_ROWS // grain_l) * grain_l
    windows = samples * nwin
    hidden = params["w_down"].shape[0]

    def row(v):
        return v.reshape(1, -1) if v.ndim == 1 else v

    vmem = pl.BlockSpec(memory_space=pltpu.VMEM)
    smem = pl.BlockSpec(memory_space=pltpu.SMEM)
    anyw = pl.BlockSpec(memory_space=pl.ANY)

    def buf(*shape):
        return pltpu.VMEM(shape, F32)

    def low(*shape):
        return [pltpu.VMEM(shape, BF16), pltpu.VMEM(shape, BF16)]

    def sems(n):
        return [pltpu.SemaphoreType.DMA((n,)), pltpu.SemaphoreType.DMA((n,))]

    tall = (flat, width)
    extended = (samples, rows + 2 * HALO, 2 * width)
    scratch = [
        buf(*pair_block.shape),
        buf(windows, heads * WQ, KW),
        buf(windows, WQ, KW),
        buf(windows, 2, WQ, KW),
        buf(windows, heads * WQ, KW),
        buf(windows, heads * WQ, KW),
        buf(*extended),
        buf(*extended),
        buf(2, samples, HALO, 2 * width),
    ]
    scratch += low(*extended)
    scratch += low(width, 2 * width)
    scratch += low(width, 4 * width)
    scratch += low(width, 2 * width)
    scratch += low(width, 2 * width)
    scratch += low(width, 2 * hidden)
    scratch += low(hidden, width)
    scratch += low(width, width)
    scratch += low(*tall) + low(*tall) + low(*tall)
    scratch += [buf(*tall) for _ in range(22)]
    scratch += [
        buf(heads * channels, 8, KW),
        buf(early, LANES),
        buf(early, LANES),
        buf(late, LANES),
        buf(late, LANES),
        buf(early // 2, LANES),
        buf(nxy - 1, early // (2 * nxy), LANES),
        buf(nz - 1, early // (2 * nxy * nz), LANES),
        buf(late // 2, LANES),
        buf(nxy - 1, late // (2 * nxy), LANES),
        buf(nz, late // (2 * nxy), LANES),
        pltpu.SemaphoreType.DMA((samples,)),
        pltpu.SemaphoreType.DMA((6,)),
    ]
    scratch += sems(4) + sems(2) + sems(2 * (nxy - 1)) + sems(2 * (nz - 1))
    scratch += sems(2) + sems(2 * (nxy - 1)) + sems(nz - 1)
    sizes = (samples, rows, dpn, seqn, early, late)
    big = pl.pallas_call(
        functools.partial(block_kernel, sizes),
        out_shape=[
            jax.ShapeDtypeStruct(tall, F32),
            jax.ShapeDtypeStruct(tall, F32),
            jax.ShapeDtypeStruct(tall, F32),
            jax.ShapeDtypeStruct(pair_block.shape, F32),
            jax.ShapeDtypeStruct((early, LANES), F32),
            jax.ShapeDtypeStruct((late, LANES), F32),
        ],
        in_specs=[smem] * 3 + [vmem] * (3 + len(PARAMS)) + [anyw],
        out_specs=[anyw] * 6,
        scratch_shapes=scratch,
        compiler_params=pltpu.CompilerParams(
            collective_id=0, has_side_effects=True, vmem_limit_bytes=60 * 2**20
        ),
        name="block",
    )(
        atom_count,
        params["pair_gain"],
        params["w_pair"],
        atoms.reshape(tall),
        single_cond.reshape(tall),
        cotangent.reshape(tall),
        *[row(params[name]) for name in PARAMS],
        pair_block,
    )

    names = [name for name, _, _ in EARLY + LATE]
    mats = [jax.ShapeDtypeStruct(params[name].shape, F32) for name in names]
    vecs = [jax.ShapeDtypeStruct((1, params[name].shape[0]), F32) for name in VECTORS]
    big = list(big)
    for i in range(3):
        big[i] = big[i].reshape(1, *tall)
    big[3] = big[3].reshape((windows,) + pair_block.shape[2:])
    results = pl.pallas_call(
        unpack_kernel,
        out_shape=[jax.ShapeDtypeStruct(v.shape, F32) for v in big[:4]]
        + mats
        + vecs
        + [jax.ShapeDtypeStruct((heads, channels), F32)],
        in_specs=[anyw] * 6,
        out_specs=[anyw] * (4 + len(mats)) + [vmem] * (len(vecs) + 1),
        scratch_shapes=[buf(*v.shape) for v in big]
        + [
            pltpu.SemaphoreType.DMA((2 + sum(v.shape[0] for v in big[:4]),)),
            pltpu.SemaphoreType.DMA((sum(c for _, _, c in EARLY + LATE) + sum(v.shape[0] for v in big[:4]),)),
        ],
        compiler_params=pltpu.CompilerParams(vmem_limit_bytes=60 * 2**20),
        name="unpack",
    )(*big)
    grads = dict(zip(names, results[4:]))
    for name, value in zip(VECTORS, results[4 + len(mats) :]):
        grads[name] = value.reshape(-1)
    grads["w_pair"] = results[-1].T
    out, g_atoms, g_single, g_pair = results[:4]
    return (
        out.reshape(atoms.shape),
        g_atoms.reshape(atoms.shape),
        g_single.reshape(atoms.shape),
        g_pair.reshape(pair_block.shape),
    ) + tuple(grads[name] for name in PARAMS)


def solution(mesh):
    data = P("dp", "seq", None)
    pairs = P("dp", "seq", None, None, None)
    return jax.shard_map(
        functools.partial(shards, mesh.shape["dp"], mesh.shape["seq"]),
        mesh=mesh,
        in_specs=(data, data, pairs, P("dp")) + (P(),) * len(PARAMS) + (data,),
        out_specs=(data, data, data, pairs) + (P(),) * len(PARAMS),
        check_vma=False,
    )
```

```python
import functools
import math

import jax
import jax.numpy as jnp
from jax import lax
from jax.experimental import pallas as pl
from jax.experimental.pallas import tpu as pltpu
from jax.sharding import PartitionSpec as P

WQ = 32
KW = 128
HALO = 48
LANES = 128
MESH = pl.DeviceIdType.MESH
F32 = jnp.float32

EARLY = (
    ("w_down", 2, 1),
    ("w_hidden_gate", 1, 2),
    ("w_hidden_up", 1, 2),
    ("w_zero2", 1, 1),
    ("w_scale2", 1, 1),
    ("w_shift2", 1, 1),
    ("w_out", 1, 1),
    ("w_zero1", 1, 1),
    ("w_gate", 1, 1),
)
LATE = (
    ("w_query", 1, 1),
    ("w_key", 1, 1),
    ("w_value", 1, 1),
    ("w_scale1", 1, 1),
    ("w_shift1", 1, 1),
)
VECTORS = ("b_scale1", "b_query", "b_scale2", "b_zero1", "b_zero2", "s_gain1", "s_gain2", "pair_gain")
PARAMS = (
    "s_gain1",
    "w_scale1",
    "b_scale1",
    "w_shift1",
    "w_query",
    "b_query",
    "w_key",
    "w_value",
    "w_gate",
    "pair_gain",
    "w_pair",
    "w_out",
    "w_zero1",
    "b_zero1",
    "s_gain2",
    "w_scale2",
    "b_scale2",
    "w_shift2",
    "w_hidden_gate",
    "w_hidden_up",
    "w_down",
    "w_zero2",
    "b_zero2",
)


def offsets():
    place, used = {}, []
    for group in (EARLY, LATE):
        row = 0
        for name, rows, columns in group:
            place[name] = row
            row += rows * columns * LANES
        used.append(row)
    place["vectors"] = used[1]
    place["w_pair"] = used[1] + 8
    return place, used[0], used[1] + 16


PLACE, EARLY_ROWS, LATE_ROWS = offsets()
BF16 = jnp.bfloat16
NN = (((1,), (0,)), ((), ()))
NT = (((1,), (1,)), ((), ()))
TN = (((0,), (0,)), ((), ()))


def dot(a, b, dims):
    return lax.dot_general(a, b, dims, preferred_element_type=F32)


def cat(parts, axis):
    return jnp.concatenate(parts, axis=axis)


def split(x):
    high = x.astype(BF16)
    return high, (x - high.astype(F32)).astype(BF16)


def product(a, b, dims):
    (ah, al), (bh, bl) = a, b
    (ka,), (kb,) = dims[0]
    return dot(cat([ah, al, ah], ka), cat([bh, bh, bl], kb), dims)


def nn(a, b):
    return product(a, b, NN)


def nt(a, b):
    return product(a, b, NT)


def tn(a, b):
    return product(a, b, TN)


def mean_lanes(x):
    weight = jnp.full((2 * LANES, LANES), 1.0 / LANES, BF16)
    return dot(cat(split(x), 1), weight, NN)


def norm(x):
    cent = x - mean_lanes(x)
    inv = lax.rsqrt(mean_lanes(cent * cent) + 1e-05)
    return cent * inv, inv


def norm_back(d, xhat, inv):
    return (d - mean_lanes(d) - xhat * mean_lanes(d * xhat)) * inv


def sigmoid(x):
    return 1.0 / (1.0 + jnp.exp(-x))


def column_sum(x):
    return jnp.sum(x, axis=0, keepdims=True)


def block_kernel(sizes, *refs):
    samples, rows, dpn, seqn, early, late = sizes
    nwin = rows // WQ
    windows = samples * nwin
    flat = samples * rows
    nz = 4
    nx = seqn // (2 * nz)
    nxy = dpn * nx
    n_in = 6 + len(PARAMS)
    given, refs = refs[:n_in], refs[n_in:]
    held, refs = refs[-n_in - 1 : -1], refs[:-n_in - 1] + refs[-1:]
    (
        count,
        gain_s,
        wpair_s,
        atoms,
        single,
        cot,
        p_s_gain1,
        p_w_scale1,
        p_b_scale1,
        p_w_shift1,
        p_w_query,
        p_b_query,
        p_w_key,
        p_w_value,
        p_w_gate,
        p_pair_gain,
        p_w_pair,
        p_w_out,
        p_w_zero1,
        p_b_zero1,
        p_s_gain2,
        p_w_scale2,
        p_b_scale2,
        p_w_shift2,
        p_w_hidden_gate,
        p_w_hidden_up,
        p_w_down,
        p_w_zero2,
        p_b_zero2,
    ) = held
    (
        pair_hbm,
        out,
        g_atoms,
        g_single,
        g_pair,
        res_e,
        res_l,
        pair,
        bias,
        pmean,
        prs,
        prob,
        ds,
        kv,
        dkv,
        dhalo,
        kvh,
        kvl,
        w1h,
        w1l,
        wqh,
        wql,
        wzh,
        wzl,
        w2h,
        w2l,
        whh,
        whl,
        wdh,
        wdl,
        woh,
        wol,
        qh_s,
        ql_s,
        mh_s,
        ml_s,
        th_s,
        tl_s,
        mixed_s,
        ns_s,
        na_s,
        n1_s,
        sc1_s,
        sc2_s,
        sh2_s,
        gate_s,
        z1_s,
        z2_s,
        rs_s,
        ra_s,
        dq_s,
        dfirst_s,
        dz1_s,
        dz2_s,
        dn2_s,
        dsc2_s,
        gpre_s,
        gacc,
        acc_e,
        acc_l,
        recv_ec,
        recv_exy,
        recv_ez,
        recv_lc,
        recv_lxy,
        recv_lz,
        pair_sem,
        h_send,
        h_recv,
        ec_send,
        ec_recv,
        exy_send,
        exy_recv,
        ez_send,
        ez_recv,
        lc_send,
        lc_recv,
        lxy_send,
        lxy_recv,
        lz_send,
        lz_recv,
        in_sem,
    ) = refs
    dp = lax.axis_index("dp")
    me = lax.axis_index("seq")
    core = lax.rem(me, 2)
    x = lax.rem(me // 2, nx)
    z = me // (2 * nx)
    k = dp * nx + x
    left = (dp, lax.rem(me + seqn - 1, seqn))
    right = (dp, lax.rem(me + 1, seqn))
    other = (dp, me + 1 - 2 * core)

    def xy_peer(o):
        kk = lax.rem(k + o, nxy)
        return kk, (kk // nx, (z * nx + lax.rem(kk, nx)) * 2 + core)

    def z_peer(o):
        zz = lax.rem(z + o, nz)
        return zz, (dp, (zz * nx + x) * 2 + core)

    def load(ref):
        i = [ref is h for h in held].index(True)
        return pltpu.make_async_copy(given[i], ref, in_sem.at[i])

    def bring(*which):
        for ref in which:
            load(ref).start()

    def ready(*which):
        for ref in which:
            load(ref).wait()

    norms = (single, atoms, p_s_gain1, p_w_scale1, p_w_shift1, p_b_scale1)
    projections = (p_w_query, p_w_key, p_w_value, p_w_gate, p_b_query)
    scalars = (count, gain_s, wpair_s)
    conditions = (p_w_zero1, p_w_zero2, p_w_scale2, p_w_shift2, p_s_gain2, p_b_scale2, p_b_zero1, p_b_zero2)
    transition = (p_w_hidden_gate, p_w_hidden_up, p_w_down, p_w_out, cot, p_pair_gain, p_w_pair)
    bring(*norms, *projections, *scalars)
    for s in range(samples):
        pltpu.make_async_copy(pair_hbm.at[s], pair.at[s], pair_sem.at[s]).start()
    bring(*conditions, *transition)

    barrier = pltpu.get_barrier_semaphore()
    greeted = [left, right, other]
    greeted += [xy_peer(o)[1] for o in range(1, nxy)]
    greeted += [z_peer(o)[1] for o in range(1, nz)]
    for device in greeted:
        pl.semaphore_signal(barrier, inc=1, device_id=device, device_id_type=MESH)

    def remote(src, dst, send, recv, device):
        return pltpu.make_async_remote_copy(
            src_ref=src, dst_ref=dst, send_sem=send, recv_sem=recv, device_id=device, device_id_type=MESH
        )

    def start(copies):
        for copy in copies:
            copy.start()
        return copies

    def wait(copies):
        for copy in copies:
            copy.wait()

    def span(first, size):
        return pl.ds(pl.multiple_of(first, 8), size)

    def hold(high, low, *weights):
        for c, w in enumerate(weights):
            width = w.shape[1]
            high[:, c * width : (c + 1) * width], low[:, c * width : (c + 1) * width] = split(w[...])

    ready(*norms)
    hold(w1h, w1l, p_w_scale1, p_w_shift1)
    ns, rs = norm(single[...])
    na, ra = norm(atoms[...])
    ns_s[...] = ns
    na_s[...] = na
    rs_s[...] = rs
    ra_s[...] = ra
    first1 = nn(split(ns * p_s_gain1[...]), (w1h[...], w1l[...]))
    sc1 = sigmoid(first1[:, :LANES] + p_b_scale1[...])
    sc1_s[...] = sc1
    n1 = sc1 * na + first1[:, LANES:]
    n1_s[...] = n1
    n1_split = split(n1)
    ready(*projections)
    hold(wqh, wql, p_w_query, p_w_key, p_w_value, p_w_gate)
    keys_values = nn(n1_split, (wqh[:, LANES : 3 * LANES], wql[:, LANES : 3 * LANES]))
    for s in range(samples):
        kv[s, HALO : HALO + rows] = keys_values[s * rows : (s + 1) * rows]

    pl.semaphore_wait(barrier, len(greeted))
    halos = start(
        [
            remote(kv.at[:, rows : rows + HALO], kv.at[:, 0:HALO], h_send.at[0], h_recv.at[0], right),
            remote(
                kv.at[:, HALO : 2 * HALO], kv.at[:, HALO + rows : 2 * HALO + rows], h_send.at[1], h_recv.at[1], left
            ),
        ]
    )

    ready(*conditions, *transition)
    hold(wzh, wzl, p_w_zero1, p_w_zero2)
    hold(w2h, w2l, p_w_scale2, p_w_shift2)
    hold(whh, whl, p_w_hidden_gate, p_w_hidden_up)
    hold(wdh, wdl, p_w_down)
    hold(woh, wol, p_w_out)
    scale = 1.0 / math.sqrt(32)
    query = (nn(n1_split, (wqh[:, :LANES], wql[:, :LANES])) + p_b_query[...]) * scale
    qh_s[...], ql_s[...] = split(query)
    gate_s[...] = sigmoid(nn(n1_split, (wqh[:, 3 * LANES :], wql[:, 3 * LANES :])))
    first2 = nn(split(ns * p_s_gain2[...]), (w2h[...], w2l[...]))
    sc2_s[...] = sigmoid(first2[:, :LANES] + p_b_scale2[...])
    sh2_s[...] = first2[:, LANES:]
    zeros = nn(split(single[...]), (wzh[...], wzl[...]))
    z1_s[...] = sigmoid(zeros[:, :LANES] + p_b_zero1[...])
    z2_s[...] = sigmoid(zeros[:, LANES:] + p_b_zero2[...])

    ready(*scalars)
    channels = gain_s.shape[0]
    heads = wpair_s.shape[0]
    wg = [[gain_s[p] * wpair_s[h, p] for h in range(heads)] for p in range(channels)]
    wsum = [functools.reduce(lambda a, b: a + b, [wg[p][h] for p in range(channels)]) for h in range(heads)]

    for s in range(samples):
        pltpu.make_async_copy(pair_hbm.at[s], pair.at[s], pair_sem.at[s]).wait()

    key_lane = lax.broadcasted_iota(jnp.int32, (WQ, KW), 1)
    same = key_lane == lax.broadcasted_iota(jnp.int32, (WQ, KW), 0) + HALO

    def pair_bias(t, carry):
        s, w = t // nwin, lax.rem(t, nwin)
        first = pair[s, w, 0]
        total, square = first, first * first
        b = [first * wg[0][h] for h in range(heads)]
        for p in range(1, channels):
            v = pair[s, w, p]
            total = total + v
            square = square + v * v
            b = [b[h] + v * wg[p][h] for h in range(heads)]
        mean = total * (1.0 / channels)
        var = square * (1.0 / channels) - mean * mean
        inv = lax.rsqrt(jnp.maximum(var, 0.25))
        pmean[t] = mean
        live = jnp.where(var > 0.25, 1.0, jnp.where(var == 0.25, 0.5, 0.0))
        prs[t, 0] = inv
        prs[t, 1] = inv * inv * live * (1.0 / channels)
        begin = me * rows + w * WQ - HALO
        valid = ((key_lane >= -begin) & (key_lane < count[s] - begin)) | same
        for h in range(heads):
            bias[t, h * WQ : (h + 1) * WQ] = jnp.where(valid, inv * (b[h] - mean * wsum[h]), -1e9)
        return carry

    lax.fori_loop(0, samples * nwin, pair_bias, 0)

    wait(halos)
    for s in range(samples):
        kv[s, 0:HALO] = jnp.where(me == 0, 0.0, kv[s, 0:HALO])
        kv[s, HALO + rows :] = jnp.where(me == seqn - 1, 0.0, kv[s, HALO + rows :])
    kvh[...], kvl[...] = split(kv[...])

    lane = lax.broadcasted_iota(jnp.int32, (heads * WQ, LANES), 1)
    row = lax.broadcasted_iota(jnp.int32, (heads * WQ, LANES), 0)
    own = (lane // 32 == row // WQ).astype(F32)
    own_low = own.astype(BF16)
    ones = jnp.ones((KW, LANES), BF16)
    nothing = jnp.zeros((KW, LANES), BF16)

    def heads_in(ref, at):
        return cat([ref[at, :]] * heads, 0) * own_low

    def heads_out(v):
        v = v * own
        return (v[0:WQ] + v[WQ : 2 * WQ]) + (v[2 * WQ : 3 * WQ] + v[3 * WQ : 4 * WQ])

    def window(t):
        s, w = divmod(t, nwin)
        return s, slice(s * rows + w * WQ, s * rows + (w + 1) * WQ), slice(w * WQ, w * WQ + KW)

    for t in range(windows):
        s, at, keys = window(t)
        queries = heads_in(qh_s, at), heads_in(ql_s, at)
        prob[t] = nt(queries, (kvh[s, keys, :LANES], kvl[s, keys, :LANES])) + bias[t]
    for t in range(windows):
        s, at, keys = window(t)
        scores = prob[t]
        expo = jnp.exp(scores - jnp.max(scores, axis=-1, keepdims=True))
        eh, el = split(expo)
        vh, vl = kvh[s, keys, LANES:], kvl[s, keys, LANES:]
        high = cat([vh, ones], 1)
        both = dot(cat([eh, el, eh], 1), cat([high, high, cat([vl, nothing], 1)], 0), NN)
        inv = 1.0 / both[:, LANES:]
        prob[t] = expo * inv
        mixed_s[at, :] = heads_out(both[:, :LANES] * inv)

    gated = gate_s[...] * mixed_s[...]
    gated_split = split(gated)
    projected = nn(gated_split, (woh[...], wol[...]))
    first = atoms[...] + z1_s[...] * projected
    nf, rf = norm(first)
    n2 = sc2_s[...] * nf + sh2_s[...]
    n2_split = split(n2)
    up = nn(n2_split, (whh[...], whl[...]))
    hidden_width = up.shape[1] // 2
    hg, hu = up[:, :hidden_width], up[:, hidden_width:]
    sg = sigmoid(hg)
    silu = hg * sg
    hidden = silu * hu
    hidden_split = split(hidden)
    down = nn(hidden_split, (wdh[...], wdl[...]))
    z2 = z2_s[...]
    g = cot[...]
    out[...] = first + z2 * down

    def put(acc, names, value):
        at = 0
        for name in names:
            base = PLACE[name]
            for b in range(dict((n, c) for n, _, c in EARLY + LATE)[name]):
                acc[base + b * value.shape[0] : base + (b + 1) * value.shape[0]] = value[:, at : at + LANES]
                at += LANES

    d_down = g * z2
    dz2 = g * down * z2 * (1.0 - z2)
    dz2_s[...] = dz2
    d_down_split = split(d_down)
    put(acc_e, ["w_down"], tn(hidden_split, d_down_split))
    d_hidden = nt(d_down_split, (wdh[...], wdl[...]))
    d_up = cat([d_hidden * hu * (sg * (1.0 + hg * (1.0 - sg))), d_hidden * silu], 1)
    d_up_split = split(d_up)
    put(acc_e, ["w_hidden_gate", "w_hidden_up"], tn(n2_split, d_up_split))
    d_n2 = nt(d_up_split, (whh[...], whl[...]))
    dn2_s[...] = d_n2
    sc2 = sc2_s[...]
    dsc2 = d_n2 * nf * sc2 * (1.0 - sc2)
    dsc2_s[...] = dsc2
    cond2_split = split(ns_s[...] * p_s_gain2[...])
    put(acc_e, ["w_scale2", "w_shift2"], tn(cond2_split, split(cat([dsc2, d_n2], 1))))
    d_first = g + norm_back(d_n2 * sc2, nf, rf)
    dfirst_s[...] = d_first
    z1 = z1_s[...]
    d_proj = d_first * z1
    d_proj_split = split(d_proj)
    dz1 = d_first * projected * z1 * (1.0 - z1)
    dz1_s[...] = dz1
    put(acc_e, ["w_out"], tn(gated_split, d_proj_split))
    put(acc_e, ["w_zero1", "w_zero2"], tn(split(single[...]), split(cat([dz1, dz2], 1))))
    d_gated = nt(d_proj_split, (woh[...], wol[...]))
    gate = gate_s[...]
    mixed = mixed_s[...]
    d_gate = d_gated * mixed * gate * (1.0 - gate)
    gpre_s[...] = d_gate
    put(acc_e, ["w_gate"], tn(split(n1_s[...]), split(d_gate)))
    d_mixed = d_gated * gate
    mh_s[...], ml_s[...] = split(d_mixed)
    th_s[...], tl_s[...] = split(d_mixed * mixed)
    if early > EARLY_ROWS:
        acc_e[EARLY_ROWS:] = jnp.zeros((early - EARLY_ROWS, LANES), F32)

    def scatter_core(acc, size, recv, sems):
        half = size // 2
        return [remote(acc.at[span((1 - core) * half, half)], recv, sems[0].at[0], sems[1].at[0], other)]

    def add_core(acc, size, recv):
        mine = span(core * (size // 2), size // 2)
        acc[mine, :] += recv[...]

    def scatter_xy(acc, size, recv, sems):
        half = size // 2
        part = half // nxy
        copies = []
        for o in range(1, nxy):
            kk, device = xy_peer(o)
            source = acc.at[span(core * half + kk * part, part)]
            copies.append(remote(source, recv.at[o - 1], sems[0].at[o - 1], sems[1].at[o - 1], device))
        return copies

    def add_xy(acc, size, recv):
        half = size // 2
        part = half // nxy
        mine = span(core * half + k * part, part)
        value = acc[mine, :]
        for o in range(1, nxy):
            value = value + recv[o - 1]
        acc[mine, :] = value

    def gather_xy(res, size, sems):
        half = size // 2
        part = half // nxy
        mine = span(core * half + k * part, part)
        copies = []
        for o in range(1, nxy):
            at = nxy - 2 + o
            copies.append(remote(res.at[mine], res.at[mine], sems[0].at[at], sems[1].at[at], xy_peer(o)[1]))
        return copies

    def gather_core(res, size, sems):
        mine = span(core * (size // 2), size // 2)
        return [remote(res.at[mine], res.at[mine], sems[0].at[1], sems[1].at[1], other)]

    ec, exy, ez = (ec_send, ec_recv), (exy_send, exy_recv), (ez_send, ez_recv)
    lc, lxy, lz = (lc_send, lc_recv), (lxy_send, lxy_recv), (lz_send, lz_recv)
    part_e = early // (2 * nxy)
    chunk_e = part_e // nz
    at_e = core * (early // 2) + k * part_e
    part_l = late // (2 * nxy)
    at_l = core * (late // 2) + k * part_l

    e1 = start(scatter_core(acc_e, early, recv_ec, ec))

    dkv[...] = jnp.zeros_like(dkv)
    less = -jnp.ones((KW, LANES), BF16)

    for t in range(windows):
        s, at, keys = window(t)
        mh, ml = heads_in(mh_s, at), heads_in(ml_s, at)
        th, tl = heads_in(th_s, at), heads_in(tl_s, at)
        vh, vl = kvh[s, keys, LANES:], kvl[s, keys, LANES:]
        ds[t] = prob[t] * dot(cat([mh, ml, mh, th, tl], 1), cat([vh, vh, vl, less, less], 1), NT)

    wait(e1)
    add_core(acc_e, early, recv_ec)
    e2 = start(scatter_xy(acc_e, early, recv_exy, exy))

    for t in range(windows):
        s, at, keys = window(t)
        dkv[s, keys, :LANES] += tn(split(ds[t]), (heads_in(qh_s, at), heads_in(ql_s, at)))
    for t in range(windows):
        s, at, keys = window(t)
        dkv[s, keys, LANES:] += tn(split(prob[t]), (heads_in(mh_s, at), heads_in(ml_s, at)))

    halos = start(
        [
            remote(dkv.at[:, 0:HALO], dhalo.at[1], h_send.at[2], h_recv.at[2], left),
            remote(dkv.at[:, HALO + rows : 2 * HALO + rows], dhalo.at[0], h_send.at[3], h_recv.at[3], right),
        ]
    )

    for t in range(windows):
        s, at, keys = window(t)
        dq_s[at, :] = heads_out(nn(split(ds[t]), (kvh[s, keys, :LANES], kvl[s, keys, :LANES]))) * scale

    gacc[...] = jnp.zeros_like(gacc)

    def pair_back(t, carry):
        s, w = t // nwin, lax.rem(t, nwin)
        inv, live = prs[t, 0], prs[t, 1]
        mean = pmean[t]
        u, along, level = [], None, None
        for h in range(heads):
            d = ds[t, h * WQ : (h + 1) * WQ]
            u.append(d * inv)
            a = d * bias[t, h * WQ : (h + 1) * WQ]
            b = u[h] * (wsum[h] * (1.0 / channels))
            along = a if along is None else along + a
            level = b if level is None else level + b
        c1 = along * live
        c0 = mean * c1 - level
        mu = [mean * u[h] for h in range(heads)]
        for p in range(channels):
            v = pair[s, w, p]
            d = c0 - v * c1
            for h in range(heads):
                d = d + u[h] * wg[p][h]
                term = v * u[h] - mu[h]
                gacc[h * channels + p] += (term[0:8] + term[8:16]) + (term[16:24] + term[24:32])
            g_pair[s, w, p] = d
        return carry

    lax.fori_loop(0, samples * nwin, pair_back, 0)

    wait(halos)
    for s in range(samples):
        dkv[s, HALO : 2 * HALO] += dhalo[0, s]
        dkv[s, rows : rows + HALO] += dhalo[1, s]

    dq = dq_s[...]
    d_keys_values = cat([dkv[s, HALO : HALO + rows] for s in range(samples)], 0)
    d_all = split(cat([dq, d_keys_values, gpre_s[...]], 1))
    d_n1 = nt(d_all, (wqh[...], wql[...]))
    na = na_s[...]
    sc1 = sc1_s[...]
    dsc1 = d_n1 * na * sc1 * (1.0 - sc1)
    d_first1 = split(cat([dsc1, d_n1], 1))
    ns = ns_s[...]
    put(
        acc_l,
        ["w_query", "w_key", "w_value"],
        tn(split(n1_s[...]), (d_all[0][:, : 3 * LANES], d_all[1][:, : 3 * LANES])),
    )
    put(acc_l, ["w_scale1", "w_shift1"], tn(split(ns * p_s_gain1[...]), d_first1))
    d_cond1 = nt(d_first1, (w1h[...], w1l[...]))
    d_cond2 = nt(split(cat([dsc2_s[...], dn2_s[...]], 1)), (w2h[...], w2l[...]))

    eye = (
        lax.broadcasted_iota(jnp.int32, (channels, LANES), 0) == lax.broadcasted_iota(jnp.int32, (channels, LANES), 1)
    ).astype(F32)
    gsum = jnp.sum(jnp.sum(gacc[...], axis=1), axis=-1, keepdims=True)
    rows_g = [column_sum(gsum[h * channels : (h + 1) * channels] * eye) for h in range(heads)]
    blank = jnp.zeros((1, LANES - channels), F32)
    gain_row = cat([p_pair_gain[...], blank], 1)
    pair_row = jnp.zeros((1, LANES), F32)
    for h in range(heads):
        pair_row = pair_row + rows_g[h] * cat([p_w_pair[h : h + 1, :], blank], 1)
    pair_grad = cat([v * gain_row for v in rows_g] + [jnp.zeros((8 - heads, LANES), F32)], 0)
    small = {
        "b_scale1": column_sum(dsc1),
        "b_query": column_sum(dq),
        "b_scale2": column_sum(dsc2_s[...]),
        "b_zero1": column_sum(dz1_s[...]),
        "b_zero2": column_sum(dz2_s[...]),
        "s_gain1": column_sum(d_cond1 * ns),
        "s_gain2": column_sum(d_cond2 * ns),
        "pair_gain": pair_row,
    }
    acc_l[PLACE["vectors"] : PLACE["vectors"] + 8] = cat([small[name] for name in VECTORS], 0)
    acc_l[PLACE["w_pair"] : PLACE["w_pair"] + 8] = pair_grad
    if late > LATE_ROWS:
        acc_l[LATE_ROWS:] = jnp.zeros((late - LATE_ROWS, LANES), F32)

    l1 = start(scatter_core(acc_l, late, recv_lc, lc))
    wait(e2)
    add_xy(acc_e, early, recv_exy)
    copies = []
    for o in range(1, nz):
        zz, device = z_peer(o)
        source = acc_e.at[span(at_e + zz * chunk_e, chunk_e)]
        copies.append(remote(source, recv_ez.at[o - 1], ez_send.at[o - 1], ez_recv.at[o - 1], device))
    e3 = start(copies)
    wait(l1)
    add_core(acc_l, late, recv_lc)
    l2 = start(scatter_xy(acc_l, late, recv_lxy, lxy))

    g_atoms[...] = dfirst_s[...] + norm_back(d_n1 * sc1, na, ra_s[...])

    wait(e3)
    mine = span(at_e + z * chunk_e, chunk_e)
    value = acc_e[mine, :]
    for o in range(1, nz):
        value = value + recv_ez[o - 1]
    res_e[mine, :] = value
    copies = []
    for o in range(1, nz):
        at = nz - 2 + o
        copies.append(remote(res_e.at[mine], res_e.at[mine], ez_send.at[at], ez_recv.at[at], z_peer(o)[1]))
    e4 = start(copies)

    d_ns = d_cond1 * p_s_gain1[...] + d_cond2 * p_s_gain2[...]
    g_single[...] = norm_back(d_ns, ns, rs_s[...]) + nt(
        split(cat([dz1_s[...], dz2_s[...]], 1)), (wzh[...], wzl[...])
    )

    wait(l2)
    add_xy(acc_l, late, recv_lxy)
    copies = []
    for o in range(1, nz):
        copies.append(
            remote(
                acc_l.at[span(at_l, part_l)], recv_lz.at[z], lz_send.at[o - 1], lz_recv.at[o - 1], z_peer(o)[1]
            )
        )
    l3 = start(copies)
    wait(e4)
    e5 = start(gather_xy(res_e, early, exy))
    recv_lz[z] = acc_l[span(at_l, part_l), :]
    wait(l3)
    value = recv_lz[0]
    for i in range(1, nz):
        value = value + recv_lz[i]
    res_l[span(at_l, part_l), :] = value
    l4 = start(gather_xy(res_l, late, lxy))
    wait(e5)
    e6 = start(gather_core(res_e, early, ec))
    wait(l4)
    l5 = start(gather_core(res_l, late, lc))
    wait(e6)
    wait(l5)


def unpack_kernel(*refs):
    n, v = len(EARLY) + len(LATE), len(VECTORS)
    ins, refs = refs[:6], refs[6:]
    outs, mats, rows, wp, sems = refs[:4], refs[4 : 4 + n], refs[4 + n : 4 + n + v], refs[4 + n + v], refs[5 + n + v]
    copies = []

    def move(a, b):
        copies.append(pltpu.make_async_copy(a, b, sems.at[len(copies)]))
        copies[-1].start()

    for a, b in zip(ins[3::-1], outs[::-1]):
        for c in range(a.shape[0]):
            move(a.at[c], b.at[c])
    at = 0
    for group, packed in ((EARLY, ins[4]), (LATE, ins[5])):
        for name, _, columns in group:
            base, height = PLACE[name], mats[at].shape[0]
            for b in range(columns):
                move(packed.at[pl.ds(base + b * height, height)], mats[at].at[:, pl.ds(b * LANES, LANES)])
            at += 1
    base = PLACE["vectors"]
    for i, ref in enumerate(rows):
        ref[...] = ins[5][base + i : base + i + 1, 0 : ref.shape[1]]
    base = PLACE["w_pair"]
    wp[...] = ins[5][base : base + wp.shape[0], 0 : wp.shape[1]]
    for copy in copies:
        copy.wait()


def shards(dpn, seqn, atoms, single_cond, pair_block, atom_count, *rest):
    params, cotangent = dict(zip(PARAMS, rest[:-1])), rest[-1]
    params["w_pair"] = params["w_pair"].T
    samples, rows, width = atoms.shape
    nwin, channels = pair_block.shape[1:3]
    heads = params["w_pair"].shape[0]
    flat = samples * rows
    nz, nx = 4, seqn // 8
    nxy = dpn * nx
    grain_e, grain_l = 8 * 2 * nxy * nz, 8 * 2 * nxy
    early = -(-EARLY_ROWS // grain_e) * grain_e
    late = -(-LATE_ROWS // grain_l) * grain_l
    windows = samples * nwin
    hidden = params["w_down"].shape[0]

    def row(v):
        return v.reshape(1, -1) if v.ndim == 1 else v

    vmem = pl.BlockSpec(memory_space=pltpu.VMEM)
    anyw = pl.BlockSpec(memory_space=pl.ANY)

    def buf(*shape):
        return pltpu.VMEM(shape, F32)

    def low(*shape):
        return [pltpu.VMEM(shape, BF16), pltpu.VMEM(shape, BF16)]

    def sems(n):
        return [pltpu.SemaphoreType.DMA((n,)), pltpu.SemaphoreType.DMA((n,))]

    tall = (flat, width)
    extended = (samples, rows + 2 * HALO, 2 * width)
    scratch = [
        buf(*pair_block.shape),
        buf(windows, heads * WQ, KW),
        buf(windows, WQ, KW),
        buf(windows, 2, WQ, KW),
        buf(windows, heads * WQ, KW),
        buf(windows, heads * WQ, KW),
        buf(*extended),
        buf(*extended),
        buf(2, samples, HALO, 2 * width),
    ]
    scratch += low(*extended)
    scratch += low(width, 2 * width)
    scratch += low(width, 4 * width)
    scratch += low(width, 2 * width)
    scratch += low(width, 2 * width)
    scratch += low(width, 2 * hidden)
    scratch += low(hidden, width)
    scratch += low(width, width)
    scratch += low(*tall) + low(*tall) + low(*tall)
    scratch += [buf(*tall) for _ in range(19)]
    scratch += [
        buf(heads * channels, 8, KW),
        buf(early, LANES),
        buf(late, LANES),
        buf(early // 2, LANES),
        buf(nxy - 1, early // (2 * nxy), LANES),
        buf(nz - 1, early // (2 * nxy * nz), LANES),
        buf(late // 2, LANES),
        buf(nxy - 1, late // (2 * nxy), LANES),
        buf(nz, late // (2 * nxy), LANES),
        pltpu.SemaphoreType.DMA((samples,)),
    ]
    scratch += sems(4) + sems(2) + sems(2 * (nxy - 1)) + sems(2 * (nz - 1))
    scratch += sems(2) + sems(2 * (nxy - 1)) + sems(nz - 1)
    arrays = [
        atom_count,
        params["pair_gain"],
        params["w_pair"],
        atoms.reshape(tall),
        single_cond.reshape(tall),
        cotangent.reshape(tall),
        *[row(params[name]) for name in PARAMS],
        pair_block,
    ]
    scratch += [pltpu.SMEM(v.shape, v.dtype) for v in arrays[:3]]
    scratch += [buf(*v.shape) for v in arrays[3:-1]]
    scratch += [pltpu.SemaphoreType.DMA((len(arrays) - 1,))]
    sizes = (samples, rows, dpn, seqn, early, late)
    big = pl.pallas_call(
        functools.partial(block_kernel, sizes),
        out_shape=[buf(*shape) for shape in (tall, tall, tall, pair_block.shape, (early, LANES), (late, LANES))],
        in_specs=[anyw] * (7 + len(PARAMS)),
        out_specs=[vmem] * 6,
        scratch_shapes=scratch,
        compiler_params=pltpu.CompilerParams(
            collective_id=0, has_side_effects=True, vmem_limit_bytes=40 * 2**20
        ),
        name="block",
    )(*[pltpu.with_memory_space_constraint(v, pltpu.HBM) for v in arrays])

    names = [name for name, _, _ in EARLY + LATE]
    mats = [jax.ShapeDtypeStruct(params[name].shape, F32) for name in names]
    vecs = [jax.ShapeDtypeStruct((1, params[name].shape[0]), F32) for name in VECTORS]
    big = list(big)
    for i in range(3):
        big[i] = big[i].reshape(1, *tall)
    results = pl.pallas_call(
        unpack_kernel,
        out_shape=[jax.ShapeDtypeStruct(v.shape, F32) for v in big[:4]]
        + mats
        + vecs
        + [jax.ShapeDtypeStruct((heads, channels), F32)],
        in_specs=[vmem] * 6,
        out_specs=[anyw] * (4 + len(mats)) + [vmem] * (len(vecs) + 1),
        scratch_shapes=[
            pltpu.SemaphoreType.DMA((sum(c for _, _, c in EARLY + LATE) + sum(v.shape[0] for v in big[:4]),)),
        ],
        compiler_params=pltpu.CompilerParams(vmem_limit_bytes=16 * 2**20),
        name="unpack",
    )(*[pltpu.with_memory_space_constraint(v, pltpu.VMEM) for v in big])
    grads = dict(zip(names, results[4:]))
    for name, value in zip(VECTORS, results[4 + len(mats) :]):
        grads[name] = value.reshape(-1)
    grads["w_pair"] = results[-1].T
    out, g_atoms, g_single, g_pair = results[:4]
    return (
        out.reshape(atoms.shape),
        g_atoms.reshape(atoms.shape),
        g_single.reshape(atoms.shape),
        g_pair.reshape(pair_block.shape),
    ) + tuple(grads[name] for name in PARAMS)


def solution(mesh):
    data = P("dp", "seq", None)
    pairs = P("dp", "seq", None, None, None)
    return jax.shard_map(
        functools.partial(shards, mesh.shape["dp"], mesh.shape["seq"]),
        mesh=mesh,
        in_specs=(data, data, pairs, P("dp")) + (P(),) * len(PARAMS) + (data,),
        out_specs=(data, data, data, pairs) + (P(),) * len(PARAMS),
        check_vma=False,
    )
```

```python
import functools
import math

import jax
import jax.numpy as jnp
from jax import lax
from jax.experimental import pallas as pl
from jax.experimental.pallas import tpu as pltpu
from jax.sharding import PartitionSpec as P

WQ = 32
KW = 128
HALO = 48
LANES = 128
MESH = pl.DeviceIdType.MESH
F32 = jnp.float32

EARLY = (
    ("w_down", 2, 1),
    ("w_hidden_gate", 1, 2),
    ("w_hidden_up", 1, 2),
    ("w_zero2", 1, 1),
    ("w_scale2", 1, 1),
    ("w_shift2", 1, 1),
    ("w_out", 1, 1),
    ("w_zero1", 1, 1),
    ("w_gate", 1, 1),
)
LATE = (
    ("w_query", 1, 1),
    ("w_key", 1, 1),
    ("w_value", 1, 1),
    ("w_scale1", 1, 1),
    ("w_shift1", 1, 1),
)
VECTORS = ("b_scale1", "b_query", "b_scale2", "b_zero1", "b_zero2", "s_gain1", "s_gain2", "pair_gain")
PARAMS = (
    "s_gain1",
    "w_scale1",
    "b_scale1",
    "w_shift1",
    "w_query",
    "b_query",
    "w_key",
    "w_value",
    "w_gate",
    "pair_gain",
    "w_pair",
    "w_out",
    "w_zero1",
    "b_zero1",
    "s_gain2",
    "w_scale2",
    "b_scale2",
    "w_shift2",
    "w_hidden_gate",
    "w_hidden_up",
    "w_down",
    "w_zero2",
    "b_zero2",
)


def offsets():
    place, used = {}, []
    for group in (EARLY, LATE):
        row = 0
        for name, rows, columns in group:
            place[name] = row
            row += rows * columns * LANES
        used.append(row)
    return place, used[0], used[1]


PLACE, EARLY_ROWS, LATE_ROWS = offsets()
BF16 = jnp.bfloat16
NN = (((1,), (0,)), ((), ()))
NT = (((1,), (1,)), ((), ()))
TN = (((0,), (0,)), ((), ()))


def dot(a, b, dims):
    return lax.dot_general(a, b, dims, preferred_element_type=F32)


def cat(parts, axis):
    return jnp.concatenate(parts, axis=axis)


def split(x):
    high = x.astype(BF16)
    return high, (x - high.astype(F32)).astype(BF16)


def product(a, b, dims):
    (ah, al), (bh, bl) = a, b
    (ka,), (kb,) = dims[0]
    return dot(cat([ah, al, ah], ka), cat([bh, bh, bl], kb), dims)


def nn(a, b):
    return product(a, b, NN)


def nt(a, b):
    return product(a, b, NT)


def tn(a, b):
    return product(a, b, TN)


def mean_lanes(x):
    weight = jnp.full((2 * LANES, LANES), 1.0 / LANES, BF16)
    return dot(cat(split(x), 1), weight, NN)


def norm(x):
    cent = x - mean_lanes(x)
    inv = lax.rsqrt(mean_lanes(cent * cent) + 1e-05)
    return cent * inv, inv


def norm_back(d, xhat, inv):
    return (d - mean_lanes(d) - xhat * mean_lanes(d * xhat)) * inv


def sigmoid(x):
    return 1.0 / (1.0 + jnp.exp(-x))


def column_sum(x):
    return jnp.sum(x, axis=0, keepdims=True)


def block_kernel(sizes, *refs):
    samples, rows, dpn, seqn, early, late = sizes
    nwin = rows // WQ
    windows = samples * nwin
    flat = samples * rows
    nz = 4
    nx = seqn // (2 * nz)
    nxy = dpn * nx
    n_in = 6 + len(PARAMS)
    given, refs = refs[:n_in], refs[n_in:]
    held, refs = refs[-n_in - 1 : -1], refs[:-n_in - 1] + refs[-1:]
    n_e, n_l = 1 + 2 * len(early.parts), 1 + 2 * len(late.parts)
    landing_e, landing_l, refs = refs[-n_e - n_l - 1 : -n_l - 1], refs[-n_l - 1 : -1], refs[: -n_e - n_l - 1] + refs[-1:]
    (
        count,
        gain_s,
        wpair_s,
        atoms,
        single,
        cot,
        p_s_gain1,
        p_w_scale1,
        p_b_scale1,
        p_w_shift1,
        p_w_query,
        p_b_query,
        p_w_key,
        p_w_value,
        p_w_gate,
        p_pair_gain,
        p_w_pair,
        p_w_out,
        p_w_zero1,
        p_b_zero1,
        p_s_gain2,
        p_w_scale2,
        p_b_scale2,
        p_w_shift2,
        p_w_hidden_gate,
        p_w_hidden_up,
        p_w_down,
        p_w_zero2,
        p_b_zero2,
    ) = held
    (
        pair_hbm,
        out,
        g_atoms,
        g_single,
        g_pair,
        res_e,
        res_l,
        res_s,
        pair,
        bias,
        pmean,
        prs,
        prob,
        ds,
        kv,
        dkv,
        dhalo,
        kvh,
        kvl,
        w1h,
        w1l,
        wqh,
        wql,
        wzh,
        wzl,
        w2h,
        w2l,
        whh,
        whl,
        wdh,
        wdl,
        woh,
        wol,
        qh_s,
        ql_s,
        mh_s,
        ml_s,
        th_s,
        tl_s,
        mixed_s,
        ns_s,
        na_s,
        n1_s,
        sc1_s,
        sc2_s,
        sh2_s,
        gate_s,
        z1_s,
        z2_s,
        rs_s,
        ra_s,
        dq_s,
        dfirst_s,
        dz1_s,
        dz2_s,
        dn2_s,
        dsc2_s,
        gpre_s,
        gacc,
        acc_e,
        acc_l,
        acc_s,
        recv_sc,
        recv_sxy,
        recv_sz,
        pair_sem,
        h_send,
        h_recv,
        e_send,
        e_recv,
        l_send,
        l_recv,
        s_send,
        s_recv,
        in_sem,
    ) = refs
    dp = lax.axis_index("dp")
    me = lax.axis_index("seq")
    core = lax.rem(me, 2)
    x = lax.rem(me // 2, nx)
    z = me // (2 * nx)
    k = dp * nx + x
    left = (dp, lax.rem(me + seqn - 1, seqn))
    right = (dp, lax.rem(me + 1, seqn))
    other = (dp, me + 1 - 2 * core)

    def xy_peer(o):
        kk = lax.rem(k + o, nxy)
        return kk, (kk // nx, (z * nx + lax.rem(kk, nx)) * 2 + core)

    def z_peer(o):
        zz = lax.rem(z + o, nz)
        return zz, (dp, (zz * nx + x) * 2 + core)

    def load(ref):
        i = [ref is h for h in held].index(True)
        return pltpu.make_async_copy(given[i], ref, in_sem.at[i])

    def bring(*which):
        for ref in which:
            load(ref).start()

    def ready(*which):
        for ref in which:
            load(ref).wait()

    norms = (single, atoms, p_s_gain1, p_w_scale1, p_w_shift1, p_b_scale1)
    projections = (p_w_query, p_w_key, p_w_value, p_w_gate, p_b_query)
    scalars = (count, gain_s, wpair_s)
    conditions = (p_w_zero1, p_w_zero2, p_w_scale2, p_w_shift2, p_s_gain2, p_b_scale2, p_b_zero1, p_b_zero2)
    transition = (p_w_hidden_gate, p_w_hidden_up, p_w_down, p_w_out, cot, p_pair_gain, p_w_pair)
    bring(*norms, *projections, *scalars)
    for s in range(samples):
        pltpu.make_async_copy(pair_hbm.at[s], pair.at[s], pair_sem.at[s]).start()
    bring(*conditions, *transition)

    barrier = pltpu.get_barrier_semaphore()
    greeted = [left, right, other]
    greeted += [xy_peer(o)[1] for o in range(1, nxy)]
    greeted += [z_peer(o)[1] for o in range(1, nz)]
    for device in greeted:
        pl.semaphore_signal(barrier, inc=1, device_id=device, device_id_type=MESH)

    def remote(src, dst, send, recv, device):
        return pltpu.make_async_remote_copy(
            src_ref=src, dst_ref=dst, send_sem=send, recv_sem=recv, device_id=device, device_id_type=MESH
        )

    def start(copies):
        for copy in copies:
            copy.start()
        return copies

    def wait(copies):
        for copy in copies:
            copy.wait()

    def span(first, size):
        return pl.ds(pl.multiple_of(first, 8), size)

    def hold(high, low, *weights):
        for c, w in enumerate(weights):
            width = w.shape[1]
            high[:, c * width : (c + 1) * width], low[:, c * width : (c + 1) * width] = split(w[...])

    ready(*norms)
    hold(w1h, w1l, p_w_scale1, p_w_shift1)
    ns, rs = norm(single[...])
    na, ra = norm(atoms[...])
    ns_s[...] = ns
    na_s[...] = na
    rs_s[...] = rs
    ra_s[...] = ra
    first1 = nn(split(ns * p_s_gain1[...]), (w1h[...], w1l[...]))
    sc1 = sigmoid(first1[:, :LANES] + p_b_scale1[...])
    sc1_s[...] = sc1
    n1 = sc1 * na + first1[:, LANES:]
    n1_s[...] = n1
    n1_split = split(n1)
    ready(*projections)
    hold(wqh, wql, p_w_query, p_w_key, p_w_value, p_w_gate)
    keys_values = nn(n1_split, (wqh[:, LANES : 3 * LANES], wql[:, LANES : 3 * LANES]))
    for s in range(samples):
        block = keys_values[s * rows : (s + 1) * rows]
        kv[s, HALO : HALO + rows] = block
        kvh[s, HALO : HALO + rows], kvl[s, HALO : HALO + rows] = split(block)

    def swap(leftward, rightward):
        def begin():
            @pl.when(me > 0)
            def _():
                leftward.start()

            @pl.when(me < seqn - 1)
            def _():
                rightward.start()

        def end():
            @pl.when(me > 0)
            def _():
                leftward.wait_send()
                rightward.wait_recv()

            @pl.when(me < seqn - 1)
            def _():
                rightward.wait_send()
                leftward.wait_recv()

        begin()
        return end

    pl.semaphore_wait(barrier, len(greeted))
    halos_here = swap(
        remote(kv.at[:, HALO : 2 * HALO], kv.at[:, HALO + rows : 2 * HALO + rows], h_send.at[1], h_recv.at[1], left),
        remote(kv.at[:, rows : rows + HALO], kv.at[:, 0:HALO], h_send.at[0], h_recv.at[0], right),
    )

    ready(*conditions, *transition)
    hold(wzh, wzl, p_w_zero1, p_w_zero2)
    hold(w2h, w2l, p_w_scale2, p_w_shift2)
    hold(whh, whl, p_w_hidden_gate, p_w_hidden_up)
    hold(wdh, wdl, p_w_down)
    hold(woh, wol, p_w_out)
    scale = 1.0 / math.sqrt(32)
    query = (nn(n1_split, (wqh[:, :LANES], wql[:, :LANES])) + p_b_query[...]) * scale
    qh_s[...], ql_s[...] = split(query)
    gate_s[...] = sigmoid(nn(n1_split, (wqh[:, 3 * LANES :], wql[:, 3 * LANES :])))
    first2 = nn(split(ns * p_s_gain2[...]), (w2h[...], w2l[...]))
    sc2_s[...] = sigmoid(first2[:, :LANES] + p_b_scale2[...])
    sh2_s[...] = first2[:, LANES:]
    zeros = nn(split(single[...]), (wzh[...], wzl[...]))
    z1_s[...] = sigmoid(zeros[:, :LANES] + p_b_zero1[...])
    z2_s[...] = sigmoid(zeros[:, LANES:] + p_b_zero2[...])

    ready(*scalars)
    channels = gain_s.shape[0]
    heads = wpair_s.shape[0]
    wg = [[gain_s[p] * wpair_s[h, p] for h in range(heads)] for p in range(channels)]
    wsum = [functools.reduce(lambda a, b: a + b, [wg[p][h] for p in range(channels)]) for h in range(heads)]

    for s in range(samples):
        pltpu.make_async_copy(pair_hbm.at[s], pair.at[s], pair_sem.at[s]).wait()

    key_lane = lax.broadcasted_iota(jnp.int32, (WQ, KW), 1)
    same = key_lane == lax.broadcasted_iota(jnp.int32, (WQ, KW), 0) + HALO

    def pair_bias(t, carry):
        s, w = t // nwin, lax.rem(t, nwin)
        first = pair[s, w, 0]
        total, square = first, first * first
        b = [first * wg[0][h] for h in range(heads)]
        for p in range(1, channels):
            v = pair[s, w, p]
            total = total + v
            square = square + v * v
            b = [b[h] + v * wg[p][h] for h in range(heads)]
        mean = total * (1.0 / channels)
        var = square * (1.0 / channels) - mean * mean
        inv = lax.rsqrt(jnp.maximum(var, 0.25))
        pmean[t] = mean
        live = jnp.where(var > 0.25, 1.0, jnp.where(var == 0.25, 0.5, 0.0))
        prs[t, 0] = inv
        prs[t, 1] = inv * inv * live * (1.0 / channels)
        begin = me * rows + w * WQ - HALO
        valid = ((key_lane >= -begin) & (key_lane < count[s] - begin)) | same
        for h in range(heads):
            bias[t, h * WQ : (h + 1) * WQ] = jnp.where(valid, inv * (b[h] - mean * wsum[h]), -1e9)
        return carry

    lax.fori_loop(0, samples * nwin, pair_bias, 0)

    lane = lax.broadcasted_iota(jnp.int32, (heads * WQ, LANES), 1)
    row = lax.broadcasted_iota(jnp.int32, (heads * WQ, LANES), 0)
    own = (lane // 32 == row // WQ).astype(F32)
    own_low = own.astype(BF16)
    ones = jnp.ones((KW, LANES), BF16)
    nothing = jnp.zeros((KW, LANES), BF16)

    def heads_in(ref, at):
        return cat([ref[at, :]] * heads, 0) * own_low

    def heads_out(v):
        v = v * own
        return (v[0:WQ] + v[WQ : 2 * WQ]) + (v[2 * WQ : 3 * WQ] + v[3 * WQ : 4 * WQ])

    def window(t):
        s, w = divmod(t, nwin)
        return s, slice(s * rows + w * WQ, s * rows + (w + 1) * WQ), slice(w * WQ, w * WQ + KW)

    def inner(t):
        w = t % nwin
        return w * WQ >= HALO and w * WQ + KW <= HALO + rows

    middle = [t for t in range(windows) if inner(t)]
    border = [t for t in range(windows) if not inner(t)]

    def attend(ts):
        for t in ts:
            s, at, keys = window(t)
            queries = heads_in(qh_s, at), heads_in(ql_s, at)
            prob[t] = nt(queries, (kvh[s, keys, :LANES], kvl[s, keys, :LANES])) + bias[t]
        for t in ts:
            s, at, keys = window(t)
            scores = prob[t]
            expo = jnp.exp(scores - jnp.max(scores, axis=-1, keepdims=True))
            eh, el = split(expo)
            vh, vl = kvh[s, keys, LANES:], kvl[s, keys, LANES:]
            high = cat([vh, ones], 1)
            both = dot(cat([eh, el, eh], 1), cat([high, high, cat([vl, nothing], 1)], 0), NN)
            inv = 1.0 / both[:, LANES:]
            prob[t] = expo * inv
            mixed_s[at, :] = heads_out(both[:, :LANES] * inv)

    attend(middle)
    halos_here()
    for s in range(samples):
        for absent, at in ((me == 0, slice(0, HALO)), (me == seqn - 1, slice(HALO + rows, 2 * HALO + rows))):
            kvh[s, at], kvl[s, at] = split(jnp.where(absent, 0.0, kv[s, at]))
    attend(border)

    gated = gate_s[...] * mixed_s[...]
    gated_split = split(gated)
    projected = nn(gated_split, (woh[...], wol[...]))
    first = atoms[...] + z1_s[...] * projected
    nf, rf = norm(first)
    n2 = sc2_s[...] * nf + sh2_s[...]
    n2_split = split(n2)
    up = nn(n2_split, (whh[...], whl[...]))
    hidden_width = up.shape[1] // 2
    hg, hu = up[:, :hidden_width], up[:, hidden_width:]
    sg = sigmoid(hg)
    silu = hg * sg
    hidden = silu * hu
    hidden_split = split(hidden)
    down = nn(hidden_split, (wdh[...], wdl[...]))
    z2 = z2_s[...]
    g = cot[...]
    out[...] = first + z2 * down

    def put(acc, names, value):
        at = 0
        for name in names:
            base = PLACE[name]
            for b in range(dict((n, c) for n, _, c in EARLY + LATE)[name]):
                acc[base + b * value.shape[0] : base + (b + 1) * value.shape[0]] = value[:, at : at + LANES]
                at += LANES

    d_down = g * z2
    dz2 = g * down * z2 * (1.0 - z2)
    dz2_s[...] = dz2
    d_down_split = split(d_down)
    put(acc_e, ["w_down"], tn(hidden_split, d_down_split))
    d_hidden = nt(d_down_split, (wdh[...], wdl[...]))
    d_up = cat([d_hidden * hu * (sg * (1.0 + hg * (1.0 - sg))), d_hidden * silu], 1)
    d_up_split = split(d_up)
    put(acc_e, ["w_hidden_gate", "w_hidden_up"], tn(n2_split, d_up_split))
    d_n2 = nt(d_up_split, (whh[...], whl[...]))
    dn2_s[...] = d_n2
    sc2 = sc2_s[...]
    dsc2 = d_n2 * nf * sc2 * (1.0 - sc2)
    dsc2_s[...] = dsc2
    cond2_split = split(ns_s[...] * p_s_gain2[...])
    put(acc_e, ["w_scale2", "w_shift2"], tn(cond2_split, split(cat([dsc2, d_n2], 1))))
    d_first = g + norm_back(d_n2 * sc2, nf, rf)
    dfirst_s[...] = d_first
    z1 = z1_s[...]
    d_proj = d_first * z1
    d_proj_split = split(d_proj)
    dz1 = d_first * projected * z1 * (1.0 - z1)
    dz1_s[...] = dz1
    put(acc_e, ["w_out"], tn(gated_split, d_proj_split))
    put(acc_e, ["w_zero1", "w_zero2"], tn(split(single[...]), split(cat([dz1, dz2], 1))))
    d_gated = nt(d_proj_split, (woh[...], wol[...]))
    gate = gate_s[...]
    mixed = mixed_s[...]
    d_gate = d_gated * mixed * gate * (1.0 - gate)
    gpre_s[...] = d_gate
    put(acc_e, ["w_gate"], tn(split(n1_s[...]), split(d_gate)))
    d_mixed = d_gated * gate
    mh_s[...], ml_s[...] = split(d_mixed)
    th_s[...], tl_s[...] = split(d_mixed * mixed)
    if early.size > EARLY_ROWS:
        acc_e[EARLY_ROWS:] = jnp.zeros((early.size - EARLY_ROWS, LANES), F32)

    groups = {"plane": (nxy, k, xy_peer), "line": (nz, z, z_peer)}

    def travelling(plan, acc, res, landing, sems):
        half = plan.size // 2
        base = core * half
        used = [0]

        def send(src, dst, device):
            i = used[0]
            used[0] += 1
            return remote(src, dst, sems[0].at[i], sems[1].at[i], device)

        def gathers(name, where):
            n, _, peer = groups[name]
            return [send(res.at[where], res.at[where], peer(o)[1]) for o in range(1, n)]

        places = []
        for i, (first, rows_at, rows_in) in enumerate(plan.parts):
            second = "line" if first == "plane" else "plane"
            here = base + rows_at
            one = rows_in // groups[first][0]
            two = one // groups[second][0]
            mine = here + groups[first][1] * one
            places.append((first, second, here, one, two, mine, landing[1 + 2 * i], landing[2 + 2 * i]))

        def run():
            copies = start([send(acc.at[span((1 - core) * half, half)], landing[0], other)])
            yield
            wait(copies)
            acc[span(base, half), :] += landing[0][...]
            copies = []
            for first, _, here, one, _, _, land, _ in places:
                n, _, peer = groups[first]
                for o in range(1, n):
                    index, device = peer(o)
                    copies.append(send(acc.at[span(here + index * one, one)], land.at[o - 1], device))
            start(copies)
            yield
            wait(copies)
            copies = []
            for first, second, _, one, two, mine, land, land2 in places:
                value = acc[span(mine, one), :]
                for o in range(1, groups[first][0]):
                    value = value + land[o - 1]
                acc[span(mine, one), :] = value
                n, own_index, peer = groups[second]
                for o in range(1, n):
                    index, device = peer(o)
                    if plan.whole:
                        copies.append(send(acc.at[span(mine, one)], land2.at[own_index], device))
                    else:
                        copies.append(send(acc.at[span(mine + index * two, two)], land2.at[o - 1], device))
            start(copies)
            if plan.whole:
                for _, second, _, one, _, mine, _, land2 in places:
                    land2[groups[second][1]] = acc[span(mine, one), :]
            yield
            wait(copies)
            copies = []
            for first, second, _, one, two, mine, _, land2 in places:
                n, own_index, _ = groups[second]
                if plan.whole:
                    res[span(mine, one), :] = add_up(land2, n)
                    copies += gathers(first, span(mine, one))
                else:
                    at = mine + own_index * two
                    value = acc[span(at, two), :]
                    for o in range(1, n):
                        value = value + land2[o - 1]
                    res[span(at, two), :] = value
                    copies += gathers(second, span(at, two))
            start(copies)
            yield
            if not plan.whole:
                wait(copies)
                copies = []
                for first, _, _, one, _, mine, _, _ in places:
                    copies += gathers(first, span(mine, one))
                start(copies)
                yield
            wait(copies)
            copies = start([send(res.at[span(base, half)], res.at[span(base, half)], other)])
            yield
            wait(copies)
            yield

        steps = run()
        return lambda: next(steps)

    def add_up(slots, count):
        value = slots[0]
        for i in range(1, count):
            value = value + slots[i]
        return value

    go_early = travelling(early, acc_e, res_e, landing_e, (e_send, e_recv))
    go_late = travelling(late, acc_l, res_l, landing_l, (l_send, l_recv))
    go_early()

    dkv[...] = jnp.zeros_like(dkv)
    less = -jnp.ones((KW, LANES), BF16)

    def back_values(ts):
        for t in ts:
            s, at, keys = window(t)
            dkv[s, keys, LANES:] += tn(split(prob[t]), (heads_in(mh_s, at), heads_in(ml_s, at)))

    def back_keys(ts):
        for t in ts:
            s, at, keys = window(t)
            dkv[s, keys, :LANES] += tn(split(ds[t]), (heads_in(qh_s, at), heads_in(ql_s, at)))

    def swap_back(lanes, i):
        ends = slice(0, HALO), slice(HALO + rows, 2 * HALO + rows)
        return swap(
            remote(dkv.at[:, ends[0], lanes], dhalo.at[1, :, :, lanes], h_send.at[i], h_recv.at[i], left),
            remote(dkv.at[:, ends[1], lanes], dhalo.at[0, :, :, lanes], h_send.at[i + 1], h_recv.at[i + 1], right),
        )

    back_values(border)
    values_here = swap_back(slice(LANES, 2 * LANES), 2)
    for t in border + middle:
        s, at, keys = window(t)
        mh, ml = heads_in(mh_s, at), heads_in(ml_s, at)
        th, tl = heads_in(th_s, at), heads_in(tl_s, at)
        vh, vl = kvh[s, keys, LANES:], kvl[s, keys, LANES:]
        ds[t] = prob[t] * dot(cat([mh, ml, mh, th, tl], 1), cat([vh, vh, vl, less, less], 1), NT)
    back_keys(border)
    keys_here = swap_back(slice(0, LANES), 4)

    go_early()

    back_keys(middle)
    back_values(middle)
    for t in range(windows):
        s, at, keys = window(t)
        dq_s[at, :] = heads_out(nn(split(ds[t]), (kvh[s, keys, :LANES], kvl[s, keys, :LANES]))) * scale

    gacc[...] = jnp.zeros_like(gacc)

    def pair_back(t, carry):
        s, w = t // nwin, lax.rem(t, nwin)
        inv, live = prs[t, 0], prs[t, 1]
        mean = pmean[t]
        u, along, level = [], None, None
        for h in range(heads):
            d = ds[t, h * WQ : (h + 1) * WQ]
            u.append(d * inv)
            a = d * bias[t, h * WQ : (h + 1) * WQ]
            b = u[h] * (wsum[h] * (1.0 / channels))
            along = a if along is None else along + a
            level = b if level is None else level + b
        c1 = along * live
        c0 = mean * c1 - level
        mu = [mean * u[h] for h in range(heads)]
        for p in range(channels):
            v = pair[s, w, p]
            d = c0 - v * c1
            for h in range(heads):
                d = d + u[h] * wg[p][h]
                term = v * u[h] - mu[h]
                gacc[h * channels + p] += (term[0:8] + term[8:16]) + (term[16:24] + term[24:32])
            g_pair[s, w, p] = d
        return carry

    ahead = windows // 2
    lax.fori_loop(0, ahead, pair_back, 0)

    values_here()
    keys_here()
    for s in range(samples):
        dkv[s, HALO : 2 * HALO] += jnp.where(me == 0, 0.0, dhalo[0, s])
        dkv[s, rows : rows + HALO] += jnp.where(me == seqn - 1, 0.0, dhalo[1, s])

    dq = dq_s[...]
    d_keys_values = cat([dkv[s, HALO : HALO + rows] for s in range(samples)], 0)
    d_all = split(cat([dq, d_keys_values, gpre_s[...]], 1))
    d_n1 = nt(d_all, (wqh[...], wql[...]))
    na = na_s[...]
    sc1 = sc1_s[...]
    dsc1 = d_n1 * na * sc1 * (1.0 - sc1)
    d_first1 = split(cat([dsc1, d_n1], 1))
    ns = ns_s[...]
    put(
        acc_l,
        ["w_query", "w_key", "w_value"],
        tn(split(n1_s[...]), (d_all[0][:, : 3 * LANES], d_all[1][:, : 3 * LANES])),
    )
    put(acc_l, ["w_scale1", "w_shift1"], tn(split(ns * p_s_gain1[...]), d_first1))
    if late.size > LATE_ROWS:
        acc_l[LATE_ROWS:] = jnp.zeros((late.size - LATE_ROWS, LANES), F32)
    go_late()

    g_atoms[...] = dfirst_s[...] + norm_back(d_n1 * sc1, na, ra_s[...])
    go_late()
    go_early()
    lax.fori_loop(ahead, windows, pair_back, 0)

    d_cond1 = nt(d_first1, (w1h[...], w1l[...]))
    d_cond2 = nt(split(cat([dsc2_s[...], dn2_s[...]], 1)), (w2h[...], w2l[...]))

    eye = (
        lax.broadcasted_iota(jnp.int32, (channels, LANES), 0) == lax.broadcasted_iota(jnp.int32, (channels, LANES), 1)
    ).astype(F32)
    gsum = jnp.sum(jnp.sum(gacc[...], axis=1), axis=-1, keepdims=True)
    rows_g = [column_sum(gsum[h * channels : (h + 1) * channels] * eye) for h in range(heads)]
    blank = jnp.zeros((1, LANES - channels), F32)
    gain_row = cat([p_pair_gain[...], blank], 1)
    pair_row = jnp.zeros((1, LANES), F32)
    for h in range(heads):
        pair_row = pair_row + rows_g[h] * cat([p_w_pair[h : h + 1, :], blank], 1)
    pair_grad = cat([v * gain_row for v in rows_g] + [jnp.zeros((8 - heads, LANES), F32)], 0)
    small = {
        "b_scale1": column_sum(dsc1),
        "b_query": column_sum(dq),
        "b_scale2": column_sum(dsc2_s[...]),
        "b_zero1": column_sum(dz1_s[...]),
        "b_zero2": column_sum(dz2_s[...]),
        "s_gain1": column_sum(d_cond1 * ns),
        "s_gain2": column_sum(d_cond2 * ns),
        "pair_gain": pair_row,
    }
    acc_s[...] = cat([small[name] for name in VECTORS] + [pair_grad], 0)
    s1 = start([remote(acc_s, recv_sc, s_send.at[0], s_recv.at[0], other)])
    d_ns = d_cond1 * p_s_gain1[...] + d_cond2 * p_s_gain2[...]
    g_single[...] = norm_back(d_ns, ns, rs_s[...]) + nt(
        split(cat([dz1_s[...], dz2_s[...]], 1)), (wzh[...], wzl[...])
    )

    def spread(slots, mine, peers, first):
        slots[mine] = acc_s[...]
        return start(
            [
                remote(acc_s, slots.at[mine], s_send.at[first + i], s_recv.at[first + i], device)
                for i, device in enumerate(peers)
            ]
        )

    go_late()
    go_early()
    wait(s1)
    acc_s[...] = acc_s[...] + recv_sc[...]
    s2 = spread(recv_sxy, k, [xy_peer(o)[1] for o in range(1, nxy)], 1)
    wait(s2)
    acc_s[...] = add_up(recv_sxy, nxy)
    s3 = spread(recv_sz, z, [z_peer(o)[1] for o in range(1, nz)], nxy)
    go_late()
    go_early()
    wait(s3)
    res_s[...] = add_up(recv_sz, nz)
    go_late()
    go_early()
    go_late()
    go_early()


class Plan:
    def __init__(self, needed, nxy, nz, whole):
        half = -(-needed // 2)
        grains = (8 * nxy, 8 * nz) if whole else (8 * nxy * nz,) * 2
        line = int(half * (0.4 if whole else 0.34)) // grains[1] * grains[1]
        plane = -(-(half - line) // grains[0]) * grains[0]
        self.whole, self.size = whole, 2 * (plane + line)
        self.parts = [("plane", 0, plane)] + ([("line", plane, line)] if line else [])

    def landing(self, nxy, nz):
        count = {"plane": (nxy, nz), "line": (nz, nxy)}
        shapes = [(self.size // 2, LANES)]
        for first, _, rows in self.parts:
            n, m = count[first]
            shapes.append((n - 1, rows // n, LANES))
            shapes.append((m, rows // n, LANES) if self.whole else (m - 1, rows // n // m, LANES))
        return shapes

    def copies(self, nxy, nz):
        return 2 + 2 * len(self.parts) * (nxy + nz - 2)


def unpack_kernel(*refs):
    n, v = len(EARLY) + len(LATE), len(VECTORS)
    ins, refs = refs[:7], refs[7:]
    outs, mats, rows, wp, sems = refs[:4], refs[4 : 4 + n], refs[4 + n : 4 + n + v], refs[4 + n + v], refs[5 + n + v]
    copies = []

    def move(a, b):
        copies.append(pltpu.make_async_copy(a, b, sems.at[len(copies)]))
        copies[-1].start()

    for a, b in zip(ins[3::-1], outs[::-1]):
        for c in range(a.shape[0]):
            move(a.at[c], b.at[c])
    at = 0
    for group, packed in ((EARLY, ins[4]), (LATE, ins[5])):
        for name, _, columns in group:
            base, height = PLACE[name], mats[at].shape[0]
            for b in range(columns):
                move(packed.at[pl.ds(base + b * height, height)], mats[at].at[:, pl.ds(b * LANES, LANES)])
            at += 1
    for i, ref in enumerate(rows):
        ref[...] = ins[6][i : i + 1, 0 : ref.shape[1]]
    wp[...] = ins[6][v : v + wp.shape[0], 0 : wp.shape[1]]
    for copy in copies:
        copy.wait()


def shards(dpn, seqn, atoms, single_cond, pair_block, atom_count, *rest):
    params, cotangent = dict(zip(PARAMS, rest[:-1])), rest[-1]
    params["w_pair"] = params["w_pair"].T
    samples, rows, width = atoms.shape
    nwin, channels = pair_block.shape[1:3]
    heads = params["w_pair"].shape[0]
    flat = samples * rows
    nz, nx = 4, seqn // 8
    nxy = dpn * nx
    early = Plan(EARLY_ROWS, nxy, nz, False)
    late = Plan(LATE_ROWS, nxy, nz, True)
    windows = samples * nwin
    hidden = params["w_down"].shape[0]

    def row(v):
        return v.reshape(1, -1) if v.ndim == 1 else v

    vmem = pl.BlockSpec(memory_space=pltpu.VMEM)
    anyw = pl.BlockSpec(memory_space=pl.ANY)

    def buf(*shape):
        return pltpu.VMEM(shape, F32)

    def low(*shape):
        return [pltpu.VMEM(shape, BF16), pltpu.VMEM(shape, BF16)]

    def sems(n):
        return [pltpu.SemaphoreType.DMA((n,)), pltpu.SemaphoreType.DMA((n,))]

    tall = (flat, width)
    extended = (samples, rows + 2 * HALO, 2 * width)
    scratch = [
        buf(*pair_block.shape),
        buf(windows, heads * WQ, KW),
        buf(windows, WQ, KW),
        buf(windows, 2, WQ, KW),
        buf(windows, heads * WQ, KW),
        buf(windows, heads * WQ, KW),
        buf(*extended),
        buf(*extended),
        buf(2, samples, HALO, 2 * width),
    ]
    scratch += low(*extended)
    scratch += low(width, 2 * width)
    scratch += low(width, 4 * width)
    scratch += low(width, 2 * width)
    scratch += low(width, 2 * width)
    scratch += low(width, 2 * hidden)
    scratch += low(hidden, width)
    scratch += low(width, width)
    scratch += low(*tall) + low(*tall) + low(*tall)
    scratch += [buf(*tall) for _ in range(19)]
    scratch += [
        buf(heads * channels, 8, KW),
        buf(early.size, LANES),
        buf(late.size, LANES),
        buf(16, LANES),
        buf(16, LANES),
        buf(nxy, 16, LANES),
        buf(nz, 16, LANES),
        pltpu.SemaphoreType.DMA((samples,)),
    ]
    scratch += sems(6) + sems(early.copies(nxy, nz)) + sems(late.copies(nxy, nz)) + sems(nxy + nz - 1)
    scratch += [buf(*shape) for plan in (early, late) for shape in plan.landing(nxy, nz)]
    arrays = [
        atom_count,
        params["pair_gain"],
        params["w_pair"],
        atoms.reshape(tall),
        single_cond.reshape(tall),
        cotangent.reshape(tall),
        *[row(params[name]) for name in PARAMS],
        pair_block,
    ]
    scratch += [pltpu.SMEM(v.shape, v.dtype) for v in arrays[:3]]
    scratch += [buf(*v.shape) for v in arrays[3:-1]]
    scratch += [pltpu.SemaphoreType.DMA((len(arrays) - 1,))]
    sizes = (samples, rows, dpn, seqn, early, late)
    big = pl.pallas_call(
        functools.partial(block_kernel, sizes),
        out_shape=[buf(*shape) for shape in (tall, tall, tall, pair_block.shape, (early.size, LANES), (late.size, LANES), (16, LANES))],
        in_specs=[anyw] * (7 + len(PARAMS)),
        out_specs=[vmem] * 7,
        scratch_shapes=scratch,
        compiler_params=pltpu.CompilerParams(
            collective_id=0, has_side_effects=True, vmem_limit_bytes=40 * 2**20
        ),
        name="block",
    )(*[pltpu.with_memory_space_constraint(v, pltpu.HBM) for v in arrays])

    names = [name for name, _, _ in EARLY + LATE]
    mats = [jax.ShapeDtypeStruct(params[name].shape, F32) for name in names]
    vecs = [jax.ShapeDtypeStruct((1, params[name].shape[0]), F32) for name in VECTORS]
    big = list(big)
    for i in range(3):
        big[i] = big[i].reshape(1, *tall)
    results = pl.pallas_call(
        unpack_kernel,
        out_shape=[jax.ShapeDtypeStruct(v.shape, F32) for v in big[:4]]
        + mats
        + vecs
        + [jax.ShapeDtypeStruct((heads, channels), F32)],
        in_specs=[vmem] * 7,
        out_specs=[anyw] * (4 + len(mats)) + [vmem] * (len(vecs) + 1),
        scratch_shapes=[
            pltpu.SemaphoreType.DMA((sum(c for _, _, c in EARLY + LATE) + sum(v.shape[0] for v in big[:4]),)),
        ],
        compiler_params=pltpu.CompilerParams(vmem_limit_bytes=16 * 2**20),
        name="unpack",
    )(*[pltpu.with_memory_space_constraint(v, pltpu.VMEM) for v in big])
    grads = dict(zip(names, results[4:]))
    for name, value in zip(VECTORS, results[4 + len(mats) :]):
        grads[name] = value.reshape(-1)
    grads["w_pair"] = results[-1].T
    out, g_atoms, g_single, g_pair = results[:4]
    return (
        out.reshape(atoms.shape),
        g_atoms.reshape(atoms.shape),
        g_single.reshape(atoms.shape),
        g_pair.reshape(pair_block.shape),
    ) + tuple(grads[name] for name in PARAMS)


def solution(mesh):
    data = P("dp", "seq", None)
    pairs = P("dp", "seq", None, None, None)
    return jax.shard_map(
        functools.partial(shards, mesh.shape["dp"], mesh.shape["seq"]),
        mesh=mesh,
        in_specs=(data, data, pairs, P("dp")) + (P(),) * len(PARAMS) + (data,),
        out_specs=(data, data, data, pairs) + (P(),) * len(PARAMS),
        check_vma=False,
    )
```

```python
import functools
import math

import jax
import jax.numpy as jnp
from jax import lax
from jax.experimental import pallas as pl
from jax.experimental.pallas import tpu as pltpu
from jax.sharding import PartitionSpec as P

WQ = 32
KW = 128
HALO = 48
LANES = 128
MESH = pl.DeviceIdType.MESH
F32 = jnp.float32

EARLY = (
    ("w_down", 2, 1),
    ("w_hidden_gate", 1, 2),
    ("w_hidden_up", 1, 2),
    ("w_zero2", 1, 1),
    ("w_scale2", 1, 1),
    ("w_shift2", 1, 1),
    ("w_out", 1, 1),
    ("w_zero1", 1, 1),
    ("w_gate", 1, 1),
)
LATE = (
    ("w_query", 1, 1),
    ("w_key", 1, 1),
    ("w_value", 1, 1),
    ("w_scale1", 1, 1),
    ("w_shift1", 1, 1),
)
VECTORS = ("b_scale1", "b_query", "b_scale2", "b_zero1", "b_zero2", "s_gain1", "s_gain2", "pair_gain")
PARAMS = (
    "s_gain1",
    "w_scale1",
    "b_scale1",
    "w_shift1",
    "w_query",
    "b_query",
    "w_key",
    "w_value",
    "w_gate",
    "pair_gain",
    "w_pair",
    "w_out",
    "w_zero1",
    "b_zero1",
    "s_gain2",
    "w_scale2",
    "b_scale2",
    "w_shift2",
    "w_hidden_gate",
    "w_hidden_up",
    "w_down",
    "w_zero2",
    "b_zero2",
)


def offsets():
    place, used = {}, []
    for group in (EARLY, LATE):
        row = 0
        for name, rows, columns in group:
            place[name] = row
            row += rows * columns * LANES
        used.append(row)
    return place, used[0], used[1]


PLACE, EARLY_ROWS, LATE_ROWS = offsets()
BF16 = jnp.bfloat16
NN = (((1,), (0,)), ((), ()))
NT = (((1,), (1,)), ((), ()))
TN = (((0,), (0,)), ((), ()))


def dot(a, b, dims):
    return lax.dot_general(a, b, dims, preferred_element_type=F32)


def cat(parts, axis):
    return jnp.concatenate(parts, axis=axis)


def split(x):
    high = x.astype(BF16)
    return high, (x - high.astype(F32)).astype(BF16)


def product(a, b, dims):
    (ah, al), (bh, bl) = a, b
    (ka,), (kb,) = dims[0]
    return dot(cat([ah, al, ah], ka), cat([bh, bh, bl], kb), dims)


def beside(a, b, dims):
    (ah, al), (bh, bl) = a, b
    free = 1 - dims[0][1][0]
    width = bh.shape[free]
    both = dot(ah, cat([bh, bl], free), dims)
    return both[:, :width] + (both[:, width:] + dot(al, bh, dims))


def nn(a, b):
    return product(a, b, NN)


def nt(a, b):
    return product(a, b, NT)


def tn(a, b):
    return product(a, b, TN)


def mean_lanes(x):
    weight = jnp.full((2 * LANES, LANES), 1.0 / LANES, BF16)
    return dot(cat(split(x), 1), weight, NN)


def norm(x):
    cent = x - mean_lanes(x)
    inv = lax.rsqrt(mean_lanes(cent * cent) + 1e-05)
    return cent * inv, inv


def norm_back(d, xhat, inv):
    return (d - mean_lanes(d) - xhat * mean_lanes(d * xhat)) * inv


def sigmoid(x):
    return 1.0 / (1.0 + jnp.exp(-x))


def column_sum(x):
    return jnp.sum(x, axis=0, keepdims=True)


def block_kernel(sizes, *refs):
    samples, rows, dpn, seqn, early, late = sizes
    nwin = rows // WQ
    windows = samples * nwin
    flat = samples * rows
    nz = 4
    nx = seqn // (2 * nz)
    nxy = dpn * nx
    n_in = 6 + len(PARAMS)
    given, refs = refs[:n_in], refs[n_in:]
    held, refs = refs[-n_in - 1 : -1], refs[:-n_in - 1] + refs[-1:]
    n_e, n_l = 1 + 2 * len(early.parts), 1 + 2 * len(late.parts)
    landing_e, landing_l, refs = refs[-n_e - n_l - 1 : -n_l - 1], refs[-n_l - 1 : -1], refs[: -n_e - n_l - 1] + refs[-1:]
    (
        count,
        gain_s,
        wpair_s,
        atoms,
        single,
        cot,
        p_s_gain1,
        p_w_scale1,
        p_b_scale1,
        p_w_shift1,
        p_w_query,
        p_b_query,
        p_w_key,
        p_w_value,
        p_w_gate,
        p_pair_gain,
        p_w_pair,
        p_w_out,
        p_w_zero1,
        p_b_zero1,
        p_s_gain2,
        p_w_scale2,
        p_b_scale2,
        p_w_shift2,
        p_w_hidden_gate,
        p_w_hidden_up,
        p_w_down,
        p_w_zero2,
        p_b_zero2,
    ) = held
    (
        pair_hbm,
        out,
        g_atoms,
        g_single,
        g_pair,
        res_e,
        res_l,
        res_s,
        pair,
        bias,
        pmean,
        prs,
        prob,
        ds,
        kv,
        dkv,
        dhalo,
        kvh,
        kvl,
        w1h,
        w1l,
        wqh,
        wql,
        wzh,
        wzl,
        w2h,
        w2l,
        whh,
        whl,
        wdh,
        wdl,
        woh,
        wol,
        qh_s,
        ql_s,
        mh_s,
        ml_s,
        th_s,
        tl_s,
        mixed_s,
        ns_s,
        na_s,
        n1_s,
        sc1_s,
        sc2_s,
        sh2_s,
        gate_s,
        z1_s,
        z2_s,
        rs_s,
        ra_s,
        dq_s,
        dfirst_s,
        dz1_s,
        dz2_s,
        dn2_s,
        dsc2_s,
        gpre_s,
        gacc,
        gmid,
        acc_e,
        acc_l,
        acc_s,
        recv_sc,
        recv_sxy,
        recv_sz,
        pair_sem,
        h_send,
        h_recv,
        e_send,
        e_recv,
        l_send,
        l_recv,
        s_send,
        s_recv,
        in_sem,
    ) = refs
    dp = lax.axis_index("dp")
    me = lax.axis_index("seq")
    core = lax.rem(me, 2)
    x = lax.rem(me // 2, nx)
    z = me // (2 * nx)
    k = dp * nx + x
    left = (dp, lax.rem(me + seqn - 1, seqn))
    right = (dp, lax.rem(me + 1, seqn))
    other = (dp, me + 1 - 2 * core)

    def xy_peer(o):
        kk = lax.rem(k + o, nxy)
        return kk, (kk // nx, (z * nx + lax.rem(kk, nx)) * 2 + core)

    def z_peer(o):
        zz = lax.rem(z + o, nz)
        return zz, (dp, (zz * nx + x) * 2 + core)

    norm_weights = (p_w_scale1, p_w_shift1)
    projections = (p_w_key, p_w_value, p_w_query, p_w_gate)
    conditions = (p_w_zero1, p_w_zero2, p_w_scale2, p_w_shift2)
    transition = (p_w_hidden_gate, p_w_hidden_up, p_w_down, p_w_out)
    together = (norm_weights, projections, conditions, transition)
    sem_of = [[i for i, group in enumerate(together) if any(ref is r for r in group)] for ref in held]
    used = len(together)
    for found in sem_of:
        if not found:
            found.append(used)
            used += 1

    def where(ref):
        return [ref is h for h in held].index(True)

    def bring(*which):
        for ref in which:
            i = where(ref)
            pltpu.make_async_copy(given[i], ref, in_sem.at[sem_of[i][0]]).start()

    def ready(*which):
        for ref in which:
            if isinstance(ref, tuple):
                total = sum(r.shape[0] * r.shape[1] for r in ref) // LANES
                some = acc_e.at[0:total]
                pltpu.make_async_copy(some, some, in_sem.at[sem_of[where(ref[0])][0]]).wait()
            else:
                i = where(ref)
                pltpu.make_async_copy(given[i], ref, in_sem.at[sem_of[i][0]]).wait()

    scalars = (count, gain_s, wpair_s)
    bring(single, atoms, p_s_gain1, *norm_weights, p_b_scale1, *projections, p_b_query, *scalars)
    bring(*conditions, p_s_gain2, p_b_scale2, p_b_zero1, p_b_zero2)

    def pair_load(s, w):
        return pltpu.make_async_copy(pair_hbm.at[s, w], pair.at[s, w], pair_sem.at[s])

    for t in range(windows):
        pair_load(t // nwin, t % nwin).start()
    bring(*transition, cot, p_pair_gain, p_w_pair)

    barrier = pltpu.get_barrier_semaphore()
    greeted = [left, right, other]
    greeted += [xy_peer(o)[1] for o in range(1, nxy)]
    greeted += [z_peer(o)[1] for o in range(1, nz)]
    for device in greeted:
        pl.semaphore_signal(barrier, inc=1, device_id=device, device_id_type=MESH)

    def remote(src, dst, send, recv, device):
        return pltpu.make_async_remote_copy(
            src_ref=src, dst_ref=dst, send_sem=send, recv_sem=recv, device_id=device, device_id_type=MESH
        )

    def start(copies):
        for copy in copies:
            copy.start()
        return copies

    def wait(copies):
        for copy in copies:
            copy.wait()

    def span(first, size):
        return pl.ds(pl.multiple_of(first, 8), size)

    def hold(high, low, *weights):
        for c, w in enumerate(weights):
            width = w.shape[1]
            high[:, c * width : (c + 1) * width], low[:, c * width : (c + 1) * width] = split(w[...])

    ready(single, atoms, norm_weights, p_s_gain1, p_b_scale1)
    hold(w1h, w1l, p_w_scale1, p_w_shift1)
    xs, xa = single[...], atoms[...]
    cs, ca = xs - mean_lanes(xs), xa - mean_lanes(xa)
    rs, ra = lax.rsqrt(mean_lanes(cs * cs) + 1e-05), lax.rsqrt(mean_lanes(ca * ca) + 1e-05)
    ns, na = cs * rs, ca * ra
    ns_s[...] = ns
    na_s[...] = na
    rs_s[...] = rs
    ra_s[...] = ra
    first1 = nn(split(ns * p_s_gain1[...]), (w1h[...], w1l[...]))
    sc1 = sigmoid(first1[:, :LANES] + p_b_scale1[...])
    sc1_s[...] = sc1
    n1 = sc1 * na + first1[:, LANES:]
    n1_s[...] = n1
    n1_split = split(n1)
    ready(projections, p_b_query)
    hold(wqh, wql, p_w_key, p_w_value, p_w_query, p_w_gate)
    keys_values = nn(n1_split, (wqh[:, : 2 * LANES], wql[:, : 2 * LANES]))
    for s in range(samples):
        block = keys_values[s * rows : (s + 1) * rows]
        kv[s, HALO : HALO + rows] = block
        kvh[s, HALO : HALO + rows], kvl[s, HALO : HALO + rows] = split(block)

    def swap(leftward, rightward):
        def begin():
            @pl.when(me > 0)
            def _():
                leftward.start()

            @pl.when(me < seqn - 1)
            def _():
                rightward.start()

        def end():
            @pl.when(me > 0)
            def _():
                leftward.wait_send()
                rightward.wait_recv()

            @pl.when(me < seqn - 1)
            def _():
                rightward.wait_send()
                leftward.wait_recv()

        begin()
        return end

    pl.semaphore_wait(barrier, len(greeted))
    halos_here = swap(
        remote(kv.at[:, HALO : 2 * HALO], kv.at[:, HALO + rows : 2 * HALO + rows], h_send.at[1], h_recv.at[1], left),
        remote(kv.at[:, rows : rows + HALO], kv.at[:, 0:HALO], h_send.at[0], h_recv.at[0], right),
    )

    ready(conditions, p_s_gain2, p_b_scale2, p_b_zero1, p_b_zero2)
    hold(wzh, wzl, p_w_zero1, p_w_zero2)
    hold(w2h, w2l, p_w_scale2, p_w_shift2)
    scale = 1.0 / math.sqrt(32)
    query_gate = nn(n1_split, (wqh[:, 2 * LANES :], wql[:, 2 * LANES :]))
    qh_s[...], ql_s[...] = split((query_gate[:, :LANES] + p_b_query[...]) * scale)
    gate_s[...] = sigmoid(query_gate[:, LANES:])
    first2 = nn(split(ns * p_s_gain2[...]), (w2h[...], w2l[...]))
    sc2_s[...] = sigmoid(first2[:, :LANES] + p_b_scale2[...])
    sh2_s[...] = first2[:, LANES:]
    zeros = nn(split(single[...]), (wzh[...], wzl[...]))
    z1_s[...] = sigmoid(zeros[:, :LANES] + p_b_zero1[...])
    z2_s[...] = sigmoid(zeros[:, LANES:] + p_b_zero2[...])

    ready(*scalars)
    channels = gain_s.shape[0]
    heads = wpair_s.shape[0]
    wg = [[gain_s[p] * wpair_s[h, p] for h in range(heads)] for p in range(channels)]
    mid = [functools.reduce(lambda a, b: a + b, [wg[p][h] for p in range(channels)]) * (1.0 / channels) for h in range(heads)]
    centred = [[wg[p][h] - mid[h] for h in range(heads)] for p in range(channels)]

    key_lane = lax.broadcasted_iota(jnp.int32, (WQ, KW), 1)
    same = key_lane == lax.broadcasted_iota(jnp.int32, (WQ, KW), 0) + HALO

    def pair_bias(t, carry):
        s, w = t // nwin, lax.rem(t, nwin)
        first = pair[s, w, 0]
        total, square = first, first * first
        b = [first * centred[0][h] for h in range(heads)]
        for p in range(1, channels):
            v = pair[s, w, p]
            total = total + v
            square = square + v * v
            b = [b[h] + v * centred[p][h] for h in range(heads)]
        mean = total * (1.0 / channels)
        var = square * (1.0 / channels) - mean * mean
        inv = lax.rsqrt(jnp.maximum(var, 0.25))
        pmean[t] = mean
        live = jnp.where(var > 0.25, 1.0, jnp.where(var == 0.25, 0.5, 0.0))
        prs[t, 0] = inv
        prs[t, 1] = inv * inv * live * (1.0 / channels)
        begin = me * rows + w * WQ - HALO
        valid = ((key_lane >= -begin) & (key_lane < count[s] - begin)) | same
        for h in range(heads):
            bias[t, h * WQ : (h + 1) * WQ] = jnp.where(valid, inv * b[h], -1e9)
        return carry

    for s in range(samples):
        pltpu.make_async_copy(pair_hbm.at[s], pair.at[s], pair_sem.at[s]).wait()
        lax.fori_loop(s * nwin, (s + 1) * nwin, pair_bias, 0)
    ready(transition, cot, p_pair_gain, p_w_pair)
    hold(whh, whl, p_w_hidden_gate, p_w_hidden_up)
    hold(wdh, wdl, p_w_down)
    hold(woh, wol, p_w_out)

    lane = lax.broadcasted_iota(jnp.int32, (heads * WQ, LANES), 1)
    row = lax.broadcasted_iota(jnp.int32, (heads * WQ, LANES), 0)
    own = (lane // 32 == row // WQ).astype(F32)
    own_low = own.astype(BF16)
    ones = jnp.ones((KW, LANES), BF16)
    nothing = jnp.zeros((KW, LANES), BF16)

    def heads_in(ref, at):
        return cat([ref[at, :]] * heads, 0) * own_low

    def heads_out(v):
        v = v * own
        return (v[0:WQ] + v[WQ : 2 * WQ]) + (v[2 * WQ : 3 * WQ] + v[3 * WQ : 4 * WQ])

    def window(t):
        s, w = divmod(t, nwin)
        return s, slice(s * rows + w * WQ, s * rows + (w + 1) * WQ), slice(w * WQ, w * WQ + KW)

    def inner(t):
        w = t % nwin
        return w * WQ >= HALO and w * WQ + KW <= HALO + rows

    middle = [t for t in range(windows) if inner(t)]
    border = [t for t in range(windows) if not inner(t)]

    def attend(ts):
        for t in ts:
            s, at, keys = window(t)
            queries = heads_in(qh_s, at), heads_in(ql_s, at)
            prob[t] = nt(queries, (kvh[s, keys, :LANES], kvl[s, keys, :LANES])) + bias[t]
        for t in ts:
            s, at, keys = window(t)
            scores = prob[t]
            expo = jnp.exp(scores - jnp.max(scores, axis=-1, keepdims=True))
            eh, el = split(expo)
            vh, vl = kvh[s, keys, LANES:], kvl[s, keys, LANES:]
            high = cat([vh, ones], 1)
            both = dot(cat([eh, el, eh], 1), cat([high, high, cat([vl, nothing], 1)], 0), NN)
            inv = 1.0 / both[:, LANES:]
            prob[t] = expo * inv
            mixed_s[at, :] = heads_out(both[:, :LANES] * inv)

    attend(middle)
    halos_here()
    for s in range(samples):
        for absent, at in ((me == 0, slice(0, HALO)), (me == seqn - 1, slice(HALO + rows, 2 * HALO + rows))):
            kvh[s, at], kvl[s, at] = split(jnp.where(absent, 0.0, kv[s, at]))
    attend(border)

    def put(acc, names, value):
        at = 0
        for name in names:
            base = PLACE[name]
            for b in range(dict((n, c) for n, _, c in EARLY + LATE)[name]):
                acc[base + b * value.shape[0] : base + (b + 1) * value.shape[0]] = value[:, at : at + LANES]
                at += LANES

    gated = gate_s[...] * mixed_s[...]
    gated_split = split(gated)
    projected = beside(gated_split, (woh[...], wol[...]), NN)
    z2 = z2_s[...]
    g = cot[...]
    d_down_split = split(g * z2)
    d_hidden = nt(d_down_split, (wdh[...], wdl[...]))
    first = atoms[...] + z1_s[...] * projected
    nf, rf = norm(first)
    sc2 = sc2_s[...]
    n2_split = split(sc2 * nf + sh2_s[...])
    up = nn(n2_split, (whh[...], whl[...]))
    hidden_width = up.shape[1] // 2
    hg, hu = up[:, :hidden_width], up[:, hidden_width:]
    sg = sigmoid(hg)
    silu = hg * sg
    hidden_split = split(silu * hu)
    d_up_split = split(cat([d_hidden * hu * (sg + silu * (1.0 - sg)), d_hidden * silu], 1))

    d_n2 = beside(d_up_split, (whh[...], whl[...]), NT)
    down = beside(hidden_split, (wdh[...], wdl[...]), NN)
    dn2_s[...] = d_n2
    d_first = g + norm_back(d_n2 * sc2, nf, rf)
    dfirst_s[...] = d_first
    put(acc_e, ["w_down"], tn(hidden_split, d_down_split))
    put(acc_e, ["w_hidden_gate", "w_hidden_up"], tn(n2_split, d_up_split))
    z1 = z1_s[...]
    d_proj_split = split(d_first * z1)
    d_gated = beside(d_proj_split, (woh[...], wol[...]), NT)
    dsc2 = d_n2 * nf * sc2 * (1.0 - sc2)
    dsc2_s[...] = dsc2
    cond2_split = split(ns_s[...] * p_s_gain2[...])
    put(acc_e, ["w_scale2", "w_shift2"], tn(cond2_split, split(cat([dsc2, d_n2], 1))))
    out[...] = first + z2 * down
    dz2 = g * down * z2 * (1.0 - z2)
    dz2_s[...] = dz2
    dz1 = d_first * projected * z1 * (1.0 - z1)
    dz1_s[...] = dz1
    gate = gate_s[...]
    mixed = mixed_s[...]
    d_gate = d_gated * mixed * gate * (1.0 - gate)
    gpre_s[...] = d_gate
    d_mixed = d_gated * gate
    mh_s[...], ml_s[...] = split(d_mixed)
    th_s[...], tl_s[...] = split(d_mixed * mixed)
    put(acc_e, ["w_out"], tn(gated_split, d_proj_split))
    put(acc_e, ["w_zero1", "w_zero2"], tn(split(single[...]), split(cat([dz1, dz2], 1))))
    put(acc_e, ["w_gate"], tn(split(n1_s[...]), split(d_gate)))
    if early.size > EARLY_ROWS:
        acc_e[EARLY_ROWS:] = jnp.zeros((early.size - EARLY_ROWS, LANES), F32)

    groups = {"plane": (nxy, k, xy_peer), "line": (nz, z, z_peer)}

    def travelling(plan, acc, res, landing, sems):
        half = plan.size // 2
        base = core * half
        step = [0]

        def send(src, dst, device):
            return remote(src, dst, sems[0].at[step[0]], sems[1].at[step[0]], device)

        def arrived(rows_in):
            some = acc_e.at[0:rows_in]
            remote(some, some, sems[0].at[step[0]], sems[1].at[step[0]], other).wait()
            step[0] += 1

        def gathers(name, where):
            n, _, peer = groups[name]
            return [send(res.at[where], res.at[where], peer(o)[1]) for o in range(1, n)]

        places = []
        for i, (first, rows_at, rows_in) in enumerate(plan.parts):
            second = "line" if first == "plane" else "plane"
            here = base + rows_at
            one = rows_in // groups[first][0]
            two = one // groups[second][0]
            mine = here + groups[first][1] * one
            places.append((first, second, here, one, two, mine, landing[1 + 2 * i], landing[2 + 2 * i]))

        def run():
            copies = start([send(acc.at[span((1 - core) * half, half)], landing[0], other)])
            yield
            arrived(half)
            acc[span(base, half), :] += landing[0][...]
            copies = []
            for first, _, here, one, _, _, land, _ in places:
                n, _, peer = groups[first]
                for o in range(1, n):
                    index, device = peer(o)
                    copies.append(send(acc.at[span(here + index * one, one)], land.at[o - 1], device))
            start(copies)
            yield
            arrived(sum((groups[p[0]][0] - 1) * p[3] for p in places))
            copies = []
            for first, second, _, one, two, mine, land, land2 in places:
                value = acc[span(mine, one), :]
                for o in range(1, groups[first][0]):
                    value = value + land[o - 1]
                acc[span(mine, one), :] = value
                n, own_index, peer = groups[second]
                for o in range(1, n):
                    index, device = peer(o)
                    if plan.whole:
                        copies.append(send(acc.at[span(mine, one)], land2.at[own_index], device))
                    else:
                        copies.append(send(acc.at[span(mine + index * two, two)], land2.at[o - 1], device))
            start(copies)
            if plan.whole:
                for _, second, _, one, _, mine, _, land2 in places:
                    land2[groups[second][1]] = acc[span(mine, one), :]
            yield
            arrived(sum((groups[p[1]][0] - 1) * (p[3] if plan.whole else p[4]) for p in places))
            copies = []
            for first, second, _, one, two, mine, _, land2 in places:
                n, own_index, _ = groups[second]
                if plan.whole:
                    res[span(mine, one), :] = add_up(land2, n)
                    copies += gathers(first, span(mine, one))
                else:
                    at = mine + own_index * two
                    value = acc[span(at, two), :]
                    for o in range(1, n):
                        value = value + land2[o - 1]
                    res[span(at, two), :] = value
                    copies += gathers(second, span(at, two))
            start(copies)
            yield
            if not plan.whole:
                arrived(sum((groups[p[1]][0] - 1) * p[4] for p in places))
                copies = []
                for first, _, _, one, _, mine, _, _ in places:
                    copies += gathers(first, span(mine, one))
                start(copies)
                yield
            arrived(sum((groups[p[0]][0] - 1) * p[3] for p in places))
            copies = start([send(res.at[span(base, half)], res.at[span(base, half)], other)])
            yield
            arrived(half)
            yield

        steps = run()
        return lambda: next(steps)

    def add_up(slots, count):
        value = slots[0]
        for i in range(1, count):
            value = value + slots[i]
        return value

    go_early = travelling(early, acc_e, res_e, landing_e, (e_send, e_recv))
    go_late = travelling(late, acc_l, res_l, landing_l, (l_send, l_recv))
    go_early()

    dkv[...] = jnp.zeros_like(dkv)
    less = -jnp.ones((KW, LANES), BF16)

    def back_values(ts):
        for t in ts:
            s, at, keys = window(t)
            dkv[s, keys, LANES:] += tn(split(prob[t]), (heads_in(mh_s, at), heads_in(ml_s, at)))

    def back_keys(ts):
        for t in ts:
            s, at, keys = window(t)
            dkv[s, keys, :LANES] += tn(split(ds[t]), (heads_in(qh_s, at), heads_in(ql_s, at)))

    def swap_back(lanes, i):
        ends = slice(0, HALO), slice(HALO + rows, 2 * HALO + rows)
        return swap(
            remote(dkv.at[:, ends[0], lanes], dhalo.at[1, :, :, lanes], h_send.at[i], h_recv.at[i], left),
            remote(dkv.at[:, ends[1], lanes], dhalo.at[0, :, :, lanes], h_send.at[i + 1], h_recv.at[i + 1], right),
        )

    def back_scores(ts):
        for t in ts:
            s, at, keys = window(t)
            mh, ml = heads_in(mh_s, at), heads_in(ml_s, at)
            th, tl = heads_in(th_s, at), heads_in(tl_s, at)
            vh, vl = kvh[s, keys, LANES:], kvl[s, keys, LANES:]
            ds[t] = prob[t] * dot(cat([mh, ml, mh, th, tl], 1), cat([vh, vh, vl, less, less], 1), NT)

    back_values(border)
    values_here = swap_back(slice(LANES, 2 * LANES), 2)
    back_scores(border)
    back_keys(border)
    keys_here = swap_back(slice(0, LANES), 4)
    back_scores(middle)
    go_early()

    back_keys(middle)
    back_values(middle)
    for t in range(windows):
        s, at, keys = window(t)
        dq_s[at, :] = heads_out(nn(split(ds[t]), (kvh[s, keys, :LANES], kvl[s, keys, :LANES]))) * scale

    dq = dq_s[...]
    rest = split(cat([dq, gpre_s[...]], 1))
    n1_split = split(n1_s[...])
    d_n1 = beside(rest, (wqh[:, 2 * LANES :], wql[:, 2 * LANES :]), NT)
    put(acc_l, ["w_query"], tn(n1_split, (rest[0][:, :LANES], rest[1][:, :LANES])))

    gacc[...] = jnp.zeros_like(gacc)
    gmid[...] = jnp.zeros_like(gmid)

    def fold(v):
        return (v[0:8] + v[8:16]) + (v[16:24] + v[24:32])

    def pair_back(t, carry):
        s, w = t // nwin, lax.rem(t, nwin)
        inv, live = prs[t, 0], prs[t, 1]
        mean = pmean[t]
        u, along = [], None
        for h in range(heads):
            d = ds[t, h * WQ : (h + 1) * WQ]
            u.append(d * inv)
            a = d * bias[t, h * WQ : (h + 1) * WQ]
            along = a if along is None else along + a
            gmid[h] += fold(mean * u[h])
        c1 = along * live
        c0 = mean * c1
        for p in range(channels):
            v = pair[s, w, p]
            d = c0 - v * c1
            for h in range(heads):
                d = d + u[h] * centred[p][h]
                gacc[h * channels + p] += fold(v * u[h])
            g_pair[s, w, p] = d
        return carry

    ahead = 3 * windows // 8
    lax.fori_loop(0, ahead, pair_back, 0)

    values_here()
    keys_here()
    for s in range(samples):
        dkv[s, HALO : 2 * HALO] += jnp.where(me == 0, 0.0, dhalo[0, s])
        dkv[s, rows : rows + HALO] += jnp.where(me == seqn - 1, 0.0, dhalo[1, s])

    d_keys_values = split(cat([dkv[s, HALO : HALO + rows] for s in range(samples)], 0))
    d_n1 = d_n1 + beside(d_keys_values, (wqh[:, : 2 * LANES], wql[:, : 2 * LANES]), NT)
    na = na_s[...]
    sc1 = sc1_s[...]
    dsc1 = d_n1 * na * sc1 * (1.0 - sc1)
    d_first1 = split(cat([dsc1, d_n1], 1))
    ns = ns_s[...]
    put(acc_l, ["w_key", "w_value"], tn(n1_split, d_keys_values))
    put(acc_l, ["w_scale1", "w_shift1"], tn(split(ns * p_s_gain1[...]), d_first1))
    if late.size > LATE_ROWS:
        acc_l[LATE_ROWS:] = jnp.zeros((late.size - LATE_ROWS, LANES), F32)
    go_late()

    g_atoms[...] = dfirst_s[...] + norm_back(d_n1 * sc1, na, ra_s[...])
    go_late()
    go_early()
    lax.fori_loop(ahead, windows, pair_back, 0)

    d_cond1 = beside(d_first1, (w1h[...], w1l[...]), NT)
    d_cond2 = beside(split(cat([dsc2_s[...], dn2_s[...]], 1)), (w2h[...], w2l[...]), NT)

    eye = (
        lax.broadcasted_iota(jnp.int32, (channels, LANES), 0) == lax.broadcasted_iota(jnp.int32, (channels, LANES), 1)
    ).astype(F32)
    gsum = jnp.sum(jnp.sum(gacc[...], axis=1), axis=-1, keepdims=True)
    gless = jnp.sum(jnp.sum(gmid[...], axis=1, keepdims=True), axis=-1, keepdims=True)
    rows_g = [column_sum((gsum[h * channels : (h + 1) * channels] - gless[h]) * eye) for h in range(heads)]
    blank = jnp.zeros((1, LANES - channels), F32)
    gain_row = cat([p_pair_gain[...], blank], 1)
    pair_row = jnp.zeros((1, LANES), F32)
    for h in range(heads):
        pair_row = pair_row + rows_g[h] * cat([p_w_pair[h : h + 1, :], blank], 1)
    pair_grad = cat([v * gain_row for v in rows_g] + [jnp.zeros((8 - heads, LANES), F32)], 0)
    small = {
        "b_scale1": column_sum(dsc1),
        "b_query": column_sum(dq),
        "b_scale2": column_sum(dsc2_s[...]),
        "b_zero1": column_sum(dz1_s[...]),
        "b_zero2": column_sum(dz2_s[...]),
        "s_gain1": column_sum(d_cond1 * ns),
        "s_gain2": column_sum(d_cond2 * ns),
        "pair_gain": pair_row,
    }
    acc_s[...] = cat([small[name] for name in VECTORS] + [pair_grad], 0)
    s1 = start([remote(acc_s, recv_sc, s_send.at[0], s_recv.at[0], other)])
    d_ns = d_cond1 * p_s_gain1[...] + d_cond2 * p_s_gain2[...]
    g_single[...] = norm_back(d_ns, ns, rs_s[...]) + nt(
        split(cat([dz1_s[...], dz2_s[...]], 1)), (wzh[...], wzl[...])
    )

    def spread(slots, mine, peers, i):
        slots[mine] = acc_s[...]
        start([remote(acc_s, slots.at[mine], s_send.at[i], s_recv.at[i], device) for device in peers])

        def end():
            some = acc_e.at[0 : 16 * len(peers)]
            remote(some, some, s_send.at[i], s_recv.at[i], other).wait()

        return end

    go_late()
    go_early()
    wait(s1)
    acc_s[...] = acc_s[...] + recv_sc[...]
    s2 = spread(recv_sxy, k, [xy_peer(o)[1] for o in range(1, nxy)], 1)
    s2()
    acc_s[...] = add_up(recv_sxy, nxy)
    s3 = spread(recv_sz, z, [z_peer(o)[1] for o in range(1, nz)], 2)
    go_late()
    go_early()
    s3()
    res_s[...] = add_up(recv_sz, nz)
    go_late()
    go_early()
    go_late()
    go_early()


class Plan:
    def __init__(self, needed, nxy, nz, whole):
        half = -(-needed // 2)
        grains = (8 * nxy, 8 * nz) if whole else (8 * nxy * nz,) * 2
        line = int(half * (0.4 if whole else 0.34)) // grains[1] * grains[1]
        plane = -(-(half - line) // grains[0]) * grains[0]
        self.whole, self.size = whole, 2 * (plane + line)
        self.parts = [("plane", 0, plane)] + ([("line", plane, line)] if line else [])

    def landing(self, nxy, nz):
        count = {"plane": (nxy, nz), "line": (nz, nxy)}
        shapes = [(self.size // 2, LANES)]
        for first, _, rows in self.parts:
            n, m = count[first]
            shapes.append((n - 1, rows // n, LANES))
            shapes.append((m, rows // n, LANES) if self.whole else (m - 1, rows // n // m, LANES))
        return shapes

    def steps(self):
        return 5 if self.whole else 6


def unpack_kernel(*refs):
    n, v = len(EARLY) + len(LATE), len(VECTORS)
    ins, refs = refs[:7], refs[7:]
    outs, mats, rows, wp, sems = refs[:4], refs[4 : 4 + n], refs[4 + n : 4 + n + v], refs[4 + n + v], refs[5 + n + v]
    copies = []

    def move(a, b):
        copies.append(pltpu.make_async_copy(a, b, sems.at[len(copies)]))
        copies[-1].start()

    for a, b in zip(ins[3::-1], outs[::-1]):
        for c in range(a.shape[0]):
            move(a.at[c], b.at[c])
    at = 0
    for group, packed in ((EARLY, ins[4]), (LATE, ins[5])):
        for name, _, columns in group:
            base, height = PLACE[name], mats[at].shape[0]
            for b in range(columns):
                move(packed.at[pl.ds(base + b * height, height)], mats[at].at[:, pl.ds(b * LANES, LANES)])
            at += 1
    for i, ref in enumerate(rows):
        ref[...] = ins[6][i : i + 1, 0 : ref.shape[1]]
    wp[...] = ins[6][v : v + wp.shape[0], 0 : wp.shape[1]]
    for copy in copies:
        copy.wait()


def shards(dpn, seqn, atoms, single_cond, pair_block, atom_count, *rest):
    params, cotangent = dict(zip(PARAMS, rest[:-1])), rest[-1]
    params["w_pair"] = params["w_pair"].T
    samples, rows, width = atoms.shape
    nwin, channels = pair_block.shape[1:3]
    heads = params["w_pair"].shape[0]
    flat = samples * rows
    nz, nx = 4, seqn // 8
    nxy = dpn * nx
    early = Plan(EARLY_ROWS, nxy, nz, False)
    late = Plan(LATE_ROWS, nxy, nz, True)
    windows = samples * nwin
    hidden = params["w_down"].shape[0]

    def row(v):
        return v.reshape(1, -1) if v.ndim == 1 else v

    vmem = pl.BlockSpec(memory_space=pltpu.VMEM)
    anyw = pl.BlockSpec(memory_space=pl.ANY)

    def buf(*shape):
        return pltpu.VMEM(shape, F32)

    def low(*shape):
        return [pltpu.VMEM(shape, BF16), pltpu.VMEM(shape, BF16)]

    def sems(n):
        return [pltpu.SemaphoreType.DMA((n,)), pltpu.SemaphoreType.DMA((n,))]

    tall = (flat, width)
    extended = (samples, rows + 2 * HALO, 2 * width)
    scratch = [
        buf(*pair_block.shape),
        buf(windows, heads * WQ, KW),
        buf(windows, WQ, KW),
        buf(windows, 2, WQ, KW),
        buf(windows, heads * WQ, KW),
        buf(windows, heads * WQ, KW),
        buf(*extended),
        buf(*extended),
        buf(2, samples, HALO, 2 * width),
    ]
    scratch += low(*extended)
    scratch += low(width, 2 * width)
    scratch += low(width, 4 * width)
    scratch += low(width, 2 * width)
    scratch += low(width, 2 * width)
    scratch += low(width, 2 * hidden)
    scratch += low(hidden, width)
    scratch += low(width, width)
    scratch += low(*tall) + low(*tall) + low(*tall)
    scratch += [buf(*tall) for _ in range(19)]
    scratch += [
        buf(heads * channels, 8, KW),
        buf(heads, 8, KW),
        buf(early.size, LANES),
        buf(late.size, LANES),
        buf(16, LANES),
        buf(16, LANES),
        buf(nxy, 16, LANES),
        buf(nz, 16, LANES),
        pltpu.SemaphoreType.DMA((samples,)),
    ]
    scratch += sems(6) + sems(early.steps()) + sems(late.steps()) + sems(3)
    scratch += [buf(*shape) for plan in (early, late) for shape in plan.landing(nxy, nz)]
    arrays = [
        atom_count,
        params["pair_gain"],
        params["w_pair"],
        atoms.reshape(tall),
        single_cond.reshape(tall),
        cotangent.reshape(tall),
        *[row(params[name]) for name in PARAMS],
        pair_block,
    ]
    scratch += [pltpu.SMEM(v.shape, v.dtype) for v in arrays[:3]]
    scratch += [buf(*v.shape) for v in arrays[3:-1]]
    scratch += [pltpu.SemaphoreType.DMA((4 + len(arrays) - 1 - 14,))]
    sizes = (samples, rows, dpn, seqn, early, late)
    big = pl.pallas_call(
        functools.partial(block_kernel, sizes),
        out_shape=[buf(*shape) for shape in (tall, tall, tall, pair_block.shape, (early.size, LANES), (late.size, LANES), (16, LANES))],
        in_specs=[anyw] * (7 + len(PARAMS)),
        out_specs=[vmem] * 7,
        scratch_shapes=scratch,
        compiler_params=pltpu.CompilerParams(
            collective_id=0, has_side_effects=True, vmem_limit_bytes=40 * 2**20
        ),
        name="block",
    )(*[pltpu.with_memory_space_constraint(v, pltpu.HBM) for v in arrays])

    names = [name for name, _, _ in EARLY + LATE]
    mats = [jax.ShapeDtypeStruct(params[name].shape, F32) for name in names]
    vecs = [jax.ShapeDtypeStruct((1, params[name].shape[0]), F32) for name in VECTORS]
    big = list(big)
    for i in range(3):
        big[i] = big[i].reshape(1, *tall)
    results = pl.pallas_call(
        unpack_kernel,
        out_shape=[jax.ShapeDtypeStruct(v.shape, F32) for v in big[:4]]
        + mats
        + vecs
        + [jax.ShapeDtypeStruct((heads, channels), F32)],
        in_specs=[vmem] * 7,
        out_specs=[anyw] * (4 + len(mats)) + [vmem] * (len(vecs) + 1),
        scratch_shapes=[
            pltpu.SemaphoreType.DMA((sum(c for _, _, c in EARLY + LATE) + sum(v.shape[0] for v in big[:4]),)),
        ],
        compiler_params=pltpu.CompilerParams(vmem_limit_bytes=16 * 2**20),
        name="unpack",
    )(*[pltpu.with_memory_space_constraint(v, pltpu.VMEM) for v in big])
    grads = dict(zip(names, results[4:]))
    for name, value in zip(VECTORS, results[4 + len(mats) :]):
        grads[name] = value.reshape(-1)
    grads["w_pair"] = results[-1].T
    out, g_atoms, g_single, g_pair = results[:4]
    return (
        out.reshape(atoms.shape),
        g_atoms.reshape(atoms.shape),
        g_single.reshape(atoms.shape),
        g_pair.reshape(pair_block.shape),
    ) + tuple(grads[name] for name in PARAMS)


def solution(mesh):
    data = P("dp", "seq", None)
    pairs = P("dp", "seq", None, None, None)
    return jax.shard_map(
        functools.partial(shards, mesh.shape["dp"], mesh.shape["seq"]),
        mesh=mesh,
        in_specs=(data, data, pairs, P("dp")) + (P(),) * len(PARAMS) + (data,),
        out_specs=(data, data, data, pairs) + (P(),) * len(PARAMS),
        check_vma=False,
    )
```

```python
import functools
import math

import jax
import jax.numpy as jnp
from jax import lax
from jax.experimental import pallas as pl
from jax.experimental.pallas import tpu as pltpu
from jax.sharding import PartitionSpec as P

WQ = 32
KW = 128
HALO = 48
LANES = 128
MESH = pl.DeviceIdType.MESH
F32 = jnp.float32

EARLY = (
    ("w_down", 2, 1),
    ("w_hidden_gate", 1, 2),
    ("w_hidden_up", 1, 2),
    ("w_zero2", 1, 1),
    ("w_scale2", 1, 1),
    ("w_shift2", 1, 1),
    ("w_out", 1, 1),
    ("w_zero1", 1, 1),
    ("w_gate", 1, 1),
)
LATE = (
    ("w_query", 1, 1),
    ("w_key", 1, 1),
    ("w_value", 1, 1),
    ("w_scale1", 1, 1),
    ("w_shift1", 1, 1),
)
VECTORS = ("b_scale1", "b_query", "b_scale2", "b_zero1", "b_zero2", "s_gain1", "s_gain2", "pair_gain")
PARAMS = (
    "s_gain1",
    "w_scale1",
    "b_scale1",
    "w_shift1",
    "w_query",
    "b_query",
    "w_key",
    "w_value",
    "w_gate",
    "pair_gain",
    "w_pair",
    "w_out",
    "w_zero1",
    "b_zero1",
    "s_gain2",
    "w_scale2",
    "b_scale2",
    "w_shift2",
    "w_hidden_gate",
    "w_hidden_up",
    "w_down",
    "w_zero2",
    "b_zero2",
)


def offsets():
    place, used = {}, []
    for group in (EARLY, LATE):
        row = 0
        for name, rows, columns in group:
            place[name] = row
            row += rows * columns * LANES
        used.append(row)
    return place, used[0], used[1]


PLACE, EARLY_ROWS, LATE_ROWS = offsets()
BF16 = jnp.bfloat16
NN = (((1,), (0,)), ((), ()))
NT = (((1,), (1,)), ((), ()))
TN = (((0,), (0,)), ((), ()))


def dot(a, b, dims):
    return lax.dot_general(a, b, dims, preferred_element_type=F32)


def cat(parts, axis):
    return jnp.concatenate(parts, axis=axis)


def split(x):
    high = x.astype(BF16)
    return high, (x - high.astype(F32)).astype(BF16)


def product(a, b, dims):
    (ah, al), (bh, bl) = a, b
    (ka,), (kb,) = dims[0]
    return dot(cat([ah, al, ah], ka), cat([bh, bh, bl], kb), dims)


def beside(a, b, dims):
    (ah, al), (bh, bl) = a, b
    free = 1 - dims[0][1][0]
    width = bh.shape[free]
    both = dot(ah, cat([bh, bl], free), dims)
    return both[:, :width] + (both[:, width:] + dot(al, bh, dims))


def nn(a, b):
    return product(a, b, NN)


def nt(a, b):
    return product(a, b, NT)


def tn(a, b):
    return product(a, b, TN)


def mean_lanes(x):
    weight = jnp.full((2 * LANES, LANES), 1.0 / LANES, BF16)
    return dot(cat(split(x), 1), weight, NN)


def norm(x):
    cent = x - mean_lanes(x)
    inv = lax.rsqrt(mean_lanes(cent * cent) + 1e-05)
    return cent * inv, inv


def norm_back(d, xhat, inv):
    return (d - mean_lanes(d) - xhat * mean_lanes(d * xhat)) * inv


def sigmoid(x):
    return 1.0 / (1.0 + jnp.exp(-x))


def column_sum(x):
    return jnp.sum(x, axis=0, keepdims=True)


def block_kernel(sizes, *refs):
    samples, rows, dpn, seqn, early, late = sizes
    nwin = rows // WQ
    windows = samples * nwin
    flat = samples * rows
    nz = 4
    nx = seqn // (2 * nz)
    nxy = dpn * nx
    n_in = 6 + len(PARAMS)
    given, refs = refs[:n_in], refs[n_in:]
    held, refs = refs[-n_in - 1 : -1], refs[:-n_in - 1] + refs[-1:]
    n_e, n_l = 1 + 2 * len(early.parts), 1 + 2 * len(late.parts)
    landing_e, landing_l, refs = refs[-n_e - n_l - 1 : -n_l - 1], refs[-n_l - 1 : -1], refs[: -n_e - n_l - 1] + refs[-1:]
    (
        count,
        gain_s,
        wpair_s,
        atoms,
        single,
        cot,
        p_s_gain1,
        p_w_scale1,
        p_b_scale1,
        p_w_shift1,
        p_w_query,
        p_b_query,
        p_w_key,
        p_w_value,
        p_w_gate,
        p_pair_gain,
        p_w_pair,
        p_w_out,
        p_w_zero1,
        p_b_zero1,
        p_s_gain2,
        p_w_scale2,
        p_b_scale2,
        p_w_shift2,
        p_w_hidden_gate,
        p_w_hidden_up,
        p_w_down,
        p_w_zero2,
        p_b_zero2,
    ) = held
    (
        pair_hbm,
        out,
        g_atoms,
        g_single,
        g_pair,
        res_e,
        res_l,
        res_s,
        pair,
        bias,
        pmean,
        prs,
        prob,
        ds,
        kv,
        dkv,
        dhalo,
        kvh,
        kvl,
        w1h,
        w1l,
        wqh,
        wql,
        wzh,
        wzl,
        w2h,
        w2l,
        whh,
        whl,
        wdh,
        wdl,
        woh,
        wol,
        qh_s,
        ql_s,
        mh_s,
        ml_s,
        th_s,
        tl_s,
        mixed_s,
        ns_s,
        na_s,
        n1_s,
        sc1_s,
        sc2_s,
        sh2_s,
        gate_s,
        z1_s,
        z2_s,
        rs_s,
        ra_s,
        dq_s,
        dfirst_s,
        dz1_s,
        dz2_s,
        dn2_s,
        dsc2_s,
        gpre_s,
        gacc,
        gmid,
        acc_e,
        acc_l,
        acc_s,
        recv_sc,
        recv_sxy,
        recv_sz,
        pair_sem,
        h_send,
        h_recv,
        e_send,
        e_recv,
        l_send,
        l_recv,
        s_send,
        s_recv,
        in_sem,
    ) = refs
    dp = lax.axis_index("dp")
    me = lax.axis_index("seq")
    core = lax.rem(me, 2)
    x = lax.rem(me // 2, nx)
    z = me // (2 * nx)
    k = dp * nx + x
    left = (dp, lax.rem(me + seqn - 1, seqn))
    right = (dp, lax.rem(me + 1, seqn))
    other = (dp, me + 1 - 2 * core)

    def flipped(index, o):
        bit = 1
        while bit <= o:
            if o // bit % 2:
                index = index + bit - 2 * bit * lax.rem(index // bit, 2)
            bit *= 2
        return index

    def xy_peer(o):
        kk = flipped(k, o)
        return kk, (kk // nx, (z * nx + lax.rem(kk, nx)) * 2 + core)

    def z_peer(o):
        zz = flipped(z, o)
        return zz, (dp, (zz * nx + x) * 2 + core)

    norm_weights = (p_w_scale1, p_w_shift1)
    projections = (p_w_key, p_w_value, p_w_query, p_w_gate)
    conditions = (p_w_zero1, p_w_zero2, p_w_scale2, p_w_shift2)
    transition = (p_w_hidden_gate, p_w_hidden_up, p_w_down, p_w_out)
    together = (norm_weights, projections, conditions, transition)
    sem_of = [[i for i, group in enumerate(together) if any(ref is r for r in group)] for ref in held]
    used = len(together)
    for found in sem_of:
        if not found:
            found.append(used)
            used += 1

    def where(ref):
        return [ref is h for h in held].index(True)

    def bring(*which):
        for ref in which:
            i = where(ref)
            pltpu.make_async_copy(given[i], ref, in_sem.at[sem_of[i][0]]).start()

    def ready(*which):
        for ref in which:
            if isinstance(ref, tuple):
                total = sum(r.shape[0] * r.shape[1] for r in ref) // LANES
                some = acc_e.at[0:total]
                pltpu.make_async_copy(some, some, in_sem.at[sem_of[where(ref[0])][0]]).wait()
            else:
                i = where(ref)
                pltpu.make_async_copy(given[i], ref, in_sem.at[sem_of[i][0]]).wait()

    scalars = (count, gain_s, wpair_s)
    bring(single, atoms, p_s_gain1, *norm_weights, p_b_scale1, *projections, p_b_query, *scalars)
    bring(*conditions, p_s_gain2, p_b_scale2, p_b_zero1, p_b_zero2)

    def pair_load(s, w):
        return pltpu.make_async_copy(pair_hbm.at[s, w], pair.at[s, w], pair_sem.at[s])

    for t in range(windows):
        pair_load(t // nwin, t % nwin).start()
    bring(*transition, cot, p_pair_gain, p_w_pair)

    barrier = pltpu.get_barrier_semaphore()
    greeted = [left, right, other]
    greeted += [xy_peer(o)[1] for o in range(1, nxy)]
    greeted += [z_peer(o)[1] for o in range(1, nz)]
    for device in greeted:
        pl.semaphore_signal(barrier, inc=1, device_id=device, device_id_type=MESH)

    def remote(src, dst, send, recv, device):
        return pltpu.make_async_remote_copy(
            src_ref=src, dst_ref=dst, send_sem=send, recv_sem=recv, device_id=device, device_id_type=MESH
        )

    def start(copies):
        for copy in copies:
            copy.start()
        return copies

    def wait(copies):
        for copy in copies:
            copy.wait()

    def span(first, size):
        return pl.ds(pl.multiple_of(first, 8), size)

    def hold(high, low, *weights):
        for c, w in enumerate(weights):
            width = w.shape[1]
            high[:, c * width : (c + 1) * width], low[:, c * width : (c + 1) * width] = split(w[...])

    ready(single, atoms, norm_weights, p_s_gain1, p_b_scale1)
    hold(w1h, w1l, p_w_scale1, p_w_shift1)
    xs, xa = single[...], atoms[...]
    cs, ca = xs - mean_lanes(xs), xa - mean_lanes(xa)
    rs, ra = lax.rsqrt(mean_lanes(cs * cs) + 1e-05), lax.rsqrt(mean_lanes(ca * ca) + 1e-05)
    ns, na = cs * rs, ca * ra
    ns_s[...] = ns
    na_s[...] = na
    rs_s[...] = rs
    ra_s[...] = ra
    first1 = nn(split(ns * p_s_gain1[...]), (w1h[...], w1l[...]))
    sc1 = sigmoid(first1[:, :LANES] + p_b_scale1[...])
    sc1_s[...] = sc1
    n1 = sc1 * na + first1[:, LANES:]
    n1_s[...] = n1
    n1_split = split(n1)
    ready(projections, p_b_query)
    hold(wqh, wql, p_w_key, p_w_value, p_w_query, p_w_gate)
    keys_values = nn(n1_split, (wqh[:, : 2 * LANES], wql[:, : 2 * LANES]))
    for s in range(samples):
        block = keys_values[s * rows : (s + 1) * rows]
        kv[s, HALO : HALO + rows] = block
        kvh[s, HALO : HALO + rows], kvl[s, HALO : HALO + rows] = split(block)

    def swap(leftward, rightward):
        def begin():
            @pl.when(me > 0)
            def _():
                leftward.start()

            @pl.when(me < seqn - 1)
            def _():
                rightward.start()

        def end():
            @pl.when(me > 0)
            def _():
                leftward.wait_send()
                rightward.wait_recv()

            @pl.when(me < seqn - 1)
            def _():
                rightward.wait_send()
                leftward.wait_recv()

        begin()
        return end

    pl.semaphore_wait(barrier, len(greeted))
    halos_here = swap(
        remote(kv.at[:, HALO : 2 * HALO], kv.at[:, HALO + rows : 2 * HALO + rows], h_send.at[1], h_recv.at[1], left),
        remote(kv.at[:, rows : rows + HALO], kv.at[:, 0:HALO], h_send.at[0], h_recv.at[0], right),
    )

    ready(*scalars)
    channels = gain_s.shape[0]
    heads = wpair_s.shape[0]
    wg = [[gain_s[p] * wpair_s[h, p] for h in range(heads)] for p in range(channels)]
    mid = [functools.reduce(lambda a, b: a + b, [wg[p][h] for p in range(channels)]) * (1.0 / channels) for h in range(heads)]
    centred = [[wg[p][h] - mid[h] for h in range(heads)] for p in range(channels)]

    key_lane = lax.broadcasted_iota(jnp.int32, (WQ, KW), 1)
    same = key_lane == lax.broadcasted_iota(jnp.int32, (WQ, KW), 0) + HALO

    def pair_bias(t, carry):
        s, w = divmod(t, nwin) if isinstance(t, int) else (t // nwin, lax.rem(t, nwin))
        first = pair[s, w, 0]
        total, square = first, first * first
        b = [first * centred[0][h] for h in range(heads)]
        for p in range(1, channels):
            v = pair[s, w, p]
            total = total + v
            square = square + v * v
            b = [b[h] + v * centred[p][h] for h in range(heads)]
        mean = total * (1.0 / channels)
        var = square * (1.0 / channels) - mean * mean
        inv = lax.rsqrt(jnp.maximum(var, 0.25))
        pmean[t] = mean
        live = jnp.where(var > 0.25, 1.0, jnp.where(var == 0.25, 0.5, 0.0))
        prs[t, 0] = inv
        prs[t, 1] = inv * inv * live * (1.0 / channels)
        begin = me * rows + w * WQ - HALO
        valid = ((key_lane >= -begin) & (key_lane < count[s] - begin)) | same
        for h in range(heads):
            bias[t, h * WQ : (h + 1) * WQ] = jnp.where(valid, inv * b[h], -1e9)
        return carry

    def pair_sample(s):
        pltpu.make_async_copy(pair_hbm.at[s], pair.at[s], pair_sem.at[s]).wait()
        for t in range(s * nwin, (s + 1) * nwin):
            pair_bias(t, 0)

    ready(conditions, p_s_gain2, p_b_scale2, p_b_zero1, p_b_zero2)
    pair_sample(0)
    hold(wzh, wzl, p_w_zero1, p_w_zero2)
    hold(w2h, w2l, p_w_scale2, p_w_shift2)
    scale = 1.0 / math.sqrt(32)
    query_gate = nn(n1_split, (wqh[:, 2 * LANES :], wql[:, 2 * LANES :]))
    qh_s[...], ql_s[...] = split((query_gate[:, :LANES] + p_b_query[...]) * scale)
    gate_s[...] = sigmoid(query_gate[:, LANES:])
    first2 = nn(split(ns * p_s_gain2[...]), (w2h[...], w2l[...]))
    sc2_s[...] = sigmoid(first2[:, :LANES] + p_b_scale2[...])
    sh2_s[...] = first2[:, LANES:]
    zeros = nn(split(single[...]), (wzh[...], wzl[...]))
    z1_s[...] = sigmoid(zeros[:, :LANES] + p_b_zero1[...])
    z2_s[...] = sigmoid(zeros[:, LANES:] + p_b_zero2[...])

    for s in range(1, samples):
        pair_sample(s)
    ready(transition, cot, p_pair_gain, p_w_pair)
    hold(whh, whl, p_w_hidden_gate, p_w_hidden_up)
    hold(wdh, wdl, p_w_down)
    hold(woh, wol, p_w_out)

    lane = lax.broadcasted_iota(jnp.int32, (heads * WQ, LANES), 1)
    row = lax.broadcasted_iota(jnp.int32, (heads * WQ, LANES), 0)
    own = (lane // 32 == row // WQ).astype(F32)
    own_low = own.astype(BF16)
    ones = jnp.ones((KW, LANES), BF16)
    nothing = jnp.zeros((KW, LANES), BF16)

    def heads_in(ref, at):
        return cat([ref[at, :]] * heads, 0) * own_low

    def heads_out(v):
        v = v * own
        return (v[0:WQ] + v[WQ : 2 * WQ]) + (v[2 * WQ : 3 * WQ] + v[3 * WQ : 4 * WQ])

    def window(t):
        s, w = divmod(t, nwin)
        return s, slice(s * rows + w * WQ, s * rows + (w + 1) * WQ), slice(w * WQ, w * WQ + KW)

    def inner(t):
        w = t % nwin
        return w * WQ >= HALO and w * WQ + KW <= HALO + rows

    middle = [t for t in range(windows) if inner(t)]
    border = [t for t in range(windows) if not inner(t)]

    def attend(ts):
        for t in ts:
            s, at, keys = window(t)
            queries = heads_in(qh_s, at), heads_in(ql_s, at)
            prob[t] = nt(queries, (kvh[s, keys, :LANES], kvl[s, keys, :LANES])) + bias[t]
        for t in ts:
            s, at, keys = window(t)
            scores = prob[t]
            expo = jnp.exp(scores - jnp.max(scores, axis=-1, keepdims=True))
            eh, el = split(expo)
            vh, vl = kvh[s, keys, LANES:], kvl[s, keys, LANES:]
            high = cat([vh, ones], 1)
            both = dot(cat([eh, el, eh], 1), cat([high, high, cat([vl, nothing], 1)], 0), NN)
            inv = 1.0 / both[:, LANES:]
            prob[t] = expo * inv
            mixed_s[at, :] = heads_out(both[:, :LANES] * inv)

    attend(middle)
    halos_here()
    for s in range(samples):
        for absent, at in ((me == 0, slice(0, HALO)), (me == seqn - 1, slice(HALO + rows, 2 * HALO + rows))):
            kvh[s, at], kvl[s, at] = split(jnp.where(absent, 0.0, kv[s, at]))
    attend(border)

    def put(acc, names, value):
        at = 0
        for name in names:
            base = PLACE[name]
            for b in range(dict((n, c) for n, _, c in EARLY + LATE)[name]):
                acc[base + b * value.shape[0] : base + (b + 1) * value.shape[0]] = value[:, at : at + LANES]
                at += LANES

    gated = gate_s[...] * mixed_s[...]
    gated_split = split(gated)
    projected = beside(gated_split, (woh[...], wol[...]), NN)
    z2 = z2_s[...]
    g = cot[...]
    d_down_split = split(g * z2)
    d_hidden = nt(d_down_split, (wdh[...], wdl[...]))
    first = atoms[...] + z1_s[...] * projected
    nf, rf = norm(first)
    sc2 = sc2_s[...]
    n2_split = split(sc2 * nf + sh2_s[...])
    up = nn(n2_split, (whh[...], whl[...]))
    hidden_width = up.shape[1] // 2
    hg, hu = up[:, :hidden_width], up[:, hidden_width:]
    sg = sigmoid(hg)
    silu = hg * sg
    hidden_split = split(silu * hu)
    d_up_split = split(cat([d_hidden * hu * (sg + silu * (1.0 - sg)), d_hidden * silu], 1))

    d_n2 = beside(d_up_split, (whh[...], whl[...]), NT)
    down = beside(hidden_split, (wdh[...], wdl[...]), NN)
    dn2_s[...] = d_n2
    d_first = g + norm_back(d_n2 * sc2, nf, rf)
    dfirst_s[...] = d_first
    put(acc_e, ["w_down"], tn(hidden_split, d_down_split))
    put(acc_e, ["w_hidden_gate", "w_hidden_up"], tn(n2_split, d_up_split))
    z1 = z1_s[...]
    d_proj_split = split(d_first * z1)
    d_gated = beside(d_proj_split, (woh[...], wol[...]), NT)
    dsc2 = d_n2 * nf * sc2 * (1.0 - sc2)
    dsc2_s[...] = dsc2
    cond2_split = split(ns_s[...] * p_s_gain2[...])
    put(acc_e, ["w_scale2", "w_shift2"], tn(cond2_split, split(cat([dsc2, d_n2], 1))))
    out[...] = first + z2 * down
    dz2 = g * down * z2 * (1.0 - z2)
    dz2_s[...] = dz2
    dz1 = d_first * projected * z1 * (1.0 - z1)
    dz1_s[...] = dz1
    gate = gate_s[...]
    mixed = mixed_s[...]
    d_gate = d_gated * mixed * gate * (1.0 - gate)
    gpre_s[...] = d_gate
    d_mixed = d_gated * gate
    mh_s[...], ml_s[...] = split(d_mixed)
    th_s[...], tl_s[...] = split(d_mixed * mixed)
    put(acc_e, ["w_out"], tn(gated_split, d_proj_split))
    put(acc_e, ["w_zero1", "w_zero2"], tn(split(single[...]), split(cat([dz1, dz2], 1))))
    put(acc_e, ["w_gate"], tn(split(n1_s[...]), split(d_gate)))
    if early.size > EARLY_ROWS:
        acc_e[EARLY_ROWS:] = jnp.zeros((early.size - EARLY_ROWS, LANES), F32)

    groups = {"plane": (nxy, k, xy_peer), "line": (nz, z, z_peer)}

    def travelling(plan, acc, res, landing, sems):
        half = plan.size // 2
        base = core * half
        step = [0]

        def send(src, dst, device):
            return remote(src, dst, sems[0].at[step[0]], sems[1].at[step[0]], device)

        def arrived(rows_in):
            some = acc_e.at[0:rows_in]
            remote(some, some, sems[0].at[step[0]], sems[1].at[step[0]], other).wait()
            step[0] += 1

        def gathers(name, where):
            n, _, peer = groups[name]
            return [send(res.at[where], res.at[where], peer(o)[1]) for o in range(n - 1, 0, -1)]

        places = []
        for i, (first, rows_at, rows_in) in enumerate(plan.parts):
            second = "line" if first == "plane" else "plane"
            here = base + rows_at
            one = rows_in // groups[first][0]
            two = one // groups[second][0]
            mine = here + groups[first][1] * one
            places.append((first, second, here, one, two, mine, landing[1 + 2 * i], landing[2 + 2 * i]))

        def run():
            copies = start([send(acc.at[span((1 - core) * half, half)], landing[0], other)])
            yield
            arrived(half)
            acc[span(base, half), :] += landing[0][...]
            copies = []
            for first, _, here, one, _, _, land, _ in places:
                n, _, peer = groups[first]
                for o in range(n - 1, 0, -1):
                    index, device = peer(o)
                    copies.append(send(acc.at[span(here + index * one, one)], land.at[o - 1], device))
            start(copies)
            yield
            arrived(sum((groups[p[0]][0] - 1) * p[3] for p in places))
            copies = []
            for first, second, _, one, two, mine, land, land2 in places:
                value = acc[span(mine, one), :]
                for o in range(1, groups[first][0]):
                    value = value + land[o - 1]
                acc[span(mine, one), :] = value
                n, own_index, peer = groups[second]
                for o in range(n - 1, 0, -1):
                    index, device = peer(o)
                    if plan.whole:
                        copies.append(send(acc.at[span(mine, one)], land2.at[own_index], device))
                    else:
                        copies.append(send(acc.at[span(mine + index * two, two)], land2.at[o - 1], device))
                start(copies)
                copies = []
            if plan.whole:
                for _, second, _, one, _, mine, _, land2 in places:
                    land2[groups[second][1]] = acc[span(mine, one), :]
            yield
            arrived(sum((groups[p[1]][0] - 1) * (p[3] if plan.whole else p[4]) for p in places))
            copies = []
            for first, second, _, one, two, mine, _, land2 in places:
                n, own_index, _ = groups[second]
                if plan.whole:
                    res[span(mine, one), :] = add_up(land2, n)
                    start(gathers(first, span(mine, one)))
                else:
                    at = mine + own_index * two
                    value = acc[span(at, two), :]
                    for o in range(1, n):
                        value = value + land2[o - 1]
                    res[span(at, two), :] = value
                    start(gathers(second, span(at, two)))
            yield
            if not plan.whole:
                arrived(sum((groups[p[1]][0] - 1) * p[4] for p in places))
                copies = []
                for first, _, _, one, _, mine, _, _ in places:
                    copies += gathers(first, span(mine, one))
                start(copies)
                yield
            arrived(sum((groups[p[0]][0] - 1) * p[3] for p in places))
            copies = start([send(res.at[span(base, half)], res.at[span(base, half)], other)])
            yield
            arrived(half)
            yield

        steps = run()
        return lambda: next(steps)

    def add_up(slots, count):
        value = slots[0]
        for i in range(1, count):
            value = value + slots[i]
        return value

    go_early = travelling(early, acc_e, res_e, landing_e, (e_send, e_recv))
    go_late = travelling(late, acc_l, res_l, landing_l, (l_send, l_recv))
    go_early()

    dkv[...] = jnp.zeros_like(dkv)
    less = -jnp.ones((KW, LANES), BF16)

    def back_values(ts):
        for t in ts:
            s, at, keys = window(t)
            dkv[s, keys, LANES:] += tn(split(prob[t]), (heads_in(mh_s, at), heads_in(ml_s, at)))

    def back_keys(ts):
        for t in ts:
            s, at, keys = window(t)
            dkv[s, keys, :LANES] += tn(split(ds[t]), (heads_in(qh_s, at), heads_in(ql_s, at)))

    def swap_back(lanes, i):
        ends = slice(0, HALO), slice(HALO + rows, 2 * HALO + rows)
        return swap(
            remote(dkv.at[:, ends[0], lanes], dhalo.at[1, :, :, lanes], h_send.at[i], h_recv.at[i], left),
            remote(dkv.at[:, ends[1], lanes], dhalo.at[0, :, :, lanes], h_send.at[i + 1], h_recv.at[i + 1], right),
        )

    def back_scores(ts):
        for t in ts:
            s, at, keys = window(t)
            mh, ml = heads_in(mh_s, at), heads_in(ml_s, at)
            th, tl = heads_in(th_s, at), heads_in(tl_s, at)
            vh, vl = kvh[s, keys, LANES:], kvl[s, keys, LANES:]
            ds[t] = prob[t] * dot(cat([mh, ml, mh, th, tl], 1), cat([vh, vh, vl, less, less], 1), NT)

    back_values(border)
    values_here = swap_back(slice(LANES, 2 * LANES), 2)
    back_scores(border)
    back_keys(border)
    keys_here = swap_back(slice(0, LANES), 4)
    back_scores(middle)
    go_early()

    back_keys(middle)
    back_values(middle)
    for t in range(windows):
        s, at, keys = window(t)
        dq_s[at, :] = heads_out(nn(split(ds[t]), (kvh[s, keys, :LANES], kvl[s, keys, :LANES]))) * scale

    dq = dq_s[...]
    rest = split(cat([dq, gpre_s[...]], 1))
    n1_split = split(n1_s[...])
    d_n1 = beside(rest, (wqh[:, 2 * LANES :], wql[:, 2 * LANES :]), NT)
    put(acc_l, ["w_query"], tn(n1_split, (rest[0][:, :LANES], rest[1][:, :LANES])))

    gacc[...] = jnp.zeros_like(gacc)
    gmid[...] = jnp.zeros_like(gmid)

    def fold(v):
        return (v[0:8] + v[8:16]) + (v[16:24] + v[24:32])

    def pair_back(t, carry):
        s, w = t // nwin, lax.rem(t, nwin)
        inv, live = prs[t, 0], prs[t, 1]
        mean = pmean[t]
        u, along = [], None
        for h in range(heads):
            d = ds[t, h * WQ : (h + 1) * WQ]
            u.append(d * inv)
            a = d * bias[t, h * WQ : (h + 1) * WQ]
            along = a if along is None else along + a
            gmid[h] += fold(mean * u[h])
        c1 = along * live
        c0 = mean * c1
        for p in range(channels):
            v = pair[s, w, p]
            d = c0 - v * c1
            for h in range(heads):
                d = d + u[h] * centred[p][h]
                gacc[h * channels + p] += fold(v * u[h])
            g_pair[s, w, p] = d
        return carry

    ahead = 3 * windows // 8
    lax.fori_loop(0, ahead, pair_back, 0)

    values_here()
    keys_here()
    for s in range(samples):
        dkv[s, HALO : 2 * HALO] += jnp.where(me == 0, 0.0, dhalo[0, s])
        dkv[s, rows : rows + HALO] += jnp.where(me == seqn - 1, 0.0, dhalo[1, s])

    d_keys_values = split(cat([dkv[s, HALO : HALO + rows] for s in range(samples)], 0))
    d_n1 = d_n1 + beside(d_keys_values, (wqh[:, : 2 * LANES], wql[:, : 2 * LANES]), NT)
    na = na_s[...]
    sc1 = sc1_s[...]
    dsc1 = d_n1 * na * sc1 * (1.0 - sc1)
    d_first1 = split(cat([dsc1, d_n1], 1))
    ns = ns_s[...]
    put(acc_l, ["w_key", "w_value"], tn(n1_split, d_keys_values))
    put(acc_l, ["w_scale1", "w_shift1"], tn(split(ns * p_s_gain1[...]), d_first1))
    if late.size > LATE_ROWS:
        acc_l[LATE_ROWS:] = jnp.zeros((late.size - LATE_ROWS, LANES), F32)
    go_late()

    g_atoms[...] = dfirst_s[...] + norm_back(d_n1 * sc1, na, ra_s[...])
    go_late()
    go_early()
    lax.fori_loop(ahead, windows, pair_back, 0)

    d_cond1 = beside(d_first1, (w1h[...], w1l[...]), NT)
    d_cond2 = beside(split(cat([dsc2_s[...], dn2_s[...]], 1)), (w2h[...], w2l[...]), NT)

    eye = (
        lax.broadcasted_iota(jnp.int32, (channels, LANES), 0) == lax.broadcasted_iota(jnp.int32, (channels, LANES), 1)
    ).astype(F32)
    gsum = jnp.sum(jnp.sum(gacc[...], axis=1), axis=-1, keepdims=True)
    gless = jnp.sum(jnp.sum(gmid[...], axis=1, keepdims=True), axis=-1, keepdims=True)
    rows_g = [column_sum((gsum[h * channels : (h + 1) * channels] - gless[h]) * eye) for h in range(heads)]
    blank = jnp.zeros((1, LANES - channels), F32)
    gain_row = cat([p_pair_gain[...], blank], 1)
    pair_row = jnp.zeros((1, LANES), F32)
    for h in range(heads):
        pair_row = pair_row + rows_g[h] * cat([p_w_pair[h : h + 1, :], blank], 1)
    pair_grad = cat([v * gain_row for v in rows_g] + [jnp.zeros((8 - heads, LANES), F32)], 0)
    small = {
        "b_scale1": column_sum(dsc1),
        "b_query": column_sum(dq),
        "b_scale2": column_sum(dsc2_s[...]),
        "b_zero1": column_sum(dz1_s[...]),
        "b_zero2": column_sum(dz2_s[...]),
        "s_gain1": column_sum(d_cond1 * ns),
        "s_gain2": column_sum(d_cond2 * ns),
        "pair_gain": pair_row,
    }
    acc_s[...] = cat([small[name] for name in VECTORS] + [pair_grad], 0)
    s1 = start([remote(acc_s, recv_sc, s_send.at[0], s_recv.at[0], other)])
    d_ns = d_cond1 * p_s_gain1[...] + d_cond2 * p_s_gain2[...]
    g_single[...] = norm_back(d_ns, ns, rs_s[...]) + nt(
        split(cat([dz1_s[...], dz2_s[...]], 1)), (wzh[...], wzl[...])
    )

    def spread(slots, mine, peers, i):
        slots[mine] = acc_s[...]
        start([remote(acc_s, slots.at[mine], s_send.at[i], s_recv.at[i], device) for device in peers])

        def end():
            some = acc_e.at[0 : 16 * len(peers)]
            remote(some, some, s_send.at[i], s_recv.at[i], other).wait()

        return end

    go_late()
    go_early()
    wait(s1)
    acc_s[...] = acc_s[...] + recv_sc[...]
    s2 = spread(recv_sxy, k, [xy_peer(o)[1] for o in range(nxy - 1, 0, -1)], 1)
    s2()
    acc_s[...] = add_up(recv_sxy, nxy)
    s3 = spread(recv_sz, z, [z_peer(o)[1] for o in range(nz - 1, 0, -1)], 2)
    go_late()
    go_early()
    s3()
    res_s[...] = add_up(recv_sz, nz)
    go_late()
    go_early()
    go_late()
    go_early()


class Plan:
    def __init__(self, needed, nxy, nz, whole):
        half = -(-needed // 2)
        grains = (8 * nxy, 8 * nz) if whole else (8 * nxy * nz,) * 2
        line = int(half * (0.4 if whole else 0.34)) // grains[1] * grains[1]
        plane = -(-(half - line) // grains[0]) * grains[0]
        self.whole, self.size = whole, 2 * (plane + line)
        self.parts = [("plane", 0, plane)] + ([("line", plane, line)] if line else [])

    def landing(self, nxy, nz):
        count = {"plane": (nxy, nz), "line": (nz, nxy)}
        shapes = [(self.size // 2, LANES)]
        for first, _, rows in self.parts:
            n, m = count[first]
            shapes.append((n - 1, rows // n, LANES))
            shapes.append((m, rows // n, LANES) if self.whole else (m - 1, rows // n // m, LANES))
        return shapes

    def steps(self):
        return 5 if self.whole else 6


def unpack_kernel(*refs):
    n, v = len(EARLY) + len(LATE), len(VECTORS) + 1
    ins, refs = refs[:7], refs[7:]
    outs, mats, small, held, sems = refs[:4], refs[4 : 4 + n], refs[4 + n : 4 + n + v], refs[4 + n + v : -1], refs[-1]
    for i, (a, b) in enumerate(zip(ins[3::-1], outs[::-1])):
        pltpu.make_async_copy(a, b, sems.at[i]).start()
    at = 0
    for i, (group, packed) in enumerate(((EARLY, ins[4]), (LATE, ins[5]))):
        for name, _, columns in group:
            base, height = PLACE[name], mats[at].shape[0]
            for b in range(columns):
                pltpu.make_async_copy(
                    packed.at[pl.ds(base + b * height, height)], mats[at].at[:, pl.ds(b * LANES, LANES)], sems.at[4 + i]
                ).start()
            at += 1
    row = 0
    for i, (mid, ref) in enumerate(zip(held, small)):
        mid[...] = ins[6][row : row + mid.shape[0], 0 : mid.shape[1]]
        pltpu.make_async_copy(mid, ref, sems.at[6 + i]).start()
        row += 1
    for i, a in enumerate(ins[3::-1]):
        pltpu.make_async_copy(a, a, sems.at[i]).wait()
    for i, packed in enumerate(ins[4:6]):
        some = packed.at[0 : (EARLY_ROWS, LATE_ROWS)[i]]
        pltpu.make_async_copy(some, some, sems.at[4 + i]).wait()
    for i, mid in enumerate(held):
        pltpu.make_async_copy(mid, mid, sems.at[6 + i]).wait()


def shards(dpn, seqn, atoms, single_cond, pair_block, atom_count, *rest):
    params, cotangent = dict(zip(PARAMS, rest[:-1])), rest[-1]
    params["w_pair"] = params["w_pair"].T
    samples, rows, width = atoms.shape
    nwin, channels = pair_block.shape[1:3]
    heads = params["w_pair"].shape[0]
    flat = samples * rows
    nz, nx = 4, seqn // 8
    nxy = dpn * nx
    early = Plan(EARLY_ROWS, nxy, nz, False)
    late = Plan(LATE_ROWS, nxy, nz, True)
    windows = samples * nwin
    hidden = params["w_down"].shape[0]

    def row(v):
        return v.reshape(1, -1) if v.ndim == 1 else v

    vmem = pl.BlockSpec(memory_space=pltpu.VMEM)
    anyw = pl.BlockSpec(memory_space=pl.ANY)

    def buf(*shape):
        return pltpu.VMEM(shape, F32)

    def low(*shape):
        return [pltpu.VMEM(shape, BF16), pltpu.VMEM(shape, BF16)]

    def sems(n):
        return [pltpu.SemaphoreType.DMA((n,)), pltpu.SemaphoreType.DMA((n,))]

    tall = (flat, width)
    extended = (samples, rows + 2 * HALO, 2 * width)
    scratch = [
        buf(*pair_block.shape),
        buf(windows, heads * WQ, KW),
        buf(windows, WQ, KW),
        buf(windows, 2, WQ, KW),
        buf(windows, heads * WQ, KW),
        buf(windows, heads * WQ, KW),
        buf(*extended),
        buf(*extended),
        buf(2, samples, HALO, 2 * width),
    ]
    scratch += low(*extended)
    scratch += low(width, 2 * width)
    scratch += low(width, 4 * width)
    scratch += low(width, 2 * width)
    scratch += low(width, 2 * width)
    scratch += low(width, 2 * hidden)
    scratch += low(hidden, width)
    scratch += low(width, width)
    scratch += low(*tall) + low(*tall) + low(*tall)
    scratch += [buf(*tall) for _ in range(19)]
    scratch += [
        buf(heads * channels, 8, KW),
        buf(heads, 8, KW),
        buf(early.size, LANES),
        buf(late.size, LANES),
        buf(16, LANES),
        buf(16, LANES),
        buf(nxy, 16, LANES),
        buf(nz, 16, LANES),
        pltpu.SemaphoreType.DMA((samples,)),
    ]
    scratch += sems(6) + sems(early.steps()) + sems(late.steps()) + sems(3)
    scratch += [buf(*shape) for plan in (early, late) for shape in plan.landing(nxy, nz)]
    arrays = [
        atom_count,
        params["pair_gain"],
        params["w_pair"],
        atoms.reshape(tall),
        single_cond.reshape(tall),
        cotangent.reshape(tall),
        *[row(params[name]) for name in PARAMS],
        pair_block,
    ]
    scratch += [pltpu.SMEM(v.shape, v.dtype) for v in arrays[:3]]
    scratch += [buf(*v.shape) for v in arrays[3:-1]]
    scratch += [pltpu.SemaphoreType.DMA((4 + len(arrays) - 1 - 14,))]
    sizes = (samples, rows, dpn, seqn, early, late)
    big = pl.pallas_call(
        functools.partial(block_kernel, sizes),
        out_shape=[buf(*shape) for shape in (tall, tall, tall, pair_block.shape, (early.size, LANES), (late.size, LANES), (16, LANES))],
        in_specs=[anyw] * (7 + len(PARAMS)),
        out_specs=[vmem] * 7,
        scratch_shapes=scratch,
        compiler_params=pltpu.CompilerParams(
            collective_id=0, has_side_effects=True, vmem_limit_bytes=40 * 2**20
        ),
        name="block",
    )(*[pltpu.with_memory_space_constraint(v, pltpu.HBM) for v in arrays])

    names = [name for name, _, _ in EARLY + LATE]
    mats = [jax.ShapeDtypeStruct(params[name].shape, F32) for name in names]
    vecs = [jax.ShapeDtypeStruct((1, params[name].shape[0]), F32) for name in VECTORS]
    big = list(big)
    for i in range(3):
        big[i] = big[i].reshape(1, *tall)
    results = pl.pallas_call(
        unpack_kernel,
        out_shape=[jax.ShapeDtypeStruct(v.shape, F32) for v in big[:4]]
        + mats
        + vecs
        + [jax.ShapeDtypeStruct((heads, channels), F32)],
        in_specs=[vmem] * 7,
        out_specs=[anyw] * (5 + len(mats) + len(vecs)),
        scratch_shapes=[buf(*v.shape) for v in vecs]
        + [buf(heads, channels), pltpu.SemaphoreType.DMA((7 + len(vecs),))],
        compiler_params=pltpu.CompilerParams(vmem_limit_bytes=16 * 2**20),
        name="unpack",
    )(*[pltpu.with_memory_space_constraint(v, pltpu.VMEM) for v in big])
    grads = dict(zip(names, results[4:]))
    for name, value in zip(VECTORS, results[4 + len(mats) :]):
        grads[name] = value.reshape(-1)
    grads["w_pair"] = results[-1].T
    out, g_atoms, g_single, g_pair = results[:4]
    return (
        out.reshape(atoms.shape),
        g_atoms.reshape(atoms.shape),
        g_single.reshape(atoms.shape),
        g_pair.reshape(pair_block.shape),
    ) + tuple(grads[name] for name in PARAMS)


def solution(mesh):
    data = P("dp", "seq", None)
    pairs = P("dp", "seq", None, None, None)
    return jax.shard_map(
        functools.partial(shards, mesh.shape["dp"], mesh.shape["seq"]),
        mesh=mesh,
        in_specs=(data, data, pairs, P("dp")) + (P(),) * len(PARAMS) + (data,),
        out_specs=(data, data, data, pairs) + (P(),) * len(PARAMS),
        check_vma=False,
    )
```

```python
import functools
import math

import jax
import jax.numpy as jnp
from jax import lax
from jax.experimental import pallas as pl
from jax.experimental.pallas import tpu as pltpu
from jax.sharding import PartitionSpec as P

WQ = 32
KW = 128
HALO = 48
LANES = 128
MESH = pl.DeviceIdType.MESH
F32 = jnp.float32

EARLY = (
    ("w_down", 2, 1),
    ("w_hidden_gate", 1, 2),
    ("w_hidden_up", 1, 2),
    ("w_zero2", 1, 1),
    ("w_scale2", 1, 1),
    ("w_shift2", 1, 1),
    ("w_out", 1, 1),
    ("w_zero1", 1, 1),
    ("w_gate", 1, 1),
)
LATE = (
    ("w_query", 1, 1),
    ("w_key", 1, 1),
    ("w_value", 1, 1),
    ("w_scale1", 1, 1),
    ("w_shift1", 1, 1),
)
VECTORS = ("b_scale1", "b_query", "b_scale2", "b_zero1", "b_zero2", "s_gain1", "s_gain2", "pair_gain")
PARAMS = (
    "s_gain1",
    "w_scale1",
    "b_scale1",
    "w_shift1",
    "w_query",
    "b_query",
    "w_key",
    "w_value",
    "w_gate",
    "pair_gain",
    "w_pair",
    "w_out",
    "w_zero1",
    "b_zero1",
    "s_gain2",
    "w_scale2",
    "b_scale2",
    "w_shift2",
    "w_hidden_gate",
    "w_hidden_up",
    "w_down",
    "w_zero2",
    "b_zero2",
)


def offsets():
    place, used = {}, []
    for group in (EARLY, LATE):
        row = 0
        for name, rows, columns in group:
            place[name] = row
            row += rows * columns * LANES
        used.append(row)
    return place, used[0], used[1]


PLACE, EARLY_ROWS, LATE_ROWS = offsets()
BF16 = jnp.bfloat16
NN = (((1,), (0,)), ((), ()))
NT = (((1,), (1,)), ((), ()))
TN = (((0,), (0,)), ((), ()))


def dot(a, b, dims):
    return lax.dot_general(a, b, dims, preferred_element_type=F32)


def cat(parts, axis):
    return jnp.concatenate(parts, axis=axis)


def split(x):
    high = x.astype(BF16)
    return high, (x - high.astype(F32)).astype(BF16)


def product(a, b, dims):
    (ah, al), (bh, bl) = a, b
    (ka,), (kb,) = dims[0]
    return dot(cat([ah, al, ah], ka), cat([bh, bh, bl], kb), dims)


def beside(a, b, dims):
    (ah, al), (bh, bl) = a, b
    free = 1 - dims[0][1][0]
    width = bh.shape[free]
    both = dot(ah, cat([bh, bl], free), dims)
    return both[:, :width] + (both[:, width:] + dot(al, bh, dims))


def nn(a, b):
    return product(a, b, NN)


def nt(a, b):
    return product(a, b, NT)


def tn(a, b):
    return product(a, b, TN)


def mean_lanes(x):
    weight = jnp.full((2 * LANES, LANES), 1.0 / LANES, BF16)
    return dot(cat(split(x), 1), weight, NN)


def norm(x):
    cent = x - mean_lanes(x)
    inv = lax.rsqrt(mean_lanes(cent * cent) + 1e-05)
    return cent * inv, inv


def norm_back(d, xhat, inv):
    return (d - mean_lanes(d) - xhat * mean_lanes(d * xhat)) * inv


def sigmoid(x):
    return 1.0 / (1.0 + jnp.exp(-x))


def column_sum(x):
    return jnp.sum(x, axis=0, keepdims=True)


def block_kernel(sizes, *refs):
    samples, rows, dpn, seqn, early, late = sizes
    nwin = rows // WQ
    windows = samples * nwin
    flat = samples * rows
    nz = 4
    nx = seqn // (2 * nz)
    nxy = dpn * nx
    n_in = 6 + len(PARAMS)
    given, refs = refs[:n_in], refs[n_in:]
    held, refs = refs[-n_in - 1 : -1], refs[:-n_in - 1] + refs[-1:]
    n_e, n_l = 1 + 2 * len(early.parts), 1 + 2 * len(late.parts)
    landing_e, landing_l, refs = refs[-n_e - n_l - 1 : -n_l - 1], refs[-n_l - 1 : -1], refs[: -n_e - n_l - 1] + refs[-1:]
    (
        count,
        gain_s,
        wpair_s,
        atoms,
        single,
        cot,
        p_s_gain1,
        p_w_scale1,
        p_b_scale1,
        p_w_shift1,
        p_w_query,
        p_b_query,
        p_w_key,
        p_w_value,
        p_w_gate,
        p_pair_gain,
        p_w_pair,
        p_w_out,
        p_w_zero1,
        p_b_zero1,
        p_s_gain2,
        p_w_scale2,
        p_b_scale2,
        p_w_shift2,
        p_w_hidden_gate,
        p_w_hidden_up,
        p_w_down,
        p_w_zero2,
        p_b_zero2,
    ) = held
    (
        pair_hbm,
        out,
        g_atoms,
        g_single,
        g_pair,
        res_e,
        res_l,
        res_s,
        pair,
        bias,
        pmean,
        prs,
        prob,
        ds,
        kv,
        dkv,
        dhalo,
        kvh,
        kvl,
        w1h,
        w1l,
        wqh,
        wql,
        wzh,
        wzl,
        w2h,
        w2l,
        whh,
        whl,
        wdh,
        wdl,
        woh,
        wol,
        qh_s,
        ql_s,
        mh_s,
        ml_s,
        th_s,
        tl_s,
        mixed_s,
        ns_s,
        na_s,
        n1_s,
        sc1_s,
        sc2_s,
        sh2_s,
        gate_s,
        z1_s,
        z2_s,
        rs_s,
        ra_s,
        dq_s,
        dfirst_s,
        dz1_s,
        dz2_s,
        dn2_s,
        dsc2_s,
        gpre_s,
        gacc,
        gmid,
        acc_e,
        acc_l,
        acc_s,
        recv_sc,
        recv_sxy,
        recv_sz,
        pair_sem,
        h_send,
        h_recv,
        e_send,
        e_recv,
        l_send,
        l_recv,
        s_send,
        s_recv,
        in_sem,
    ) = refs
    dp = lax.axis_index("dp")
    me = lax.axis_index("seq")
    core = lax.rem(me, 2)
    x = lax.rem(me // 2, nx)
    z = me // (2 * nx)
    k = dp * nx + x
    left = (dp, lax.rem(me + seqn - 1, seqn))
    right = (dp, lax.rem(me + 1, seqn))
    other = (dp, me + 1 - 2 * core)

    def xy_peer(o):
        kk = lax.rem(k + o, nxy)
        return kk, (kk // nx, (z * nx + lax.rem(kk, nx)) * 2 + core)

    def z_peer(o):
        zz = lax.rem(z + o, nz)
        return zz, (dp, (zz * nx + x) * 2 + core)

    norm_weights = (p_w_scale1, p_w_shift1)
    projections = (p_w_key, p_w_value, p_w_query, p_w_gate)
    conditions = (p_w_zero1, p_w_zero2, p_w_scale2, p_w_shift2)
    transition = (p_w_hidden_gate, p_w_hidden_up, p_w_down, p_w_out)
    together = (norm_weights, projections, conditions, transition)
    sem_of = [[i for i, group in enumerate(together) if any(ref is r for r in group)] for ref in held]
    used = len(together)
    for found in sem_of:
        if not found:
            found.append(used)
            used += 1

    def where(ref):
        return [ref is h for h in held].index(True)

    def bring(*which):
        for ref in which:
            i = where(ref)
            pltpu.make_async_copy(given[i], ref, in_sem.at[sem_of[i][0]]).start()

    def ready(*which):
        for ref in which:
            if isinstance(ref, tuple):
                total = sum(r.shape[0] * r.shape[1] for r in ref) // LANES
                some = acc_e.at[0:total]
                pltpu.make_async_copy(some, some, in_sem.at[sem_of[where(ref[0])][0]]).wait()
            else:
                i = where(ref)
                pltpu.make_async_copy(given[i], ref, in_sem.at[sem_of[i][0]]).wait()

    scalars = (count, gain_s, wpair_s)
    bring(single, atoms, p_s_gain1, *norm_weights, p_b_scale1, *projections, p_b_query, *scalars)
    bring(*conditions, p_s_gain2, p_b_scale2, p_b_zero1, p_b_zero2)

    def pair_load(s, w):
        return pltpu.make_async_copy(pair_hbm.at[s, w], pair.at[s, w], pair_sem.at[s])

    for t in range(windows):
        pair_load(t // nwin, t % nwin).start()
    bring(*transition, cot, p_pair_gain, p_w_pair)

    barrier = pltpu.get_barrier_semaphore()
    greeted = [left, right, other]
    greeted += [xy_peer(o)[1] for o in range(1, nxy)]
    greeted += [z_peer(o)[1] for o in range(1, nz)]
    for device in greeted:
        pl.semaphore_signal(barrier, inc=1, device_id=device, device_id_type=MESH)

    def remote(src, dst, send, recv, device):
        return pltpu.make_async_remote_copy(
            src_ref=src, dst_ref=dst, send_sem=send, recv_sem=recv, device_id=device, device_id_type=MESH
        )

    def start(copies):
        for copy in copies:
            copy.start()
        return copies

    def wait(copies):
        for copy in copies:
            copy.wait()

    def span(first, size):
        return pl.ds(pl.multiple_of(first, 8), size)

    def hold(high, low, *weights):
        for c, w in enumerate(weights):
            width = w.shape[1]
            high[:, c * width : (c + 1) * width], low[:, c * width : (c + 1) * width] = split(w[...])

    ready(single, atoms, norm_weights, p_s_gain1, p_b_scale1)
    hold(w1h, w1l, p_w_scale1, p_w_shift1)
    xs, xa = single[...], atoms[...]
    cs, ca = xs - mean_lanes(xs), xa - mean_lanes(xa)
    rs, ra = lax.rsqrt(mean_lanes(cs * cs) + 1e-05), lax.rsqrt(mean_lanes(ca * ca) + 1e-05)
    ns, na = cs * rs, ca * ra
    ns_s[...] = ns
    na_s[...] = na
    rs_s[...] = rs
    ra_s[...] = ra
    first1 = nn(split(ns * p_s_gain1[...]), (w1h[...], w1l[...]))
    sc1 = sigmoid(first1[:, :LANES] + p_b_scale1[...])
    sc1_s[...] = sc1
    n1 = sc1 * na + first1[:, LANES:]
    n1_s[...] = n1
    n1_split = split(n1)
    ready(projections, p_b_query)
    hold(wqh, wql, p_w_key, p_w_value, p_w_query, p_w_gate)
    keys_values = nn(n1_split, (wqh[:, : 2 * LANES], wql[:, : 2 * LANES]))
    for s in range(samples):
        block = keys_values[s * rows : (s + 1) * rows]
        kv[s, HALO : HALO + rows] = block
        kvh[s, HALO : HALO + rows], kvl[s, HALO : HALO + rows] = split(block)

    def swap(leftward, rightward):
        def begin():
            @pl.when(me > 0)
            def _():
                leftward.start()

            @pl.when(me < seqn - 1)
            def _():
                rightward.start()

        def end():
            @pl.when(me > 0)
            def _():
                leftward.wait_send()
                rightward.wait_recv()

            @pl.when(me < seqn - 1)
            def _():
                rightward.wait_send()
                leftward.wait_recv()

        begin()
        return end

    pl.semaphore_wait(barrier, len(greeted))
    halos_here = swap(
        remote(kv.at[:, HALO : 2 * HALO], kv.at[:, HALO + rows : 2 * HALO + rows], h_send.at[1], h_recv.at[1], left),
        remote(kv.at[:, rows : rows + HALO], kv.at[:, 0:HALO], h_send.at[0], h_recv.at[0], right),
    )

    ready(*scalars)
    channels = gain_s.shape[0]
    heads = wpair_s.shape[0]
    wg = [[gain_s[p] * wpair_s[h, p] for h in range(heads)] for p in range(channels)]
    mid = [functools.reduce(lambda a, b: a + b, [wg[p][h] for p in range(channels)]) * (1.0 / channels) for h in range(heads)]
    centred = [[wg[p][h] - mid[h] for h in range(heads)] for p in range(channels)]

    key_lane = lax.broadcasted_iota(jnp.int32, (WQ, KW), 1)
    same = key_lane == lax.broadcasted_iota(jnp.int32, (WQ, KW), 0) + HALO

    def pair_bias(t, carry):
        s, w = divmod(t, nwin) if isinstance(t, int) else (t // nwin, lax.rem(t, nwin))
        first = pair[s, w, 0]
        total, square = first, first * first
        b = [first * centred[0][h] for h in range(heads)]
        for p in range(1, channels):
            v = pair[s, w, p]
            total = total + v
            square = square + v * v
            b = [b[h] + v * centred[p][h] for h in range(heads)]
        mean = total * (1.0 / channels)
        var = square * (1.0 / channels) - mean * mean
        inv = lax.rsqrt(jnp.maximum(var, 0.25))
        pmean[t] = mean
        live = jnp.where(var > 0.25, 1.0, jnp.where(var == 0.25, 0.5, 0.0))
        prs[t, 0] = inv
        prs[t, 1] = inv * inv * live * (1.0 / channels)
        begin = me * rows + w * WQ - HALO
        valid = ((key_lane >= -begin) & (key_lane < count[s] - begin)) | same
        for h in range(heads):
            bias[t, h * WQ : (h + 1) * WQ] = jnp.where(valid, inv * b[h], -1e9)
        return carry

    def pair_sample(s):
        pltpu.make_async_copy(pair_hbm.at[s], pair.at[s], pair_sem.at[s]).wait()
        for t in range(s * nwin, (s + 1) * nwin):
            pair_bias(t, 0)

    ready(conditions, p_s_gain2, p_b_scale2, p_b_zero1, p_b_zero2)
    pair_sample(0)
    hold(wzh, wzl, p_w_zero1, p_w_zero2)
    hold(w2h, w2l, p_w_scale2, p_w_shift2)
    scale = 1.0 / math.sqrt(32)
    query_gate = nn(n1_split, (wqh[:, 2 * LANES :], wql[:, 2 * LANES :]))
    qh_s[...], ql_s[...] = split((query_gate[:, :LANES] + p_b_query[...]) * scale)
    gate_s[...] = sigmoid(query_gate[:, LANES:])
    first2 = nn(split(ns * p_s_gain2[...]), (w2h[...], w2l[...]))
    sc2_s[...] = sigmoid(first2[:, :LANES] + p_b_scale2[...])
    sh2_s[...] = first2[:, LANES:]
    zeros = nn(split(single[...]), (wzh[...], wzl[...]))
    z1_s[...] = sigmoid(zeros[:, :LANES] + p_b_zero1[...])
    z2_s[...] = sigmoid(zeros[:, LANES:] + p_b_zero2[...])

    for s in range(1, samples):
        pair_sample(s)
    ready(transition, cot, p_pair_gain, p_w_pair)
    hold(whh, whl, p_w_hidden_gate, p_w_hidden_up)
    hold(wdh, wdl, p_w_down)
    hold(woh, wol, p_w_out)

    lane = lax.broadcasted_iota(jnp.int32, (heads * WQ, LANES), 1)
    row = lax.broadcasted_iota(jnp.int32, (heads * WQ, LANES), 0)
    own = (lane // 32 == row // WQ).astype(F32)
    own_low = own.astype(BF16)
    ones = jnp.ones((KW, LANES), BF16)
    nothing = jnp.zeros((KW, LANES), BF16)

    def heads_in(ref, at):
        return cat([ref[at, :]] * heads, 0) * own_low

    def heads_out(v):
        v = v * own
        return (v[0:WQ] + v[WQ : 2 * WQ]) + (v[2 * WQ : 3 * WQ] + v[3 * WQ : 4 * WQ])

    def window(t):
        s, w = divmod(t, nwin)
        return s, slice(s * rows + w * WQ, s * rows + (w + 1) * WQ), slice(w * WQ, w * WQ + KW)

    def inner(t):
        w = t % nwin
        return w * WQ >= HALO and w * WQ + KW <= HALO + rows

    middle = [t for t in range(windows) if inner(t)]
    border = [t for t in range(windows) if not inner(t)]

    def attend(ts):
        for t in ts:
            s, at, keys = window(t)
            queries = heads_in(qh_s, at), heads_in(ql_s, at)
            prob[t] = nt(queries, (kvh[s, keys, :LANES], kvl[s, keys, :LANES])) + bias[t]
        for t in ts:
            s, at, keys = window(t)
            scores = prob[t]
            expo = jnp.exp(scores - jnp.max(scores, axis=-1, keepdims=True))
            eh, el = split(expo)
            vh, vl = kvh[s, keys, LANES:], kvl[s, keys, LANES:]
            high = cat([vh, ones], 1)
            both = dot(cat([eh, el, eh], 1), cat([high, high, cat([vl, nothing], 1)], 0), NN)
            inv = 1.0 / both[:, LANES:]
            prob[t] = expo * inv
            mixed_s[at, :] = heads_out(both[:, :LANES] * inv)

    attend(middle)
    halos_here()
    for s in range(samples):
        for absent, at in ((me == 0, slice(0, HALO)), (me == seqn - 1, slice(HALO + rows, 2 * HALO + rows))):
            kvh[s, at], kvl[s, at] = split(jnp.where(absent, 0.0, kv[s, at]))
    attend(border)

    def put(acc, names, value):
        at = 0
        for name in names:
            base = PLACE[name]
            for b in range(dict((n, c) for n, _, c in EARLY + LATE)[name]):
                acc[base + b * value.shape[0] : base + (b + 1) * value.shape[0]] = value[:, at : at + LANES]
                at += LANES

    gated = gate_s[...] * mixed_s[...]
    gated_split = split(gated)
    projected = beside(gated_split, (woh[...], wol[...]), NN)
    z2 = z2_s[...]
    g = cot[...]
    d_down_split = split(g * z2)
    d_hidden = nt(d_down_split, (wdh[...], wdl[...]))
    first = atoms[...] + z1_s[...] * projected
    nf, rf = norm(first)
    sc2 = sc2_s[...]
    n2_split = split(sc2 * nf + sh2_s[...])
    up = nn(n2_split, (whh[...], whl[...]))
    hidden_width = up.shape[1] // 2
    hg, hu = up[:, :hidden_width], up[:, hidden_width:]
    sg = sigmoid(hg)
    silu = hg * sg
    hidden_split = split(silu * hu)
    d_up_split = split(cat([d_hidden * hu * (sg + silu * (1.0 - sg)), d_hidden * silu], 1))

    d_n2 = beside(d_up_split, (whh[...], whl[...]), NT)
    down = beside(hidden_split, (wdh[...], wdl[...]), NN)
    dn2_s[...] = d_n2
    d_first = g + norm_back(d_n2 * sc2, nf, rf)
    dfirst_s[...] = d_first
    put(acc_e, ["w_down"], tn(hidden_split, d_down_split))
    put(acc_e, ["w_hidden_gate", "w_hidden_up"], tn(n2_split, d_up_split))
    z1 = z1_s[...]
    d_proj_split = split(d_first * z1)
    d_gated = beside(d_proj_split, (woh[...], wol[...]), NT)
    dsc2 = d_n2 * nf * sc2 * (1.0 - sc2)
    dsc2_s[...] = dsc2
    cond2_split = split(ns_s[...] * p_s_gain2[...])
    put(acc_e, ["w_scale2", "w_shift2"], tn(cond2_split, split(cat([dsc2, d_n2], 1))))
    out[...] = first + z2 * down
    dz2 = g * down * z2 * (1.0 - z2)
    dz2_s[...] = dz2
    dz1 = d_first * projected * z1 * (1.0 - z1)
    dz1_s[...] = dz1
    gate = gate_s[...]
    mixed = mixed_s[...]
    d_gate = d_gated * mixed * gate * (1.0 - gate)
    gpre_s[...] = d_gate
    d_mixed = d_gated * gate
    mh_s[...], ml_s[...] = split(d_mixed)
    th_s[...], tl_s[...] = split(d_mixed * mixed)
    put(acc_e, ["w_out"], tn(gated_split, d_proj_split))
    put(acc_e, ["w_zero1", "w_zero2"], tn(split(single[...]), split(cat([dz1, dz2], 1))))
    put(acc_e, ["w_gate"], tn(split(n1_s[...]), split(d_gate)))
    if early.size > EARLY_ROWS:
        acc_e[EARLY_ROWS:] = jnp.zeros((early.size - EARLY_ROWS, LANES), F32)

    groups = {"plane": (nxy, k, xy_peer), "line": (nz, z, z_peer)}

    def travelling(plan, acc, res, landing, sems):
        half = plan.size // 2
        base = core * half
        step = [0]

        def send(src, dst, device):
            return remote(src, dst, sems[0].at[step[0]], sems[1].at[step[0]], device)

        def arrived(rows_in):
            some = acc_e.at[0:rows_in]
            remote(some, some, sems[0].at[step[0]], sems[1].at[step[0]], other).wait()
            step[0] += 1

        def gathers(name, where):
            n, _, peer = groups[name]
            return [send(res.at[where], res.at[where], peer(o)[1]) for o in range(1, n)]

        places = []
        for i, (first, rows_at, rows_in) in enumerate(plan.parts):
            second = "line" if first == "plane" else "plane"
            here = base + rows_at
            one = rows_in // groups[first][0]
            two = one // groups[second][0]
            mine = here + groups[first][1] * one
            places.append((first, second, here, one, two, mine, landing[1 + 2 * i], landing[2 + 2 * i]))

        def run():
            copies = start([send(acc.at[span((1 - core) * half, half)], landing[0], other)])
            yield
            arrived(half)
            acc[span(base, half), :] += landing[0][...]
            copies = []
            for first, _, here, one, _, _, land, _ in places:
                n, _, peer = groups[first]
                for o in range(1, n):
                    index, device = peer(o)
                    copies.append(send(acc.at[span(here + index * one, one)], land.at[o - 1], device))
            start(copies)
            yield
            arrived(sum((groups[p[0]][0] - 1) * p[3] for p in places))
            copies = []
            for first, second, _, one, two, mine, land, land2 in places:
                value = acc[span(mine, one), :]
                for o in range(1, groups[first][0]):
                    value = value + land[o - 1]
                acc[span(mine, one), :] = value
                n, own_index, peer = groups[second]
                for o in range(1, n):
                    index, device = peer(o)
                    if plan.whole:
                        copies.append(send(acc.at[span(mine, one)], land2.at[own_index], device))
                    else:
                        copies.append(send(acc.at[span(mine + index * two, two)], land2.at[o - 1], device))
                start(copies)
                copies = []
            if plan.whole:
                for _, second, _, one, _, mine, _, land2 in places:
                    land2[groups[second][1]] = acc[span(mine, one), :]
            yield
            arrived(sum((groups[p[1]][0] - 1) * (p[3] if plan.whole else p[4]) for p in places))
            copies = []
            for first, second, _, one, two, mine, _, land2 in places:
                n, own_index, _ = groups[second]
                if plan.whole:
                    res[span(mine, one), :] = add_up(land2, n)
                    start(gathers(first, span(mine, one)))
                else:
                    at = mine + own_index * two
                    value = acc[span(at, two), :]
                    for o in range(1, n):
                        value = value + land2[o - 1]
                    res[span(at, two), :] = value
                    start(gathers(second, span(at, two)))
            yield
            if not plan.whole:
                arrived(sum((groups[p[1]][0] - 1) * p[4] for p in places))
                copies = []
                for first, _, _, one, _, mine, _, _ in places:
                    copies += gathers(first, span(mine, one))
                start(copies)
                yield
            arrived(sum((groups[p[0]][0] - 1) * p[3] for p in places))
            copies = start([send(res.at[span(base, half)], res.at[span(base, half)], other)])
            yield
            arrived(half)
            yield

        steps = run()
        return lambda: next(steps)

    def add_up(slots, count):
        value = slots[0]
        for i in range(1, count):
            value = value + slots[i]
        return value

    go_early = travelling(early, acc_e, res_e, landing_e, (e_send, e_recv))
    go_late = travelling(late, acc_l, res_l, landing_l, (l_send, l_recv))
    go_early()

    dkv[...] = jnp.zeros_like(dkv)
    less = -jnp.ones((KW, LANES), BF16)

    def back_values(ts):
        for t in ts:
            s, at, keys = window(t)
            dkv[s, keys, LANES:] += tn(split(prob[t]), (heads_in(mh_s, at), heads_in(ml_s, at)))

    def back_keys(ts):
        for t in ts:
            s, at, keys = window(t)
            dkv[s, keys, :LANES] += tn(split(ds[t]), (heads_in(qh_s, at), heads_in(ql_s, at)))

    def swap_back(lanes, i):
        ends = slice(0, HALO), slice(HALO + rows, 2 * HALO + rows)
        return swap(
            remote(dkv.at[:, ends[0], lanes], dhalo.at[1, :, :, lanes], h_send.at[i], h_recv.at[i], left),
            remote(dkv.at[:, ends[1], lanes], dhalo.at[0, :, :, lanes], h_send.at[i + 1], h_recv.at[i + 1], right),
        )

    def back_scores(ts):
        for t in ts:
            s, at, keys = window(t)
            mh, ml = heads_in(mh_s, at), heads_in(ml_s, at)
            th, tl = heads_in(th_s, at), heads_in(tl_s, at)
            vh, vl = kvh[s, keys, LANES:], kvl[s, keys, LANES:]
            ds[t] = prob[t] * dot(cat([mh, ml, mh, th, tl], 1), cat([vh, vh, vl, less, less], 1), NT)

    back_values(border)
    values_here = swap_back(slice(LANES, 2 * LANES), 2)
    back_scores(border)
    back_keys(border)
    keys_here = swap_back(slice(0, LANES), 4)
    back_scores(middle)
    back_keys(middle)
    go_early()

    back_values(middle)
    for t in range(windows):
        s, at, keys = window(t)
        dq_s[at, :] = heads_out(nn(split(ds[t]), (kvh[s, keys, :LANES], kvl[s, keys, :LANES]))) * scale

    dq = dq_s[...]
    rest = split(cat([dq, gpre_s[...]], 1))
    n1_split = split(n1_s[...])
    d_n1 = beside(rest, (wqh[:, 2 * LANES :], wql[:, 2 * LANES :]), NT)
    put(acc_l, ["w_query"], tn(n1_split, (rest[0][:, :LANES], rest[1][:, :LANES])))

    gacc[...] = jnp.zeros_like(gacc)
    gmid[...] = jnp.zeros_like(gmid)

    def fold(v):
        return (v[0:8] + v[8:16]) + (v[16:24] + v[24:32])

    def pair_back(t, carry):
        s, w = t // nwin, lax.rem(t, nwin)
        inv, live = prs[t, 0], prs[t, 1]
        mean = pmean[t]
        u, along = [], None
        for h in range(heads):
            d = ds[t, h * WQ : (h + 1) * WQ]
            u.append(d * inv)
            a = d * bias[t, h * WQ : (h + 1) * WQ]
            along = a if along is None else along + a
            gmid[h] += fold(mean * u[h])
        c1 = along * live
        c0 = mean * c1
        for p in range(channels):
            v = pair[s, w, p]
            d = c0 - v * c1
            for h in range(heads):
                d = d + u[h] * centred[p][h]
                gacc[h * channels + p] += fold(v * u[h])
            g_pair[s, w, p] = d
        return carry

    ahead = 8 * windows // 16
    lax.fori_loop(0, ahead, pair_back, 0)

    values_here()
    keys_here()
    for s in range(samples):
        dkv[s, HALO : 2 * HALO] += jnp.where(me == 0, 0.0, dhalo[0, s])
        dkv[s, rows : rows + HALO] += jnp.where(me == seqn - 1, 0.0, dhalo[1, s])

    d_keys_values = split(cat([dkv[s, HALO : HALO + rows] for s in range(samples)], 0))
    d_n1 = d_n1 + beside(d_keys_values, (wqh[:, : 2 * LANES], wql[:, : 2 * LANES]), NT)
    na = na_s[...]
    sc1 = sc1_s[...]
    dsc1 = d_n1 * na * sc1 * (1.0 - sc1)
    d_first1 = split(cat([dsc1, d_n1], 1))
    ns = ns_s[...]
    put(acc_l, ["w_key", "w_value"], tn(n1_split, d_keys_values))
    put(acc_l, ["w_scale1", "w_shift1"], tn(split(ns * p_s_gain1[...]), d_first1))
    if late.size > LATE_ROWS:
        acc_l[LATE_ROWS:] = jnp.zeros((late.size - LATE_ROWS, LANES), F32)
    go_late()

    g_atoms[...] = dfirst_s[...] + norm_back(d_n1 * sc1, na, ra_s[...])
    go_late()
    go_early()
    lax.fori_loop(ahead, windows, pair_back, 0)

    d_cond1 = beside(d_first1, (w1h[...], w1l[...]), NT)
    d_cond2 = beside(split(cat([dsc2_s[...], dn2_s[...]], 1)), (w2h[...], w2l[...]), NT)

    eye = (
        lax.broadcasted_iota(jnp.int32, (channels, LANES), 0) == lax.broadcasted_iota(jnp.int32, (channels, LANES), 1)
    ).astype(F32)
    gsum = jnp.sum(jnp.sum(gacc[...], axis=1), axis=-1, keepdims=True)
    gless = jnp.sum(jnp.sum(gmid[...], axis=1, keepdims=True), axis=-1, keepdims=True)
    rows_g = [column_sum((gsum[h * channels : (h + 1) * channels] - gless[h]) * eye) for h in range(heads)]
    blank = jnp.zeros((1, LANES - channels), F32)
    gain_row = cat([p_pair_gain[...], blank], 1)
    pair_row = jnp.zeros((1, LANES), F32)
    for h in range(heads):
        pair_row = pair_row + rows_g[h] * cat([p_w_pair[h : h + 1, :], blank], 1)
    pair_grad = cat([v * gain_row for v in rows_g] + [jnp.zeros((8 - heads, LANES), F32)], 0)
    small = {
        "b_scale1": column_sum(dsc1),
        "b_query": column_sum(dq),
        "b_scale2": column_sum(dsc2_s[...]),
        "b_zero1": column_sum(dz1_s[...]),
        "b_zero2": column_sum(dz2_s[...]),
        "s_gain1": column_sum(d_cond1 * ns),
        "s_gain2": column_sum(d_cond2 * ns),
        "pair_gain": pair_row,
    }
    acc_s[...] = cat([small[name] for name in VECTORS] + [pair_grad], 0)
    s1 = start([remote(acc_s, recv_sc, s_send.at[0], s_recv.at[0], other)])
    d_ns = d_cond1 * p_s_gain1[...] + d_cond2 * p_s_gain2[...]
    g_single[...] = norm_back(d_ns, ns, rs_s[...]) + nt(
        split(cat([dz1_s[...], dz2_s[...]], 1)), (wzh[...], wzl[...])
    )

    def spread(slots, mine, peers, i):
        slots[mine] = acc_s[...]
        start([remote(acc_s, slots.at[mine], s_send.at[i], s_recv.at[i], device) for device in peers])

        def end():
            some = acc_e.at[0 : 16 * len(peers)]
            remote(some, some, s_send.at[i], s_recv.at[i], other).wait()

        return end

    go_late()
    go_early()
    wait(s1)
    acc_s[...] = acc_s[...] + recv_sc[...]
    s2 = spread(recv_sxy, k, [xy_peer(o)[1] for o in range(1, nxy)], 1)
    s2()
    acc_s[...] = add_up(recv_sxy, nxy)
    s3 = spread(recv_sz, z, [z_peer(o)[1] for o in range(1, nz)], 2)
    go_late()
    go_early()
    s3()
    res_s[...] = add_up(recv_sz, nz)
    go_late()
    go_early()
    go_late()
    go_early()


class Plan:
    def __init__(self, needed, nxy, nz, whole):
        half = -(-needed // 2)
        grains = (8 * nxy, 8 * nz) if whole else (8 * nxy * nz,) * 2
        line = int(half * (0.4 if whole else 0.34)) // grains[1] * grains[1]
        plane = -(-(half - line) // grains[0]) * grains[0]
        self.whole, self.size = whole, 2 * (plane + line)
        self.parts = [("plane", 0, plane)] + ([("line", plane, line)] if line else [])

    def landing(self, nxy, nz):
        count = {"plane": (nxy, nz), "line": (nz, nxy)}
        shapes = [(self.size // 2, LANES)]
        for first, _, rows in self.parts:
            n, m = count[first]
            shapes.append((n - 1, rows // n, LANES))
            shapes.append((m, rows // n, LANES) if self.whole else (m - 1, rows // n // m, LANES))
        return shapes

    def steps(self):
        return 5 if self.whole else 6


def unpack_kernel(*refs):
    n, v = len(EARLY) + len(LATE), len(VECTORS) + 1
    ins, refs = refs[:7], refs[7:]
    outs, mats, small, held, sems = refs[:4], refs[4 : 4 + n], refs[4 + n : 4 + n + v], refs[4 + n + v : -1], refs[-1]
    for i, (a, b) in enumerate(zip(ins[3::-1], outs[::-1])):
        pltpu.make_async_copy(a, b, sems.at[i]).start()
    at = 0
    for i, (group, packed) in enumerate(((EARLY, ins[4]), (LATE, ins[5]))):
        for name, _, columns in group:
            base, height = PLACE[name], mats[at].shape[0]
            for b in range(columns):
                pltpu.make_async_copy(
                    packed.at[pl.ds(base + b * height, height)], mats[at].at[:, pl.ds(b * LANES, LANES)], sems.at[4 + i]
                ).start()
            at += 1
    row = 0
    for i, (mid, ref) in enumerate(zip(held, small)):
        mid[...] = ins[6][row : row + mid.shape[0], 0 : mid.shape[1]]
        pltpu.make_async_copy(mid, ref, sems.at[6 + i]).start()
        row += 1
    for i, a in enumerate(ins[3::-1]):
        pltpu.make_async_copy(a, a, sems.at[i]).wait()
    for i, packed in enumerate(ins[4:6]):
        some = packed.at[0 : (EARLY_ROWS, LATE_ROWS)[i]]
        pltpu.make_async_copy(some, some, sems.at[4 + i]).wait()
    for i, mid in enumerate(held):
        pltpu.make_async_copy(mid, mid, sems.at[6 + i]).wait()


def shards(dpn, seqn, atoms, single_cond, pair_block, atom_count, *rest):
    params, cotangent = dict(zip(PARAMS, rest[:-1])), rest[-1]
    params["w_pair"] = params["w_pair"].T
    samples, rows, width = atoms.shape
    nwin, channels = pair_block.shape[1:3]
    heads = params["w_pair"].shape[0]
    flat = samples * rows
    nz, nx = 4, seqn // 8
    nxy = dpn * nx
    early = Plan(EARLY_ROWS, nxy, nz, False)
    late = Plan(LATE_ROWS, nxy, nz, True)
    windows = samples * nwin
    hidden = params["w_down"].shape[0]

    def row(v):
        return v.reshape(1, -1) if v.ndim == 1 else v

    vmem = pl.BlockSpec(memory_space=pltpu.VMEM)
    anyw = pl.BlockSpec(memory_space=pl.ANY)

    def buf(*shape):
        return pltpu.VMEM(shape, F32)

    def low(*shape):
        return [pltpu.VMEM(shape, BF16), pltpu.VMEM(shape, BF16)]

    def sems(n):
        return [pltpu.SemaphoreType.DMA((n,)), pltpu.SemaphoreType.DMA((n,))]

    tall = (flat, width)
    extended = (samples, rows + 2 * HALO, 2 * width)
    scratch = [
        buf(*pair_block.shape),
        buf(windows, heads * WQ, KW),
        buf(windows, WQ, KW),
        buf(windows, 2, WQ, KW),
        buf(windows, heads * WQ, KW),
        buf(windows, heads * WQ, KW),
        buf(*extended),
        buf(*extended),
        buf(2, samples, HALO, 2 * width),
    ]
    scratch += low(*extended)
    scratch += low(width, 2 * width)
    scratch += low(width, 4 * width)
    scratch += low(width, 2 * width)
    scratch += low(width, 2 * width)
    scratch += low(width, 2 * hidden)
    scratch += low(hidden, width)
    scratch += low(width, width)
    scratch += low(*tall) + low(*tall) + low(*tall)
    scratch += [buf(*tall) for _ in range(19)]
    scratch += [
        buf(heads * channels, 8, KW),
        buf(heads, 8, KW),
        buf(early.size, LANES),
        buf(late.size, LANES),
        buf(16, LANES),
        buf(16, LANES),
        buf(nxy, 16, LANES),
        buf(nz, 16, LANES),
        pltpu.SemaphoreType.DMA((samples,)),
    ]
    scratch += sems(6) + sems(early.steps()) + sems(late.steps()) + sems(3)
    scratch += [buf(*shape) for plan in (early, late) for shape in plan.landing(nxy, nz)]
    arrays = [
        atom_count,
        params["pair_gain"],
        params["w_pair"],
        atoms.reshape(tall),
        single_cond.reshape(tall),
        cotangent.reshape(tall),
        *[row(params[name]) for name in PARAMS],
        pair_block,
    ]
    scratch += [pltpu.SMEM(v.shape, v.dtype) for v in arrays[:3]]
    scratch += [buf(*v.shape) for v in arrays[3:-1]]
    scratch += [pltpu.SemaphoreType.DMA((4 + len(arrays) - 1 - 14,))]
    sizes = (samples, rows, dpn, seqn, early, late)
    big = pl.pallas_call(
        functools.partial(block_kernel, sizes),
        out_shape=[buf(*shape) for shape in (tall, tall, tall, pair_block.shape, (early.size, LANES), (late.size, LANES), (16, LANES))],
        in_specs=[anyw] * (7 + len(PARAMS)),
        out_specs=[vmem] * 7,
        scratch_shapes=scratch,
        compiler_params=pltpu.CompilerParams(
            collective_id=0, has_side_effects=True, vmem_limit_bytes=40 * 2**20
        ),
        name="block",
    )(*[pltpu.with_memory_space_constraint(v, pltpu.HBM) for v in arrays])

    names = [name for name, _, _ in EARLY + LATE]
    mats = [jax.ShapeDtypeStruct(params[name].shape, F32) for name in names]
    vecs = [jax.ShapeDtypeStruct((1, params[name].shape[0]), F32) for name in VECTORS]
    big = list(big)
    for i in range(3):
        big[i] = big[i].reshape(1, *tall)
    results = pl.pallas_call(
        unpack_kernel,
        out_shape=[jax.ShapeDtypeStruct(v.shape, F32) for v in big[:4]]
        + mats
        + vecs
        + [jax.ShapeDtypeStruct((heads, channels), F32)],
        in_specs=[vmem] * 7,
        out_specs=[anyw] * (5 + len(mats) + len(vecs)),
        scratch_shapes=[buf(*v.shape) for v in vecs]
        + [buf(heads, channels), pltpu.SemaphoreType.DMA((7 + len(vecs),))],
        compiler_params=pltpu.CompilerParams(vmem_limit_bytes=16 * 2**20),
        name="unpack",
    )(*[pltpu.with_memory_space_constraint(v, pltpu.VMEM) for v in big])
    grads = dict(zip(names, results[4:]))
    for name, value in zip(VECTORS, results[4 + len(mats) :]):
        grads[name] = value.reshape(-1)
    grads["w_pair"] = results[-1].T
    out, g_atoms, g_single, g_pair = results[:4]
    return (
        out.reshape(atoms.shape),
        g_atoms.reshape(atoms.shape),
        g_single.reshape(atoms.shape),
        g_pair.reshape(pair_block.shape),
    ) + tuple(grads[name] for name in PARAMS)


def solution(mesh):
    data = P("dp", "seq", None)
    pairs = P("dp", "seq", None, None, None)
    return jax.shard_map(
        functools.partial(shards, mesh.shape["dp"], mesh.shape["seq"]),
        mesh=mesh,
        in_specs=(data, data, pairs, P("dp")) + (P(),) * len(PARAMS) + (data,),
        out_specs=(data, data, data, pairs) + (P(),) * len(PARAMS),
        check_vma=False,
    )
```

```python
import functools
import math

import jax
import jax.numpy as jnp
from jax import lax
from jax.experimental import pallas as pl
from jax.experimental.pallas import tpu as pltpu
from jax.sharding import PartitionSpec as P

WQ = 32
KW = 128
HALO = 48
LANES = 128
MESH = pl.DeviceIdType.MESH
F32 = jnp.float32

EARLY = (
    ("w_down", 2, 1),
    ("w_hidden_gate", 1, 2),
    ("w_hidden_up", 1, 2),
    ("w_zero2", 1, 1),
    ("w_scale2", 1, 1),
    ("w_shift2", 1, 1),
    ("w_out", 1, 1),
    ("w_zero1", 1, 1),
    ("w_gate", 1, 1),
)
LATE = (
    ("w_query", 1, 1),
    ("w_key", 1, 1),
    ("w_value", 1, 1),
    ("w_scale1", 1, 1),
    ("w_shift1", 1, 1),
)
VECTORS = ("b_scale1", "b_query", "b_scale2", "b_zero1", "b_zero2", "s_gain1", "s_gain2", "pair_gain")
PARAMS = (
    "s_gain1",
    "w_scale1",
    "b_scale1",
    "w_shift1",
    "w_query",
    "b_query",
    "w_key",
    "w_value",
    "w_gate",
    "pair_gain",
    "w_pair",
    "w_out",
    "w_zero1",
    "b_zero1",
    "s_gain2",
    "w_scale2",
    "b_scale2",
    "w_shift2",
    "w_hidden_gate",
    "w_hidden_up",
    "w_down",
    "w_zero2",
    "b_zero2",
)


def offsets():
    place, used = {}, []
    for group in (EARLY, LATE):
        row = 0
        for name, rows, columns in group:
            place[name] = row
            row += rows * columns * LANES
        used.append(row)
    return place, used[0], used[1]


PLACE, EARLY_ROWS, LATE_ROWS = offsets()
BF16 = jnp.bfloat16
NN = (((1,), (0,)), ((), ()))
NT = (((1,), (1,)), ((), ()))
TN = (((0,), (0,)), ((), ()))


def dot(a, b, dims):
    return lax.dot_general(a, b, dims, preferred_element_type=F32)


def cat(parts, axis):
    return jnp.concatenate(parts, axis=axis)


def split(x):
    high = x.astype(BF16)
    return high, (x - high.astype(F32)).astype(BF16)


def product(a, b, dims):
    (ah, al), (bh, bl) = a, b
    (ka,), (kb,) = dims[0]
    return dot(cat([ah, al, ah], ka), cat([bh, bh, bl], kb), dims)


def beside(a, b, dims):
    (ah, al), (bh, bl) = a, b
    free = 1 - dims[0][1][0]
    width = bh.shape[free]
    both = dot(ah, cat([bh, bl], free), dims)
    return both[:, :width] + (both[:, width:] + dot(al, bh, dims))


def nn(a, b):
    return product(a, b, NN)


def nt(a, b):
    return product(a, b, NT)


def tn(a, b):
    return product(a, b, TN)


def mean_lanes(x):
    weight = jnp.full((2 * LANES, LANES), 1.0 / LANES, BF16)
    return dot(cat(split(x), 1), weight, NN)


def norm(x):
    cent = x - mean_lanes(x)
    inv = lax.rsqrt(mean_lanes(cent * cent) + 1e-05)
    return cent * inv, inv


def norm_back(d, xhat, inv):
    return (d - mean_lanes(d) - xhat * mean_lanes(d * xhat)) * inv


def sigmoid(x):
    return 1.0 / (1.0 + jnp.exp(-x))


def column_sum(x):
    return jnp.sum(x, axis=0, keepdims=True)


def block_kernel(sizes, *refs):
    samples, rows, dpn, seqn, early, late = sizes
    nwin = rows // WQ
    windows = samples * nwin
    flat = samples * rows
    nz = 4
    nx = seqn // (2 * nz)
    nxy = dpn * nx
    n_in = 6 + len(PARAMS)
    given, refs = refs[:n_in], refs[n_in:]
    held, refs = refs[-n_in - 1 : -1], refs[:-n_in - 1] + refs[-1:]
    n_e, n_l = 1 + 2 * len(early.parts), 1 + 2 * len(late.parts)
    landing_e, landing_l, refs = refs[-n_e - n_l - 1 : -n_l - 1], refs[-n_l - 1 : -1], refs[: -n_e - n_l - 1] + refs[-1:]
    (
        count,
        gain_s,
        wpair_s,
        atoms,
        single,
        cot,
        p_s_gain1,
        p_w_scale1,
        p_b_scale1,
        p_w_shift1,
        p_w_query,
        p_b_query,
        p_w_key,
        p_w_value,
        p_w_gate,
        p_pair_gain,
        p_w_pair,
        p_w_out,
        p_w_zero1,
        p_b_zero1,
        p_s_gain2,
        p_w_scale2,
        p_b_scale2,
        p_w_shift2,
        p_w_hidden_gate,
        p_w_hidden_up,
        p_w_down,
        p_w_zero2,
        p_b_zero2,
    ) = held
    (
        pair_hbm,
        out,
        g_atoms,
        g_single,
        g_pair,
        res_e,
        res_l,
        res_s,
        pair,
        bias,
        pmean,
        prs,
        prob,
        ds,
        kv,
        dkv,
        dhalo,
        kvh,
        kvl,
        w1h,
        w1l,
        wqh,
        wql,
        wzh,
        wzl,
        w2h,
        w2l,
        whh,
        whl,
        wdh,
        wdl,
        woh,
        wol,
        qh_s,
        ql_s,
        mh_s,
        ml_s,
        th_s,
        tl_s,
        mixed_s,
        ns_s,
        na_s,
        n1_s,
        sc1_s,
        sc2_s,
        sh2_s,
        gate_s,
        z1_s,
        z2_s,
        rs_s,
        ra_s,
        dq_s,
        dfirst_s,
        dz1_s,
        dz2_s,
        dn2_s,
        dsc2_s,
        gpre_s,
        gacc,
        gmid,
        acc_e,
        acc_l,
        acc_s,
        recv_sc,
        recv_sxy,
        recv_sz,
        pair_sem,
        h_send,
        h_recv,
        e_send,
        e_recv,
        l_send,
        l_recv,
        s_send,
        s_recv,
        in_sem,
    ) = refs
    dp = lax.axis_index("dp")
    me = lax.axis_index("seq")
    core = lax.rem(me, 2)
    x = lax.rem(me // 2, nx)
    z = me // (2 * nx)
    k = dp * nx + x
    left = (dp, lax.rem(me + seqn - 1, seqn))
    right = (dp, lax.rem(me + 1, seqn))
    other = (dp, me + 1 - 2 * core)

    def xy_peer(o):
        kk = lax.rem(k + o, nxy)
        return kk, (kk // nx, (z * nx + lax.rem(kk, nx)) * 2 + core)

    def z_peer(o):
        zz = lax.rem(z + o, nz)
        return zz, (dp, (zz * nx + x) * 2 + core)

    norm_weights = (p_w_scale1, p_w_shift1)
    projections = (p_w_key, p_w_value, p_w_query, p_w_gate)
    conditions = (p_w_zero1, p_w_zero2, p_w_scale2, p_w_shift2)
    transition = (p_w_hidden_gate, p_w_hidden_up, p_w_down, p_w_out)
    together = (norm_weights, projections, conditions, transition)
    sem_of = [[i for i, group in enumerate(together) if any(ref is r for r in group)] for ref in held]
    used = len(together)
    for found in sem_of:
        if not found:
            found.append(used)
            used += 1

    def where(ref):
        return [ref is h for h in held].index(True)

    def bring(*which):
        for ref in which:
            i = where(ref)
            pltpu.make_async_copy(given[i], ref, in_sem.at[sem_of[i][0]]).start()

    def ready(*which):
        for ref in which:
            if isinstance(ref, tuple):
                total = sum(r.shape[0] * r.shape[1] for r in ref) // LANES
                some = acc_e.at[0:total]
                pltpu.make_async_copy(some, some, in_sem.at[sem_of[where(ref[0])][0]]).wait()
            else:
                i = where(ref)
                pltpu.make_async_copy(given[i], ref, in_sem.at[sem_of[i][0]]).wait()

    scalars = (count, gain_s, wpair_s)
    bring(single, atoms, p_s_gain1, *norm_weights, p_b_scale1, *projections, p_b_query, *scalars)
    bring(*conditions, p_s_gain2, p_b_scale2, p_b_zero1, p_b_zero2)

    def pair_load(s, w):
        return pltpu.make_async_copy(pair_hbm.at[s, w], pair.at[s, w], pair_sem.at[s])

    for t in range(windows):
        pair_load(t // nwin, t % nwin).start()
    bring(*transition, cot, p_pair_gain, p_w_pair)

    barrier = pltpu.get_barrier_semaphore()
    greeted = [left, right, other]
    greeted += [xy_peer(o)[1] for o in range(1, nxy)]
    greeted += [z_peer(o)[1] for o in range(1, nz)]
    for device in greeted:
        pl.semaphore_signal(barrier, inc=1, device_id=device, device_id_type=MESH)

    def remote(src, dst, send, recv, device):
        return pltpu.make_async_remote_copy(
            src_ref=src, dst_ref=dst, send_sem=send, recv_sem=recv, device_id=device, device_id_type=MESH
        )

    def start(copies):
        for copy in copies:
            copy.start()
        return copies

    def wait(copies):
        for copy in copies:
            copy.wait()

    def span(first, size):
        return pl.ds(pl.multiple_of(first, 8), size)

    def hold(high, low, *weights):
        for c, w in enumerate(weights):
            width = w.shape[1]
            high[:, c * width : (c + 1) * width], low[:, c * width : (c + 1) * width] = split(w[...])

    ready(single, atoms, norm_weights, p_s_gain1, p_b_scale1)
    hold(w1h, w1l, p_w_scale1, p_w_shift1)
    xs, xa = single[...], atoms[...]
    cs, ca = xs - mean_lanes(xs), xa - mean_lanes(xa)
    rs, ra = lax.rsqrt(mean_lanes(cs * cs) + 1e-05), lax.rsqrt(mean_lanes(ca * ca) + 1e-05)
    ns, na = cs * rs, ca * ra
    ns_s[...] = ns
    na_s[...] = na
    rs_s[...] = rs
    ra_s[...] = ra
    first1 = nn(split(ns * p_s_gain1[...]), (w1h[...], w1l[...]))
    sc1 = sigmoid(first1[:, :LANES] + p_b_scale1[...])
    sc1_s[...] = sc1
    n1 = sc1 * na + first1[:, LANES:]
    n1_s[...] = n1
    n1_split = split(n1)
    ready(projections, p_b_query)
    hold(wqh, wql, p_w_key, p_w_value, p_w_query, p_w_gate)
    keys_values = nn(n1_split, (wqh[:, : 2 * LANES], wql[:, : 2 * LANES]))
    for s in range(samples):
        block = keys_values[s * rows : (s + 1) * rows]
        kv[s, HALO : HALO + rows] = block
        kvh[s, HALO : HALO + rows], kvl[s, HALO : HALO + rows] = split(block)

    def swap(leftward, rightward):
        def begin():
            @pl.when(me > 0)
            def _():
                leftward.start()

            @pl.when(me < seqn - 1)
            def _():
                rightward.start()

        def end():
            @pl.when(me > 0)
            def _():
                leftward.wait_send()
                rightward.wait_recv()

            @pl.when(me < seqn - 1)
            def _():
                rightward.wait_send()
                leftward.wait_recv()

        begin()
        return end

    pl.semaphore_wait(barrier, len(greeted))
    halos_here = swap(
        remote(kv.at[:, HALO : 2 * HALO], kv.at[:, HALO + rows : 2 * HALO + rows], h_send.at[1], h_recv.at[1], left),
        remote(kv.at[:, rows : rows + HALO], kv.at[:, 0:HALO], h_send.at[0], h_recv.at[0], right),
    )

    ready(*scalars)
    channels = gain_s.shape[0]
    heads = wpair_s.shape[0]
    wg = [[gain_s[p] * wpair_s[h, p] for h in range(heads)] for p in range(channels)]
    mid = [functools.reduce(lambda a, b: a + b, [wg[p][h] for p in range(channels)]) * (1.0 / channels) for h in range(heads)]
    centred = [[wg[p][h] - mid[h] for h in range(heads)] for p in range(channels)]

    key_lane = lax.broadcasted_iota(jnp.int32, (WQ, KW), 1)
    same = key_lane == lax.broadcasted_iota(jnp.int32, (WQ, KW), 0) + HALO

    def pair_bias(t, carry):
        s, w = divmod(t, nwin) if isinstance(t, int) else (t // nwin, lax.rem(t, nwin))
        total = pair[s, w, 0]
        for p in range(1, channels):
            total = total + pair[s, w, p]
        mean = total * (1.0 / channels)
        square, b = None, None
        for p in range(channels):
            v = pair[s, w, p] - mean
            terms = [v * centred[p][h] for h in range(heads)]
            square = v * v if p == 0 else square + v * v
            b = terms if p == 0 else [b[h] + terms[h] for h in range(heads)]
        var = square * (1.0 / channels)
        inv = lax.rsqrt(jnp.maximum(var, 0.25))
        pmean[t] = mean
        live = jnp.where(var > 0.25, 1.0, jnp.where(var == 0.25, 0.5, 0.0))
        prs[t, 0] = inv
        prs[t, 1] = inv * inv * live * (1.0 / channels)
        begin = me * rows + w * WQ - HALO
        valid = ((key_lane >= -begin) & (key_lane < count[s] - begin)) | same
        for h in range(heads):
            bias[t, h * WQ : (h + 1) * WQ] = jnp.where(valid, inv * b[h], -1e9)
        return carry

    def pair_sample(s):
        pltpu.make_async_copy(pair_hbm.at[s], pair.at[s], pair_sem.at[s]).wait()
        for t in range(s * nwin, (s + 1) * nwin):
            pair_bias(t, 0)

    ready(conditions, p_s_gain2, p_b_scale2, p_b_zero1, p_b_zero2)
    pair_sample(0)
    hold(wzh, wzl, p_w_zero1, p_w_zero2)
    hold(w2h, w2l, p_w_scale2, p_w_shift2)
    scale = 1.0 / math.sqrt(32)
    query_gate = nn(n1_split, (wqh[:, 2 * LANES :], wql[:, 2 * LANES :]))
    qh_s[...], ql_s[...] = split((query_gate[:, :LANES] + p_b_query[...]) * scale)
    gate_s[...] = sigmoid(query_gate[:, LANES:])
    first2 = nn(split(ns * p_s_gain2[...]), (w2h[...], w2l[...]))
    sc2_s[...] = sigmoid(first2[:, :LANES] + p_b_scale2[...])
    sh2_s[...] = first2[:, LANES:]
    zeros = nn(split(single[...]), (wzh[...], wzl[...]))
    z1_s[...] = sigmoid(zeros[:, :LANES] + p_b_zero1[...])
    z2_s[...] = sigmoid(zeros[:, LANES:] + p_b_zero2[...])

    for s in range(1, samples):
        pair_sample(s)
    ready(transition, cot, p_pair_gain, p_w_pair)
    hold(whh, whl, p_w_hidden_gate, p_w_hidden_up)
    hold(wdh, wdl, p_w_down)
    hold(woh, wol, p_w_out)

    lane = lax.broadcasted_iota(jnp.int32, (heads * WQ, LANES), 1)
    row = lax.broadcasted_iota(jnp.int32, (heads * WQ, LANES), 0)
    own = (lane // 32 == row // WQ).astype(F32)
    own_low = own.astype(BF16)
    ones = jnp.ones((KW, LANES), BF16)
    nothing = jnp.zeros((KW, LANES), BF16)

    def heads_in(ref, at):
        return cat([ref[at, :]] * heads, 0) * own_low

    def heads_out(v):
        v = v * own
        return (v[0:WQ] + v[WQ : 2 * WQ]) + (v[2 * WQ : 3 * WQ] + v[3 * WQ : 4 * WQ])

    def window(t):
        s, w = divmod(t, nwin)
        return s, slice(s * rows + w * WQ, s * rows + (w + 1) * WQ), slice(w * WQ, w * WQ + KW)

    def inner(t):
        w = t % nwin
        return w * WQ >= HALO and w * WQ + KW <= HALO + rows

    middle = [t for t in range(windows) if inner(t)]
    border = [t for t in range(windows) if not inner(t)]

    def attend(ts):
        for t in ts:
            s, at, keys = window(t)
            queries = heads_in(qh_s, at), heads_in(ql_s, at)
            prob[t] = nt(queries, (kvh[s, keys, :LANES], kvl[s, keys, :LANES])) + bias[t]
        for t in ts:
            s, at, keys = window(t)
            scores = prob[t]
            expo = jnp.exp(scores - jnp.max(scores, axis=-1, keepdims=True))
            eh, el = split(expo)
            vh, vl = kvh[s, keys, LANES:], kvl[s, keys, LANES:]
            high = cat([vh, ones], 1)
            both = dot(cat([eh, el, eh], 1), cat([high, high, cat([vl, nothing], 1)], 0), NN)
            inv = 1.0 / both[:, LANES:]
            prob[t] = expo * inv
            mixed_s[at, :] = heads_out(both[:, :LANES] * inv)

    attend(middle)
    halos_here()
    for s in range(samples):
        for absent, at in ((me == 0, slice(0, HALO)), (me == seqn - 1, slice(HALO + rows, 2 * HALO + rows))):
            kvh[s, at], kvl[s, at] = split(jnp.where(absent, 0.0, kv[s, at]))
    attend(border)

    def put(acc, names, value):
        at = 0
        for name in names:
            base = PLACE[name]
            for b in range(dict((n, c) for n, _, c in EARLY + LATE)[name]):
                acc[base + b * value.shape[0] : base + (b + 1) * value.shape[0]] = value[:, at : at + LANES]
                at += LANES

    gated = gate_s[...] * mixed_s[...]
    gated_split = split(gated)
    projected = beside(gated_split, (woh[...], wol[...]), NN)
    z2 = z2_s[...]
    g = cot[...]
    d_down_split = split(g * z2)
    d_hidden = nt(d_down_split, (wdh[...], wdl[...]))
    first = atoms[...] + z1_s[...] * projected
    nf, rf = norm(first)
    sc2 = sc2_s[...]
    n2_split = split(sc2 * nf + sh2_s[...])
    up = nn(n2_split, (whh[...], whl[...]))
    hidden_width = up.shape[1] // 2
    hg, hu = up[:, :hidden_width], up[:, hidden_width:]
    sg = sigmoid(hg)
    silu = hg * sg
    hidden_split = split(silu * hu)
    d_up_split = split(cat([d_hidden * hu * (sg + silu * (1.0 - sg)), d_hidden * silu], 1))

    d_n2 = beside(d_up_split, (whh[...], whl[...]), NT)
    down = beside(hidden_split, (wdh[...], wdl[...]), NN)
    dn2_s[...] = d_n2
    d_first = g + norm_back(d_n2 * sc2, nf, rf)
    dfirst_s[...] = d_first
    put(acc_e, ["w_down"], tn(hidden_split, d_down_split))
    put(acc_e, ["w_hidden_gate", "w_hidden_up"], tn(n2_split, d_up_split))
    z1 = z1_s[...]
    d_proj_split = split(d_first * z1)
    d_gated = beside(d_proj_split, (woh[...], wol[...]), NT)
    dsc2 = d_n2 * nf * sc2 * (1.0 - sc2)
    dsc2_s[...] = dsc2
    cond2_split = split(ns_s[...] * p_s_gain2[...])
    put(acc_e, ["w_scale2", "w_shift2"], tn(cond2_split, split(cat([dsc2, d_n2], 1))))
    out[...] = first + z2 * down
    dz2 = g * down * z2 * (1.0 - z2)
    dz2_s[...] = dz2
    dz1 = d_first * projected * z1 * (1.0 - z1)
    dz1_s[...] = dz1
    gate = gate_s[...]
    mixed = mixed_s[...]
    d_gate = d_gated * mixed * gate * (1.0 - gate)
    gpre_s[...] = d_gate
    d_mixed = d_gated * gate
    mh_s[...], ml_s[...] = split(d_mixed)
    th_s[...], tl_s[...] = split(d_mixed * mixed)
    put(acc_e, ["w_out"], tn(gated_split, d_proj_split))
    put(acc_e, ["w_zero1", "w_zero2"], tn(split(single[...]), split(cat([dz1, dz2], 1))))
    put(acc_e, ["w_gate"], tn(split(n1_s[...]), split(d_gate)))
    if early.size > EARLY_ROWS:
        acc_e[EARLY_ROWS:] = jnp.zeros((early.size - EARLY_ROWS, LANES), F32)

    groups = {"plane": (nxy, k, xy_peer), "line": (nz, z, z_peer)}

    def travelling(plan, acc, res, landing, sems):
        half = plan.size // 2
        base = core * half
        step = [0]

        def send(src, dst, device):
            return remote(src, dst, sems[0].at[step[0]], sems[1].at[step[0]], device)

        def arrived(rows_in):
            some = acc_e.at[0:rows_in]
            remote(some, some, sems[0].at[step[0]], sems[1].at[step[0]], other).wait()
            step[0] += 1

        def gathers(name, where):
            n, _, peer = groups[name]
            return [send(res.at[where], res.at[where], peer(o)[1]) for o in range(1, n)]

        places = []
        for i, (first, rows_at, rows_in) in enumerate(plan.parts):
            second = "line" if first == "plane" else "plane"
            here = base + rows_at
            one = rows_in // groups[first][0]
            two = one // groups[second][0]
            mine = here + groups[first][1] * one
            places.append((first, second, here, one, two, mine, landing[1 + 2 * i], landing[2 + 2 * i]))

        def run():
            copies = start([send(acc.at[span((1 - core) * half, half)], landing[0], other)])
            yield
            arrived(half)
            acc[span(base, half), :] += landing[0][...]
            copies = []
            for first, _, here, one, _, _, land, _ in places:
                n, _, peer = groups[first]
                for o in range(1, n):
                    index, device = peer(o)
                    copies.append(send(acc.at[span(here + index * one, one)], land.at[o - 1], device))
            start(copies)
            yield
            arrived(sum((groups[p[0]][0] - 1) * p[3] for p in places))
            copies = []
            for first, second, _, one, two, mine, land, land2 in places:
                value = acc[span(mine, one), :]
                for o in range(1, groups[first][0]):
                    value = value + land[o - 1]
                acc[span(mine, one), :] = value
                n, own_index, peer = groups[second]
                for o in range(1, n):
                    index, device = peer(o)
                    if plan.whole:
                        copies.append(send(acc.at[span(mine, one)], land2.at[own_index], device))
                    else:
                        copies.append(send(acc.at[span(mine + index * two, two)], land2.at[o - 1], device))
                start(copies)
                copies = []
            if plan.whole:
                for _, second, _, one, _, mine, _, land2 in places:
                    land2[groups[second][1]] = acc[span(mine, one), :]
            yield
            arrived(sum((groups[p[1]][0] - 1) * (p[3] if plan.whole else p[4]) for p in places))
            copies = []
            for first, second, _, one, two, mine, _, land2 in places:
                n, own_index, _ = groups[second]
                if plan.whole:
                    res[span(mine, one), :] = add_up(land2, n)
                    start(gathers(first, span(mine, one)))
                else:
                    at = mine + own_index * two
                    value = acc[span(at, two), :]
                    for o in range(1, n):
                        value = value + land2[o - 1]
                    res[span(at, two), :] = value
                    start(gathers(second, span(at, two)))
            yield
            if not plan.whole:
                arrived(sum((groups[p[1]][0] - 1) * p[4] for p in places))
                copies = []
                for first, _, _, one, _, mine, _, _ in places:
                    copies += gathers(first, span(mine, one))
                start(copies)
                yield
            arrived(sum((groups[p[0]][0] - 1) * p[3] for p in places))
            copies = start([send(res.at[span(base, half)], res.at[span(base, half)], other)])
            yield
            arrived(half)
            yield

        steps = run()
        return lambda: next(steps)

    def add_up(slots, count):
        value = slots[0]
        for i in range(1, count):
            value = value + slots[i]
        return value

    go_early = travelling(early, acc_e, res_e, landing_e, (e_send, e_recv))
    go_late = travelling(late, acc_l, res_l, landing_l, (l_send, l_recv))
    go_early()

    dkv[...] = jnp.zeros_like(dkv)
    less = -jnp.ones((KW, LANES), BF16)

    def back_values(ts):
        for t in ts:
            s, at, keys = window(t)
            dkv[s, keys, LANES:] += tn(split(prob[t]), (heads_in(mh_s, at), heads_in(ml_s, at)))

    def back_keys(ts):
        for t in ts:
            s, at, keys = window(t)
            dkv[s, keys, :LANES] += tn(split(ds[t]), (heads_in(qh_s, at), heads_in(ql_s, at)))

    def swap_back(lanes, i):
        ends = slice(0, HALO), slice(HALO + rows, 2 * HALO + rows)
        return swap(
            remote(dkv.at[:, ends[0], lanes], dhalo.at[1, :, :, lanes], h_send.at[i], h_recv.at[i], left),
            remote(dkv.at[:, ends[1], lanes], dhalo.at[0, :, :, lanes], h_send.at[i + 1], h_recv.at[i + 1], right),
        )

    def back_scores(ts):
        for t in ts:
            s, at, keys = window(t)
            mh, ml = heads_in(mh_s, at), heads_in(ml_s, at)
            th, tl = heads_in(th_s, at), heads_in(tl_s, at)
            vh, vl = kvh[s, keys, LANES:], kvl[s, keys, LANES:]
            ds[t] = prob[t] * dot(cat([mh, ml, mh, th, tl], 1), cat([vh, vh, vl, less, less], 1), NT)

    back_values(border)
    values_here = swap_back(slice(LANES, 2 * LANES), 2)
    back_scores(border)
    back_keys(border)
    keys_here = swap_back(slice(0, LANES), 4)
    back_scores(middle)
    back_keys(middle)
    go_early()

    back_values(middle)
    for t in range(windows):
        s, at, keys = window(t)
        dq_s[at, :] = heads_out(nn(split(ds[t]), (kvh[s, keys, :LANES], kvl[s, keys, :LANES]))) * scale

    dq = dq_s[...]
    rest = split(cat([dq, gpre_s[...]], 1))
    n1_split = split(n1_s[...])
    d_n1 = beside(rest, (wqh[:, 2 * LANES :], wql[:, 2 * LANES :]), NT)
    put(acc_l, ["w_query"], tn(n1_split, (rest[0][:, :LANES], rest[1][:, :LANES])))

    gacc[...] = jnp.zeros_like(gacc)
    gmid[...] = jnp.zeros_like(gmid)

    def fold(v):
        return (v[0:8] + v[8:16]) + (v[16:24] + v[24:32])

    def pair_back(t, carry):
        s, w = t // nwin, lax.rem(t, nwin)
        inv, live = prs[t, 0], prs[t, 1]
        mean = pmean[t]
        u, along = [], None
        for h in range(heads):
            d = ds[t, h * WQ : (h + 1) * WQ]
            u.append(d * inv)
            a = d * bias[t, h * WQ : (h + 1) * WQ]
            along = a if along is None else along + a
            gmid[h] += fold(mean * u[h])
        c1 = along * live
        c0 = mean * c1
        for p in range(channels):
            v = pair[s, w, p]
            d = c0 - v * c1
            for h in range(heads):
                d = d + u[h] * centred[p][h]
                gacc[h * channels + p] += fold(v * u[h])
            g_pair[s, w, p] = d
        return carry

    ahead = 8 * windows // 16
    lax.fori_loop(0, ahead, pair_back, 0)

    values_here()
    keys_here()
    for s in range(samples):
        dkv[s, HALO : 2 * HALO] += jnp.where(me == 0, 0.0, dhalo[0, s])
        dkv[s, rows : rows + HALO] += jnp.where(me == seqn - 1, 0.0, dhalo[1, s])

    d_keys_values = split(cat([dkv[s, HALO : HALO + rows] for s in range(samples)], 0))
    d_n1 = d_n1 + beside(d_keys_values, (wqh[:, : 2 * LANES], wql[:, : 2 * LANES]), NT)
    na = na_s[...]
    sc1 = sc1_s[...]
    dsc1 = d_n1 * na * sc1 * (1.0 - sc1)
    d_first1 = split(cat([dsc1, d_n1], 1))
    ns = ns_s[...]
    put(acc_l, ["w_key", "w_value"], tn(n1_split, d_keys_values))
    put(acc_l, ["w_scale1", "w_shift1"], tn(split(ns * p_s_gain1[...]), d_first1))
    if late.size > LATE_ROWS:
        acc_l[LATE_ROWS:] = jnp.zeros((late.size - LATE_ROWS, LANES), F32)
    go_late()

    g_atoms[...] = dfirst_s[...] + norm_back(d_n1 * sc1, na, ra_s[...])
    go_late()
    go_early()
    lax.fori_loop(ahead, windows, pair_back, 0)

    d_cond1 = beside(d_first1, (w1h[...], w1l[...]), NT)
    d_cond2 = beside(split(cat([dsc2_s[...], dn2_s[...]], 1)), (w2h[...], w2l[...]), NT)

    eye = (
        lax.broadcasted_iota(jnp.int32, (channels, LANES), 0) == lax.broadcasted_iota(jnp.int32, (channels, LANES), 1)
    ).astype(F32)
    gsum = jnp.sum(jnp.sum(gacc[...], axis=1), axis=-1, keepdims=True)
    gless = jnp.sum(jnp.sum(gmid[...], axis=1, keepdims=True), axis=-1, keepdims=True)
    rows_g = [column_sum((gsum[h * channels : (h + 1) * channels] - gless[h]) * eye) for h in range(heads)]
    blank = jnp.zeros((1, LANES - channels), F32)
    gain_row = cat([p_pair_gain[...], blank], 1)
    pair_row = jnp.zeros((1, LANES), F32)
    for h in range(heads):
        pair_row = pair_row + rows_g[h] * cat([p_w_pair[h : h + 1, :], blank], 1)
    pair_grad = cat([v * gain_row for v in rows_g] + [jnp.zeros((8 - heads, LANES), F32)], 0)
    small = {
        "b_scale1": column_sum(dsc1),
        "b_query": column_sum(dq),
        "b_scale2": column_sum(dsc2_s[...]),
        "b_zero1": column_sum(dz1_s[...]),
        "b_zero2": column_sum(dz2_s[...]),
        "s_gain1": column_sum(d_cond1 * ns),
        "s_gain2": column_sum(d_cond2 * ns),
        "pair_gain": pair_row,
    }
    acc_s[...] = cat([small[name] for name in VECTORS] + [pair_grad], 0)
    s1 = start([remote(acc_s, recv_sc, s_send.at[0], s_recv.at[0], other)])
    d_ns = d_cond1 * p_s_gain1[...] + d_cond2 * p_s_gain2[...]
    g_single[...] = norm_back(d_ns, ns, rs_s[...]) + nt(
        split(cat([dz1_s[...], dz2_s[...]], 1)), (wzh[...], wzl[...])
    )

    def spread(slots, mine, peers, i):
        slots[mine] = acc_s[...]
        start([remote(acc_s, slots.at[mine], s_send.at[i], s_recv.at[i], device) for device in peers])

        def end():
            some = acc_e.at[0 : 16 * len(peers)]
            remote(some, some, s_send.at[i], s_recv.at[i], other).wait()

        return end

    go_late()
    go_early()
    wait(s1)
    acc_s[...] = acc_s[...] + recv_sc[...]
    s2 = spread(recv_sxy, k, [xy_peer(o)[1] for o in range(1, nxy)], 1)
    s2()
    acc_s[...] = add_up(recv_sxy, nxy)
    s3 = spread(recv_sz, z, [z_peer(o)[1] for o in range(1, nz)], 2)
    go_late()
    go_early()
    s3()
    res_s[...] = add_up(recv_sz, nz)
    go_late()
    go_early()
    go_late()
    go_early()


class Plan:
    def __init__(self, needed, nxy, nz, whole):
        half = -(-needed // 2)
        grains = (8 * nxy, 8 * nz) if whole else (8 * nxy * nz,) * 2
        line = int(half * (0.4 if whole else 0.34)) // grains[1] * grains[1]
        plane = -(-(half - line) // grains[0]) * grains[0]
        self.whole, self.size = whole, 2 * (plane + line)
        self.parts = [("plane", 0, plane)] + ([("line", plane, line)] if line else [])

    def landing(self, nxy, nz):
        count = {"plane": (nxy, nz), "line": (nz, nxy)}
        shapes = [(self.size // 2, LANES)]
        for first, _, rows in self.parts:
            n, m = count[first]
            shapes.append((n - 1, rows // n, LANES))
            shapes.append((m, rows // n, LANES) if self.whole else (m - 1, rows // n // m, LANES))
        return shapes

    def steps(self):
        return 5 if self.whole else 6


def unpack_kernel(*refs):
    n, v = len(EARLY) + len(LATE), len(VECTORS) + 1
    ins, refs = refs[:7], refs[7:]
    outs, mats, small, held, sems = refs[:4], refs[4 : 4 + n], refs[4 + n : 4 + n + v], refs[4 + n + v : -1], refs[-1]
    for i, (a, b) in enumerate(zip(ins[3::-1], outs[::-1])):
        pltpu.make_async_copy(a, b, sems.at[i]).start()
    at = 0
    for i, (group, packed) in enumerate(((EARLY, ins[4]), (LATE, ins[5]))):
        for name, _, columns in group:
            base, height = PLACE[name], mats[at].shape[0]
            for b in range(columns):
                pltpu.make_async_copy(
                    packed.at[pl.ds(base + b * height, height)], mats[at].at[:, pl.ds(b * LANES, LANES)], sems.at[4 + i]
                ).start()
            at += 1
    row = 0
    for i, (mid, ref) in enumerate(zip(held, small)):
        mid[...] = ins[6][row : row + mid.shape[0], 0 : mid.shape[1]]
        pltpu.make_async_copy(mid, ref, sems.at[6 + i]).start()
        row += 1
    for i, a in enumerate(ins[3::-1]):
        pltpu.make_async_copy(a, a, sems.at[i]).wait()
    for i, packed in enumerate(ins[4:6]):
        some = packed.at[0 : (EARLY_ROWS, LATE_ROWS)[i]]
        pltpu.make_async_copy(some, some, sems.at[4 + i]).wait()
    for i, mid in enumerate(held):
        pltpu.make_async_copy(mid, mid, sems.at[6 + i]).wait()


def shards(dpn, seqn, atoms, single_cond, pair_block, atom_count, *rest):
    params, cotangent = dict(zip(PARAMS, rest[:-1])), rest[-1]
    params["w_pair"] = params["w_pair"].T
    samples, rows, width = atoms.shape
    nwin, channels = pair_block.shape[1:3]
    heads = params["w_pair"].shape[0]
    flat = samples * rows
    nz, nx = 4, seqn // 8
    nxy = dpn * nx
    early = Plan(EARLY_ROWS, nxy, nz, False)
    late = Plan(LATE_ROWS, nxy, nz, True)
    windows = samples * nwin
    hidden = params["w_down"].shape[0]

    def row(v):
        return v.reshape(1, -1) if v.ndim == 1 else v

    vmem = pl.BlockSpec(memory_space=pltpu.VMEM)
    anyw = pl.BlockSpec(memory_space=pl.ANY)

    def buf(*shape):
        return pltpu.VMEM(shape, F32)

    def low(*shape):
        return [pltpu.VMEM(shape, BF16), pltpu.VMEM(shape, BF16)]

    def sems(n):
        return [pltpu.SemaphoreType.DMA((n,)), pltpu.SemaphoreType.DMA((n,))]

    tall = (flat, width)
    extended = (samples, rows + 2 * HALO, 2 * width)
    scratch = [
        buf(*pair_block.shape),
        buf(windows, heads * WQ, KW),
        buf(windows, WQ, KW),
        buf(windows, 2, WQ, KW),
        buf(windows, heads * WQ, KW),
        buf(windows, heads * WQ, KW),
        buf(*extended),
        buf(*extended),
        buf(2, samples, HALO, 2 * width),
    ]
    scratch += low(*extended)
    scratch += low(width, 2 * width)
    scratch += low(width, 4 * width)
    scratch += low(width, 2 * width)
    scratch += low(width, 2 * width)
    scratch += low(width, 2 * hidden)
    scratch += low(hidden, width)
    scratch += low(width, width)
    scratch += low(*tall) + low(*tall) + low(*tall)
    scratch += [buf(*tall) for _ in range(19)]
    scratch += [
        buf(heads * channels, 8, KW),
        buf(heads, 8, KW),
        buf(early.size, LANES),
        buf(late.size, LANES),
        buf(16, LANES),
        buf(16, LANES),
        buf(nxy, 16, LANES),
        buf(nz, 16, LANES),
        pltpu.SemaphoreType.DMA((samples,)),
    ]
    scratch += sems(6) + sems(early.steps()) + sems(late.steps()) + sems(3)
    scratch += [buf(*shape) for plan in (early, late) for shape in plan.landing(nxy, nz)]
    arrays = [
        atom_count,
        params["pair_gain"],
        params["w_pair"],
        atoms.reshape(tall),
        single_cond.reshape(tall),
        cotangent.reshape(tall),
        *[row(params[name]) for name in PARAMS],
        pair_block,
    ]
    scratch += [pltpu.SMEM(v.shape, v.dtype) for v in arrays[:3]]
    scratch += [buf(*v.shape) for v in arrays[3:-1]]
    scratch += [pltpu.SemaphoreType.DMA((4 + len(arrays) - 1 - 14,))]
    sizes = (samples, rows, dpn, seqn, early, late)
    big = pl.pallas_call(
        functools.partial(block_kernel, sizes),
        out_shape=[buf(*shape) for shape in (tall, tall, tall, pair_block.shape, (early.size, LANES), (late.size, LANES), (16, LANES))],
        in_specs=[anyw] * (7 + len(PARAMS)),
        out_specs=[vmem] * 7,
        scratch_shapes=scratch,
        compiler_params=pltpu.CompilerParams(
            collective_id=0, has_side_effects=True, vmem_limit_bytes=40 * 2**20
        ),
        name="block",
    )(*[pltpu.with_memory_space_constraint(v, pltpu.HBM) for v in arrays])

    names = [name for name, _, _ in EARLY + LATE]
    mats = [jax.ShapeDtypeStruct(params[name].shape, F32) for name in names]
    vecs = [jax.ShapeDtypeStruct((1, params[name].shape[0]), F32) for name in VECTORS]
    big = list(big)
    for i in range(3):
        big[i] = big[i].reshape(1, *tall)
    results = pl.pallas_call(
        unpack_kernel,
        out_shape=[jax.ShapeDtypeStruct(v.shape, F32) for v in big[:4]]
        + mats
        + vecs
        + [jax.ShapeDtypeStruct((heads, channels), F32)],
        in_specs=[vmem] * 7,
        out_specs=[anyw] * (5 + len(mats) + len(vecs)),
        scratch_shapes=[buf(*v.shape) for v in vecs]
        + [buf(heads, channels), pltpu.SemaphoreType.DMA((7 + len(vecs),))],
        compiler_params=pltpu.CompilerParams(vmem_limit_bytes=16 * 2**20),
        name="unpack",
    )(*[pltpu.with_memory_space_constraint(v, pltpu.VMEM) for v in big])
    grads = dict(zip(names, results[4:]))
    for name, value in zip(VECTORS, results[4 + len(mats) :]):
        grads[name] = value.reshape(-1)
    grads["w_pair"] = results[-1].T
    out, g_atoms, g_single, g_pair = results[:4]
    return (
        out.reshape(atoms.shape),
        g_atoms.reshape(atoms.shape),
        g_single.reshape(atoms.shape),
        g_pair.reshape(pair_block.shape),
    ) + tuple(grads[name] for name in PARAMS)


def solution(mesh):
    data = P("dp", "seq", None)
    pairs = P("dp", "seq", None, None, None)
    return jax.shard_map(
        functools.partial(shards, mesh.shape["dp"], mesh.shape["seq"]),
        mesh=mesh,
        in_specs=(data, data, pairs, P("dp")) + (P(),) * len(PARAMS) + (data,),
        out_specs=(data, data, data, pairs) + (P(),) * len(PARAMS),
        check_vma=False,
    )
```
